32 devices in a mesh: seq: 4 (over y, x), ctx: 8 (over z, core).
Axes of the slice: x: 2, y: 2, z: 4, core: 2. Of those that a mesh axis runs over, the one named last changes fastest.
Arguments:
- tokens: bfloat16 [4096, 2048], P(('seq', 'ctx')), may hold values from -6 to 6
- cotangent: bfloat16 [4096, 2048], P(('seq', 'ctx')), may hold values from -6 to 6
- norm_gain: bfloat16 [2048], P(('seq', 'ctx')), may hold values from 0.5 to 1.5
- gating_weight: bfloat16 [2048, 3072], P(('seq', 'ctx')), may hold values from -0.125 to 0.125
- inner_weight: bfloat16 [2048, 3072], P(('seq', 'ctx')), may hold values from -0.125 to 0.125
- state_weight: bfloat16 [2048, 512], P(('seq', 'ctx')), may hold values from -0.125 to 0.125
- step_weight: bfloat16 [2048, 48], P(('seq', 'ctx')), may hold values from -0.125 to 0.125
- conv_weight: bfloat16 [4, 3584], P(None, ('seq', 'ctx')), may hold values from -3 to 3
- conv_bias: bfloat16 [3584], P(('seq', 'ctx')), may hold values from -1.5 to 1.5
- mixer_gain: bfloat16 [3072], P(('seq', 'ctx')), may hold values from 0.5 to 1.5
- mixer_out: bfloat16 [3072, 2048], P(None, ('seq', 'ctx')), may hold values from -0.109375 to 0.109375
- query_weight: bfloat16 [2048, 1024], P(('seq', 'ctx')), may hold values from -0.125 to 0.125
- key_weight: bfloat16 [2048, 256], P(('seq', 'ctx')), may hold values from -0.125 to 0.125
- value_weight: bfloat16 [2048, 256], P(('seq', 'ctx')), may hold values from -0.125 to 0.125
- output_weight: bfloat16 [1024, 2048], P(None, ('seq', 'ctx')), may hold values from -0.75 to 0.75
- feed_gain: bfloat16 [2048], P(('seq', 'ctx')), may hold values from 0.5 to 1.5
- gate_matrix: bfloat16 [2048, 4096], P(('seq', 'ctx')), may hold values from -0.125 to 0.125
- lift_matrix: bfloat16 [2048, 4096], P(('seq', 'ctx')), may hold values from -0.125 to 0.125
- drop_matrix: bfloat16 [4096, 2048], P(None, ('seq', 'ctx')), may hold values from -0.09375 to 0.09375
- step_bias: float32 [48], replicated, may hold values from -4 to 0
- decay_log: float32 [48], replicated, may hold values from -10 to -1
- skip_scale: float32 [48], replicated, may hold values from 0.5 to 2
Outputs:
- layer_output: bfloat16 [4096, 2048], P(('seq', 'ctx'))
- tokens_grad: float32 [4096, 2048], P(('seq', 'ctx'))
- norm_gain_grad: float32 [2048], P(('seq', 'ctx'))
- gating_weight_grad: float32 [2048, 3072], P(('seq', 'ctx'))
- inner_weight_grad: float32 [2048, 3072], P(('seq', 'ctx'))
- state_weight_grad: float32 [2048, 512], P(('seq', 'ctx'))
- step_weight_grad: float32 [2048, 48], P(('seq', 'ctx'))
- conv_weight_grad: float32 [4, 3584], P(None, ('seq', 'ctx'))
- conv_bias_grad: float32 [3584], P(('seq', 'ctx'))
- mixer_gain_grad: float32 [3072], P(('seq', 'ctx'))
- mixer_out_grad: float32 [3072, 2048], P(None, ('seq', 'ctx'))
- query_weight_grad: float32 [2048, 1024], P(('seq', 'ctx'))
- key_weight_grad: float32 [2048, 256], P(('seq', 'ctx'))
- value_weight_grad: float32 [2048, 256], P(('seq', 'ctx'))
- output_weight_grad: float32 [1024, 2048], P(None, ('seq', 'ctx'))
- feed_gain_grad: float32 [2048], P(('seq', 'ctx'))
- gate_matrix_grad: float32 [2048, 4096], P(('seq', 'ctx'))
- lift_matrix_grad: float32 [2048, 4096], P(('seq', 'ctx'))
- drop_matrix_grad: float32 [4096, 2048], P(None, ('seq', 'ctx'))
- step_bias_grad: float32 [48], replicated
- decay_log_grad: float32 [48], replicated
- skip_scale_grad: float32 [48], replicated
The draws below stay inside these ranges and needn't reach their ends.
All inputs are finite; a program needn't handle non-finite values.
Results may differ from the reference program's by a relative error of at most 0.013.
Values may be sent and summed in bfloat16 or wider, within the bound.
No kernel may reach another device: no remote copies, remote signals or barrier semaphores. Data moves between devices by JAX's collectives and lax.ppermute only.
A program may use at most 320 MiB of HBM per device.

```python
from functools import partial
import jax
import jax.numpy as jnp
from jax import lax

D = 2048
DI = 3072
HM = 48
PM = 64
NS = 256
KC = 4
HA = 8
HK = 2
HD = 128
FF = 4096
TOK_DEV = 128
LENGTH = 1024
SEQS = 4
TOKENS = 4096


def with_spikes(array, key, source, target, shards_of, factor):
    owner, partner = [(jnp.arange(array.shape[axis_at]) // (array.shape[axis_at] // shards_of)).reshape([-1 if axis == axis_at else 1 for axis in range(array.ndim)]) for axis_at in (source, target)]
    chosen = jax.random.permutation(key, shards_of)[partner]
    strong = (owner == chosen) | (owner == (partner + shards_of // 2) % shards_of)
    return jnp.where(strong, factor * array, array)


def shard_levels(own_key, extent, shards, low, largest):
    def one(dim, blocks):
        draws = jax.random.uniform(jax.random.fold_in(jax.random.fold_in(own_key, 6), dim), (blocks,), jnp.float32, low / len(shards), largest / len(shards))
        return jnp.repeat(jnp.exp(draws), extent[dim] // blocks).reshape((-1,) + (1,) * (len(extent) - dim - 1))

    gain = one(*shards[0])
    for cut in shards[1:]:
        gain = gain * one(*cut)
    return gain


def noise(key, dims, deviation, reach, pieces=(), kind=jnp.bfloat16):
    values = deviation * jax.random.normal(key, dims, jnp.float32)
    if pieces:
        values = values * shard_levels(key, dims, pieces, -0.22, 0.18)
    return jnp.clip(values, -reach, reach).astype(kind)


def gaussian_with(stream_key, extent, spread, bound, cuts, heavy, kind=jnp.bfloat16):
    values = spread * jax.random.normal(stream_key, extent, jnp.float32)
    if cuts:
        values = values * shard_levels(stream_key, extent, cuts, -0.22, 0.18)
    return jnp.clip(with_spikes(values, jax.random.fold_in(stream_key, 3), *heavy), -bound, bound).astype(kind)


def setup_inputs(seed: int = 0) -> dict:
    splits = jax.random.split(jax.random.key(seed), 23)
    tokens = gaussian_with(splits[0], (TOKENS, D), 1.0, 6.0, ((0, 32),), (0, 1, 32, 2.75))
    cotangent = gaussian_with(splits[1], (TOKENS, D), 1.0, 6.0, ((0, 32),), (0, 1, 32, 2.75))
    norm_gain = jnp.clip(1.0 + 0.1 * jax.random.normal(splits[2], (D,), jnp.float32), 0.5, 1.5).astype(jnp.bfloat16)
    gating_weight = noise(splits[3], (D, DI), D ** -0.5, 0.125, ((0, 32),))
    inner_weight = noise(splits[4], (D, DI), D ** -0.5, 0.125, ((0, 32),))
    state_weight = noise(splits[5], (D, 2 * NS), D ** -0.5, 0.125, ((0, 32),))
    step_weight = noise(splits[6], (D, HM), D ** -0.5, 0.125, ((0, 32),))
    conv_weight = noise(splits[7], (KC, DI + 2 * NS), KC ** -0.5, 3.0, ((1, 32),))
    conv_bias = noise(splits[8], (DI + 2 * NS,), 0.3, 1.5, ((0, 32),))
    mixer_gain = jnp.clip(1.0 + 0.1 * jax.random.normal(splits[9], (DI,), jnp.float32), 0.5, 1.5).astype(jnp.bfloat16)
    mixer_out = noise(splits[10], (DI, D), DI ** -0.5, 0.109375, ((1, 32),))
    query_weight = noise(splits[11], (D, HA * HD), D ** -0.5, 0.125, ((0, 32),))
    key_weight = noise(splits[12], (D, HK * HD), D ** -0.5, 0.125, ((0, 32),))
    value_weight = noise(splits[13], (D, HK * HD), D ** -0.5, 0.125, ((0, 32),))
    output_weight = noise(splits[14], (HA * HD, D), (HA * HD // 16) ** -0.5, 0.75, ((1, 32),))
    feed_gain = jnp.clip(1.0 + 0.1 * jax.random.normal(splits[15], (D,), jnp.float32), 0.5, 1.5).astype(jnp.bfloat16)
    gate_matrix = noise(splits[16], (D, FF), D ** -0.5, 0.125, ((0, 32),))
    lift_matrix = noise(splits[17], (D, FF), D ** -0.5, 0.125, ((0, 32),))
    drop_matrix = noise(splits[18], (FF, D), FF ** -0.5, 0.09375, ((1, 32),))
    step_bias = jnp.clip(jax.random.uniform(splits[19], (HM,), jnp.float32, -4.0, 0.0), -4.0, 0.0)
    decay_log = jnp.clip(jax.random.uniform(splits[20], (HM,), jnp.float32, -10.0, -1.0), -10.0, -1.0)
    skip_scale = jnp.clip(jax.random.uniform(splits[21], (HM,), jnp.float32, 0.5, 2.0), 0.5, 2.0)
    return {"tokens": tokens, "cotangent": cotangent, "norm_gain": norm_gain, "gating_weight": gating_weight, "inner_weight": inner_weight, "state_weight": state_weight, "step_weight": step_weight, "conv_weight": conv_weight, "conv_bias": conv_bias, "mixer_gain": mixer_gain, "mixer_out": mixer_out, "query_weight": query_weight, "key_weight": key_weight, "value_weight": value_weight, "output_weight": output_weight, "feed_gain": feed_gain, "gate_matrix": gate_matrix, "lift_matrix": lift_matrix, "drop_matrix": drop_matrix, "step_bias": step_bias, "decay_log": decay_log, "skip_scale": skip_scale}


epsilon = 1e-06
highest = lax.Precision.HIGHEST
negative = -1e+30

@jax.custom_vjp
def low(v):
    return lax.optimization_barrier(v.astype(jnp.bfloat16)).astype(jnp.float32)

@jax.custom_vjp
def low_back(v):
    return v

def low_keep(v):
    return (low(v), None)

def low_pass(kept, grad):
    return (grad,)

def back_keep(v):
    return (v, None)

def back_low(kept, grad):
    return (low(grad),)
low.defvjp(low_keep, low_pass)
low_back.defvjp(back_keep, back_low)

def normalize(values):
    return values * lax.rsqrt(lax.optimization_barrier(jnp.mean(values * values, axis=-1, keepdims=True)) + epsilon)

def silu_value(values):
    return values * jax.nn.sigmoid(values)

def softplus(values):
    return jnp.maximum(values, 0.0) + jnp.log1p(jnp.exp(-jnp.abs(values)))

def matmul(operand, against):
    return jnp.dot(operand, against, precision=highest)

def ssd_block(rates, run_state, block):
    inner_heads, in_state, out_state, step_size = block
    row_total = inner_heads.shape[0]
    cumulative = jnp.cumsum(step_size * rates[None, :], axis=0)
    causal_mask = jnp.arange(row_total)[:, None] >= jnp.arange(row_total)[None, :]
    span_logs = cumulative.T[:, :, None] - cumulative.T[:, None, :]
    fading = jnp.where(causal_mask[None], jnp.exp(jnp.where(causal_mask[None], span_logs, 0.0)), 0.0)
    pairing = matmul(out_state, in_state.T)
    mixing = fading * pairing[None] * step_size.T[:, None, :]
    within = jnp.einsum('hts,shp->thp', mixing, inner_heads, precision=highest)
    readout = jnp.einsum('tn,hpn->thp', out_state, run_state, precision=highest)
    head_rows = within + jnp.exp(cumulative)[:, :, None] * readout
    feeding = jnp.exp(cumulative[-1][None, :] - cumulative) * step_size
    fresh_state = jnp.einsum('th,thp,tn->hpn', feeding, inner_heads, in_state, precision=highest)
    next_state = jnp.exp(cumulative[-1])[:, None, None] * run_state + fresh_state
    return (next_state, head_rows)

def attention_rows(keys, values, scan_item):
    queries, start_row = scan_item
    query_total = queries.shape[0]
    scores = low_back(jnp.einsum('tkgd,nkd->kgtn', queries, keys, precision=highest) * HD ** (-0.5))
    query_place = start_row + jnp.arange(query_total, dtype=jnp.int32)
    key_place = jnp.arange(keys.shape[0], dtype=jnp.int32)
    visible = query_place[:, None] >= key_place[None, :]
    scores = jnp.where(visible, scores, negative)
    row_top = lax.optimization_barrier(jnp.max(scores, axis=-1, keepdims=True))
    log_total = row_top + jnp.log(lax.optimization_barrier(jnp.sum(jnp.exp(scores - row_top), axis=-1, keepdims=True)))
    probability = jnp.exp(scores - log_total)
    return jnp.einsum('kgtn,nkd->tkgd', probability, values, precision=highest)

def layer(inputs, params):
    norm_gain, gating_weight, inner_weight, state_weight, step_weight, conv_weight, conv_bias, mixer_gain, mixer_out, query_weight, key_weight, value_weight, output_weight, feed_gain, gate_matrix, lift_matrix, drop_matrix, step_bias, decay_log, skip_scale = params
    row_total = inputs.shape[0]
    groups = HA // HK
    hidden = low(normalize(inputs) * norm_gain)
    gating = low_back(matmul(hidden, gating_weight))
    pre_conv = low_back(jnp.concatenate([matmul(hidden, inner_weight), matmul(hidden, state_weight)], 1))
    step_pre = low_back(matmul(hidden, step_weight))
    padded = jnp.concatenate([jnp.zeros((KC - 1, pre_conv.shape[1]), jnp.float32), pre_conv], 0)
    conv_sum = conv_bias[None, :]
    for offset in range(KC):
        conv_sum = conv_sum + conv_weight[offset][None, :] * padded[offset:offset + row_total]
    mixed_in = silu_value(conv_sum)
    inner_heads = mixed_in[:, :DI].reshape(row_total, HM, PM)
    in_state = mixed_in[:, DI:DI + NS]
    out_state = mixed_in[:, DI + NS:]
    step_size = softplus(step_pre + step_bias[None, :])
    decay_rates = -jnp.exp(decay_log)
    blocks = row_total // TOK_DEV
    first_state = jnp.zeros((HM, PM, NS), jnp.float32)
    unused, head_rows = lax.scan(jax.checkpoint(partial(ssd_block, decay_rates)), first_state, (inner_heads.reshape(blocks, TOK_DEV, HM, PM), in_state.reshape(blocks, TOK_DEV, NS), out_state.reshape(blocks, TOK_DEV, NS), step_size.reshape(blocks, TOK_DEV, HM)))
    ssm_heads = head_rows.reshape(row_total, HM, PM) + skip_scale[None, :, None] * inner_heads
    gated_rows = ssm_heads.reshape(row_total, DI) * silu_value(gating)
    mixer_rows = low(normalize(gated_rows) * mixer_gain)
    mamba_branch = low_back(matmul(mixer_rows, mixer_out))
    queries = low(low_back(matmul(hidden, query_weight))).reshape(row_total, HK, groups, HD)
    keys = low(low_back(matmul(hidden, key_weight))).reshape(row_total, HK, HD)
    values = low(low_back(matmul(hidden, value_weight))).reshape(row_total, HK, HD)
    block_width = min(512, row_total)
    query_blocks = queries.reshape(row_total // block_width, block_width, HK, groups, HD)
    starts = jnp.arange(row_total // block_width, dtype=jnp.int32) * block_width
    attended = lax.map(jax.checkpoint(partial(attention_rows, keys, values)), (query_blocks, starts))
    attn_rows = low(low_back(attended.reshape(row_total, HA * HD)))
    attn_branch = low_back(matmul(attn_rows, output_weight))
    residual = inputs + mamba_branch + attn_branch
    feed_rows = low(normalize(residual) * feed_gain)
    gate_pre = low_back(matmul(feed_rows, gate_matrix))
    lift_pre = low_back(matmul(feed_rows, lift_matrix))
    active = low(silu_value(gate_pre) * lift_pre)
    return residual + matmul(active, drop_matrix)

def reference(tokens, cotangent, norm_gain, gating_weight, inner_weight, state_weight, step_weight, conv_weight, conv_bias, mixer_gain, mixer_out, query_weight, key_weight, value_weight, output_weight, feed_gain, gate_matrix, lift_matrix, drop_matrix, step_bias, decay_log, skip_scale):
    params = tuple((item.astype(jnp.float32) for item in (norm_gain, gating_weight, inner_weight, state_weight, step_weight, conv_weight, conv_bias, mixer_gain, mixer_out, query_weight, key_weight, value_weight, output_weight, feed_gain, gate_matrix, lift_matrix, drop_matrix, step_bias, decay_log, skip_scale)))
    inputs = tokens.astype(jnp.float32).reshape(SEQS, LENGTH, D)
    grads_in = cotangent.astype(jnp.float32).reshape(SEQS, LENGTH, D)

    def one_sequence(grad_total, scan_item):
        outputs, pullback = jax.vjp(layer, scan_item[0], params)
        input_grad, param_grad = pullback(scan_item[1])
        return (jax.tree.map(jnp.add, grad_total, param_grad), (outputs, input_grad))
    zero_grads = jax.tree.map(jnp.zeros_like, params)
    grad_total, (outputs, input_grads) = lax.scan(one_sequence, zero_grads, (inputs, grads_in))
    norm_grad, gating_grad, inner_grad, state_grad, step_grad, conv_weight_grad, conv_bias_grad, mixer_gain_grad, mixer_out_grad, query_grad, key_grad, value_grad, output_grad, feed_grad, gate_grad, lift_grad, drop_grad, bias_grad, decay_grad, skip_grad = grad_total
    return (outputs.reshape(TOKENS, D).astype(jnp.bfloat16), input_grads.reshape(TOKENS, D), norm_grad, gating_grad, inner_grad, state_grad, step_grad, conv_weight_grad, conv_bias_grad, mixer_gain_grad, mixer_out_grad, query_grad, key_grad, value_grad, output_grad, feed_grad, gate_grad, lift_grad, drop_grad, bias_grad, decay_grad, skip_grad)
```

```python
import jax
import jax.numpy as jnp
from jax import lax
from jax.sharding import Mesh
from jax.sharding import PartitionSpec as P

DI = 3072
HM = 48
PM = 64
NS = 256
KC = 4
HA = 8
HK = 2
HD = 128
FF = 4096
BLOCK = 128

epsilon = 1e-06
negative = -1e30
BF = jnp.bfloat16
F32 = jnp.float32

TEAM = ("sl", "zl", "core")
PEERS = ("sh", "ch")
WORLD = ("sh", "sl", "ch", "zl", "core")
RANKS = 8


def swap(value, axis):
    return lax.ppermute(value, axis, [(0, 1), (1, 0)])


def paired(mine, theirs, axis_name, dim):
    bit = lax.axis_index(axis_name)
    return jnp.where(bit == 0, jnp.stack([mine, theirs], dim), jnp.stack([theirs, mine], dim))


def kept(value, axis_name, dim):
    return lax.dynamic_index_in_dim(value, lax.axis_index(axis_name), dim, False)


def given(value, axis_name, dim):
    return lax.dynamic_index_in_dim(value, 1 - lax.axis_index(axis_name), dim, False)


def added(mine, theirs):
    return mine.astype(F32) + theirs.astype(F32)


def team_gather(rows):
    count, width = rows.shape
    half = count // 2
    first, second = rows[:half], rows[half:]
    first_x = swap(first, "sl")
    second_z = swap(second, "zl")
    first = paired(first, first_x, "sl", 0)
    second = paired(second, second_z, "zl", 0)
    first_z = swap(first, "zl")
    second_x = swap(second, "sl")
    first = paired(first, first_z, "zl", 1)
    second = paired(second, second_x, "sl", 0)
    both = jnp.concatenate([first, second], 2)
    return paired(both, swap(both, "core"), "core", 2).reshape(RANKS * count, width)


def team_scatter(rows):
    total, width = rows.shape
    count = total // RANKS
    half = count // 2
    rows = rows.reshape(2, 2, 2, count, width)
    rows = added(kept(rows, "core", 2), swap(given(rows, "core", 2).astype(BF), "core"))
    first, second = rows[:, :, :half], rows[:, :, half:]
    first_z = swap(given(first, "zl", 1).astype(BF), "zl")
    second_x = swap(given(second, "sl", 0).astype(BF), "sl")
    first = added(kept(first, "zl", 1), first_z)
    second = added(kept(second, "sl", 0), second_x)
    first_x = swap(given(first, "sl", 0).astype(BF), "sl")
    second_z = swap(given(second, "zl", 0).astype(BF), "zl")
    first = added(kept(first, "sl", 0), first_x)
    second = added(kept(second, "zl", 0), second_z)
    return jnp.concatenate([first, second], 0)


def team_sum(value):
    for axis in TEAM[::-1]:
        value = value + swap(value, axis)
    return value


def columns_gather(part, axes):
    out = part[:, None, :]
    for axis in axes[::-1]:
        out = paired(out, swap(out, axis), axis, 1).reshape(out.shape[0], -1, out.shape[2])
    return out.reshape(part.shape[0], -1)


def columns_scatter(value, axes):
    rows, width = value.shape
    pieces = 2 ** len(axes)
    out = value.reshape(rows, pieces, width // pieces)
    for axis in axes:
        pieces //= 2
        out = out.reshape(rows, 2, pieces, -1)
        out = added(kept(out, axis, 1), swap(given(out, axis, 1).astype(BF), axis))
    return out.reshape(rows, -1)


def peers_gather(part):
    if lax.axis_size("ch") == 2:
        part = paired(part, swap(part, "ch"), "ch", 0).reshape(-1, part.shape[1])
    elif lax.axis_size("ch") > 2:
        part = lax.all_gather(part, "ch", axis=0, tiled=True)
    if lax.axis_size("sh") == 2:
        part = paired(part, swap(part, "sh"), "sh", 0).reshape(-1, part.shape[1])
    elif lax.axis_size("sh") > 2:
        part = lax.all_gather(part, "sh", axis=0, tiled=True)
    return part


def peers_scatter(value):
    for axis in PEERS:
        size = lax.axis_size(axis)
        if size == 2:
            value = value.reshape(2, -1, value.shape[-1])
            value = added(kept(value, axis, 0), swap(given(value, axis, 0).astype(BF), axis))
        elif size > 2:
            value = lax.psum_scatter(value.astype(BF), axis, scatter_dimension=0, tiled=True)
    return value


def weight_gather(pack):
    mixed = lax.all_to_all(pack, TEAM, split_axis=0, concat_axis=0, tiled=True)
    return peers_gather(mixed.reshape(-1, pack.shape[2]))


def weight_scatter(grad, rows):
    part = peers_scatter(grad).astype(BF).reshape(RANKS, rows, grad.shape[1])
    return lax.all_to_all(part, TEAM, split_axis=0, concat_axis=0, tiled=True).astype(F32)


def by_rank(weight):
    rows = weight.shape[0]
    return weight.reshape(rows, RANKS, -1).transpose(1, 0, 2)


def to_columns(pieces):
    return pieces.transpose(1, 0, 2).reshape(pieces.shape[1], -1)


def shuffled(rows, sh, sl, ch):
    count, width = rows.shape
    return rows.reshape(count, sh, sl, ch, -1).swapaxes(2, 3).reshape(count, width)


def unshuffled(rows, sh, sl, ch):
    count, width = rows.shape
    return rows.reshape(count, sh, ch, sl, -1).swapaxes(2, 3).reshape(count, width)


def shifted(value, steps):
    count = lax.axis_size("ch")
    if count == 1:
        return jnp.zeros_like(value)
    leading, last = max(0, -steps), min(count, count - steps)
    return lax.ppermute(value, "ch", [(at, at + steps) for at in range(leading, last)])


def entering(decay, state, reverse):
    count = lax.axis_size("ch")
    if count == 1:
        return jnp.zeros_like(state)
    if count == 2:
        return shifted(state.astype(BF), -1 if reverse else 1).astype(F32)
    place = lax.axis_index("ch")
    ahead = count - 1 - place if reverse else place
    decays = lax.all_gather(decay, "ch")
    states = lax.all_gather(state.astype(BF), "ch")

    def one(step, run):
        source = count - 1 - step if reverse else step
        factor = lax.dynamic_index_in_dim(decays, source, 0, False)
        return factor[..., None, None] * run + lax.dynamic_index_in_dim(
            states, source, 0, False
        ).astype(F32)

    return lax.fori_loop(0, ahead, one, jnp.zeros_like(state))


def inverse_root(values):
    return lax.rsqrt(jnp.mean(values * values, axis=-1, keepdims=True) + epsilon)


def norm_back(values, scaled, upstream):
    normed = values * scaled
    return scaled * (upstream - normed * jnp.mean(upstream * normed, axis=-1, keepdims=True))


def silu_value(values):
    return values * jax.nn.sigmoid(values)


def silu_slope(values):
    sigmoid_part = jax.nn.sigmoid(values)
    return sigmoid_part * (1.0 + values * (1.0 - sigmoid_part))


def softplus(values):
    return jnp.maximum(values, 0.0) + jnp.log1p(jnp.exp(-jnp.abs(values)))


def plain_dot(operand, against):
    return jnp.dot(operand, against, preferred_element_type=F32)


def tail_dot(operand, against):
    return lax.dot_general(
        operand, against, (((1,), (1,)), ((), ())), preferred_element_type=F32
    )


def lead_dot(operand, against):
    return lax.dot_general(
        operand, against, (((0,), (0,)), ((), ())), preferred_element_type=F32
    )


def dots(spec, *operands):
    return jnp.einsum(
        spec, *[o.astype(BF) for o in operands], preferred_element_type=F32
    )


def local(
    tokens,
    cotangent,
    norm_gain,
    gating_weight,
    inner_weight,
    state_weight,
    step_weight,
    conv_weight,
    conv_bias,
    mixer_gain,
    mixer_out,
    query_weight,
    key_weight,
    value_weight,
    output_weight,
    feed_gain,
    gate_matrix,
    lift_matrix,
    drop_matrix,
    step_bias,
    decay_log,
    skip_scale,
):
    sh, sl, ch = lax.axis_size("sh"), lax.axis_size("sl"), lax.axis_size("ch")
    world = sh * sl * ch * 4
    rows, width = tokens.shape
    drows = norm_gain.shape[0]
    rank = (lax.axis_index("sl") * 2 + lax.axis_index("zl")) * 2 + lax.axis_index("core")
    total = RANKS * rows
    count = 4 * rows
    heads = HM // RANKS
    inner_cols = DI // RANKS
    bc_cols = 2 * NS // RANKS
    kv_cols = 2 * HD // 4
    conv_cols = inner_cols + bc_cols

    conv_own = conv_weight.shape[1]
    gain_own = mixer_gain.shape[0]
    step_scaled = (step_weight.astype(F32) * norm_gain.astype(F32)[:, None]).astype(BF)
    small = lax.all_gather(
        jnp.concatenate(
            [conv_weight.reshape(-1), conv_bias, mixer_gain, step_scaled.reshape(-1)]
        ),
        WORLD,
        axis=0,
        tiled=False,
    )
    at = 0
    wide_conv = small[:, at : at + KC * conv_own].reshape(world, KC, conv_own)
    wide_conv = wide_conv.transpose(1, 0, 2).reshape(KC, -1).astype(F32)
    at += KC * conv_own
    wide_bias = small[:, at : at + conv_own].reshape(1, -1).astype(F32)
    at += conv_own
    wide_gain = small[:, at : at + gain_own].reshape(1, -1).astype(F32)
    at += gain_own
    wide_step = small[:, at:].reshape(sh, sl, ch, 4 * drows, HM).swapaxes(1, 2)
    wide_step = wide_step.reshape(width, HM)
    own_step = lax.dynamic_slice_in_dim(wide_step, rank * heads, heads, 1)
    taps = jnp.concatenate(
        [
            lax.dynamic_slice_in_dim(wide_conv, rank * inner_cols, inner_cols, 1),
            lax.dynamic_slice_in_dim(wide_conv, DI + rank * bc_cols, bc_cols, 1),
        ],
        1,
    )
    bias = jnp.concatenate(
        [
            lax.dynamic_slice_in_dim(wide_bias, rank * inner_cols, inner_cols, 1),
            lax.dynamic_slice_in_dim(wide_bias, DI + rank * bc_cols, bc_cols, 1),
        ],
        1,
    )
    own_gain = lax.dynamic_slice_in_dim(wide_gain, rank * inner_cols, inner_cols, 1)
    own_bias = lax.dynamic_slice_in_dim(step_bias, rank * heads, heads)
    rates = -jnp.exp(lax.dynamic_slice_in_dim(decay_log, rank * heads, heads))
    skip = lax.dynamic_slice_in_dim(skip_scale, rank * heads, heads)

    def scaled(weight, gain):
        return (weight.astype(F32) * gain.astype(F32)[:, None]).astype(BF)

    key_value = jnp.stack(
        [key_weight.reshape(drows, HK, 2, kv_cols), value_weight.reshape(drows, HK, 2, kv_cols)], 2
    ).reshape(drows, RANKS * kv_cols)
    pack_inner = jnp.concatenate(
        [by_rank(scaled(w, norm_gain)) for w in (inner_weight, state_weight, key_value)], 2
    )
    pack_gating = jnp.concatenate(
        [by_rank(scaled(w, norm_gain)) for w in (gating_weight, query_weight)], 2
    )
    pack_out = jnp.concatenate([by_rank(mixer_out.T), by_rank(output_weight.T)], 2)
    pack_gate = by_rank(scaled(gate_matrix, feed_gain))
    pack_lift = by_rank(scaled(lift_matrix, feed_gain))
    pack_drop = by_rank(drop_matrix.T)
    own_tokens = shuffled(tokens, sh, sl, ch)
    own_cotangent = shuffled(cotangent, sh, sl, ch)

    team_tokens = team_gather(own_tokens)
    w_inner = weight_gather(pack_inner)
    w_gating = weight_gather(pack_gating)
    w_out = weight_gather(pack_out)
    team_cotangent = team_gather(own_cotangent)
    w_gate = weight_gather(pack_gate)
    w_lift = weight_gather(pack_lift)
    w_drop = weight_gather(pack_drop)

    root = inverse_root(team_tokens.astype(F32))
    pre_inner = plain_dot(team_tokens, w_inner) * root
    pre_gating = plain_dot(team_tokens, w_gating) * root
    step_pre = plain_dot(team_tokens, own_step) * root
    key_value_rows = columns_gather(pre_inner[:, conv_cols:].astype(BF), ("zl", "core"))
    gating = pre_gating[:, :inner_cols]
    queries = pre_gating[:, inner_cols:].astype(BF).reshape(sl, count, HD)
    pre_conv = pre_inner[:, :conv_cols].reshape(sl, count, conv_cols)
    edge = shifted(pre_conv[:, count - (KC - 1) :], 1)
    padded = jnp.concatenate([edge, pre_conv], 1)
    conv_sum = bias
    for offset in range(KC):
        conv_sum = conv_sum + taps[offset] * padded[:, offset : offset + count]
    mixed_in = silu_value(conv_sum)
    state_io = columns_gather(mixed_in[:, :, inner_cols:].reshape(total, -1).astype(BF), TEAM)
    blocks = count // BLOCK
    in_state = state_io[:, :NS].reshape(sl, blocks, BLOCK, NS)
    out_state = state_io[:, NS:].reshape(sl, blocks, BLOCK, NS)
    inner = mixed_in[:, :, :inner_cols].reshape(sl, blocks, BLOCK, heads, PM)
    step_arg = step_pre + own_bias
    step_size = softplus(step_arg).reshape(sl, blocks, BLOCK, heads)
    cumulative = jnp.cumsum(step_size * rates, axis=2)
    causal = jnp.arange(BLOCK)[:, None] >= jnp.arange(BLOCK)[None, :]
    cum_t = cumulative.swapaxes(2, 3)
    step_t = step_size.swapaxes(2, 3)
    span = cum_t[..., :, None] - cum_t[..., None, :]
    fading = jnp.where(causal, jnp.exp(jnp.where(causal, span, 0.0)), 0.0)
    pairing = dots("nctk,ncsk->ncts", out_state, in_state)[:, :, None]
    mixing = fading * pairing * step_t[..., None, :]
    within = dots("nchts,ncshp->ncthp", mixing, inner)
    to_end = jnp.exp(cumulative[:, :, -1:] - cumulative)
    feeding = to_end * step_size
    fresh = dots("ncthp,nctk->nchpk", feeding[..., None] * inner, in_state)
    decay = jnp.exp(cumulative[:, :, -1])
    run = jnp.zeros_like(fresh[:, 0])
    for c in range(blocks):
        run = decay[:, c, :, None, None] * run + fresh[:, c]
    piece_decay = jnp.exp(jnp.sum(cumulative[:, :, -1], axis=1))
    run = entering(piece_decay, run, False)
    starts = []
    for c in range(blocks):
        starts.append(run)
        run = decay[:, c, :, None, None] * run + fresh[:, c]
    carried = jnp.stack(starts, 1)
    growth = jnp.exp(cumulative)
    readout = dots("nctk,nchpk->ncthp", out_state, carried)
    ssm = within + growth[..., None] * readout + skip[:, None] * inner
    ssm_flat = ssm.reshape(total, inner_cols)
    gate_act = silu_value(gating)
    gated = ssm_flat * gate_act
    square = team_sum(jnp.sum(gated * gated, axis=-1, keepdims=True))
    mixer_root = lax.rsqrt(square / DI + epsilon)

    whole = ch * count
    key_value_all = key_value_rows.reshape(sl, count, 2 * HD)
    if ch > 1:
        key_value_all = lax.all_gather(key_value_all, "ch", axis=1, tiled=True)
    keys, values = key_value_all[..., :HD], key_value_all[..., HD:]
    place = lax.axis_index("ch") * count + jnp.arange(count)
    visible = place[:, None] >= jnp.arange(whole)[None, :]
    scores = dots("ntd,nsd->nts", queries, keys) * HD**-0.5
    scores = jnp.where(visible, scores, negative)
    top = jnp.max(scores, axis=-1, keepdims=True)
    log_total = top + jnp.log(jnp.sum(jnp.exp(scores - top), axis=-1, keepdims=True))
    probs = jnp.exp(scores - log_total)
    attended = dots("nts,nsd->ntd", probs, values).reshape(total, HD)

    branch_rows = jnp.concatenate(
        [(gated * mixer_root * own_gain).astype(BF), attended.astype(BF)], 1
    )
    branch = team_scatter(tail_dot(branch_rows, w_out))

    residual = own_tokens.astype(F32) + branch
    feed_root = inverse_root(residual)
    feed_rows = team_gather((residual * feed_root).astype(BF))
    gate_pre = plain_dot(feed_rows, w_gate)
    lift_pre = plain_dot(feed_rows, w_lift)
    swish = silu_value(gate_pre)
    active = (swish * lift_pre).astype(BF)
    active_grad = plain_dot(team_cotangent, w_drop)
    gate_rows_grad = (active_grad * lift_pre * silu_slope(gate_pre)).astype(BF)
    lift_rows_grad = (active_grad * swish).astype(BF)
    feed_grad = team_scatter(tail_dot(gate_rows_grad, w_gate) + tail_dot(lift_rows_grad, w_lift))
    layer_output = (residual + team_scatter(tail_dot(active, w_drop))).astype(BF)
    residual_grad = own_cotangent.astype(F32) + norm_back(residual, feed_root, feed_grad)
    branch_grad = team_gather(residual_grad.astype(BF))
    drop_back = weight_scatter(lead_dot(team_cotangent, active), drows)
    gate_back = weight_scatter(lead_dot(feed_rows, gate_rows_grad), drows)
    lift_back = weight_scatter(lead_dot(feed_rows, lift_rows_grad), drows)

    rows_grad = plain_dot(branch_grad, w_out)
    out_back = weight_scatter(lead_dot(branch_grad, branch_rows), drows)
    mixer_rows_grad = rows_grad[:, :inner_cols]
    attn_grad = rows_grad[:, inner_cols:].astype(BF)

    mixer_norm = gated * mixer_root
    gain_part = jnp.sum(mixer_rows_grad * mixer_norm, axis=0)
    upstream = mixer_rows_grad * own_gain
    along = team_sum(jnp.sum(upstream * mixer_norm, axis=-1, keepdims=True)) / DI
    gated_grad = mixer_root * (upstream - mixer_norm * along)
    ssm_grad = (gated_grad * gate_act).reshape(sl, blocks, BLOCK, heads, PM)
    gating_grad = gated_grad * ssm_flat * silu_slope(gating)

    delta = jnp.sum(attn_grad.astype(F32) * attended, axis=-1).reshape(sl, count, 1)
    attn_rows_grad = attn_grad.reshape(sl, count, HD)
    probs_grad = dots("ntd,nsd->nts", attn_rows_grad, values)
    scores_grad = (probs * (probs_grad - delta)).astype(BF)
    query_grad = dots("nts,nsd->ntd", scores_grad, keys).reshape(total, HD) * HD**-0.5
    key_part = dots("nts,ntd->nsd", scores_grad, queries) * HD**-0.5
    value_part = dots("nts,ntd->nsd", probs, attn_rows_grad)
    key_value_part = jnp.concatenate([key_part, value_part], 2).reshape(sl * whole, 2 * HD)
    key_value_part = columns_scatter(key_value_part, ("zl", "core")).reshape(sl, whole, kv_cols)
    if ch == 1:
        key_value_grad = key_value_part
    else:
        key_value_grad = lax.psum_scatter(
            key_value_part.astype(BF), "ch", scatter_dimension=1, tiled=True
        ).astype(F32)
    key_value_grad = key_value_grad.reshape(total, kv_cols)

    skip_part = jnp.sum(ssm_grad * inner, axis=(0, 1, 2, 4))
    grown = growth[..., None] * ssm_grad
    carried_grad = dots("ncthp,nctk->nchpk", grown, out_state)
    run = jnp.zeros_like(carried_grad[:, 0])
    for c in range(blocks)[::-1]:
        run = carried_grad[:, c] + decay[:, c, :, None, None] * run
    run = entering(piece_decay, run, True)
    ends = [None] * blocks
    for c in range(blocks)[::-1]:
        ends[c] = run
        run = carried_grad[:, c] + decay[:, c, :, None, None] * run
    later = jnp.stack(ends, 1)
    mixing_grad = jnp.where(causal, dots("ncthp,ncshp->nchts", ssm_grad, inner), 0.0)
    faded = mixing_grad * fading
    pairing_grad = jnp.sum(faded * step_t[..., None, :], axis=2)
    stepwise = faded * pairing
    step_grad = jnp.sum(stepwise, axis=3).swapaxes(2, 3)
    flow = stepwise * step_t[..., None, :]
    cum_grad = (jnp.sum(flow, axis=4) - jnp.sum(flow, axis=3)).swapaxes(2, 3)
    spread = dots("nchpk,ncsk->ncshp", later, in_state)
    inner_grad = (
        dots("nchts,ncthp->ncshp", mixing, ssm_grad)
        + skip[:, None] * ssm_grad
        + feeding[..., None] * spread
    )
    out_state_grad = dots("ncts,ncsk->nctk", pairing_grad, in_state) + dots(
        "ncthp,nchpk->nctk", grown, carried
    )
    in_state_grad = dots("ncts,nctk->ncsk", pairing_grad, out_state) + dots(
        "ncshp,nchpk->ncsk", feeding[..., None] * inner, later
    )
    cum_grad = cum_grad + jnp.sum(ssm_grad * readout, axis=4) * growth
    feeding_grad = jnp.sum(spread * inner, axis=4)
    step_grad = step_grad + feeding_grad * to_end
    fed = feeding_grad * feeding
    last_grad = jnp.sum(fed, axis=2) + jnp.sum(later * carried, axis=(3, 4)) * decay
    increment_grad = lax.cumsum(cum_grad - fed, axis=2, reverse=True) + last_grad[:, :, None]
    step_grad = step_grad + increment_grad * rates
    decay_part = jnp.sum(increment_grad * step_size, axis=(0, 1, 2)) * rates
    arg_grad = step_grad.reshape(total, heads) * jax.nn.sigmoid(step_arg)
    bias_part = jnp.sum(arg_grad, axis=0)

    state_grad = columns_scatter(
        jnp.concatenate([in_state_grad, out_state_grad], 3).reshape(total, 2 * NS), TEAM
    )
    mixed_grad = jnp.concatenate([inner_grad.reshape(total, inner_cols), state_grad], 1)
    conv_grad = mixed_grad.reshape(sl, count, conv_cols) * silu_slope(conv_sum)
    conv_bias_part = jnp.sum(conv_grad, axis=(0, 1))
    conv_part = jnp.stack(
        [
            jnp.sum(conv_grad * padded[:, offset : offset + count], axis=(0, 1))
            for offset in range(KC)
        ],
        0,
    )
    follow = shifted(conv_grad[:, : KC - 1].astype(BF), -1).astype(F32)
    extended = jnp.concatenate([conv_grad, follow], 1)
    pre_grad = jnp.zeros_like(conv_grad)
    for offset in range(KC):
        pre_grad = pre_grad + taps[offset] * extended[:, KC - 1 - offset : KC - 1 - offset + count]
    inner_rows_grad = jnp.concatenate([pre_grad.reshape(total, conv_cols), key_value_grad], 1)
    gating_rows_grad = jnp.concatenate([gating_grad, query_grad], 1)
    inner_rows_grad = (inner_rows_grad * root).astype(BF)
    gating_rows_grad = (gating_rows_grad * root).astype(BF)
    step_rows_grad = (arg_grad * root).astype(BF)
    hidden_grad = team_scatter(
        (
            tail_dot(inner_rows_grad, w_inner)
            + tail_dot(gating_rows_grad, w_gating)
            + tail_dot(step_rows_grad, own_step)
        )
        / root
    )
    gating_back = weight_scatter(lead_dot(team_tokens, gating_rows_grad), drows)
    inner_back = weight_scatter(lead_dot(team_tokens, inner_rows_grad), drows)
    step_back = lead_dot(team_tokens, step_rows_grad)
    token_values = own_tokens.astype(F32)
    tokens_grad = residual_grad + norm_back(token_values, inverse_root(token_values), hidden_grad)

    def placed(part, extent, at):
        base = jnp.zeros(part.shape[:-1] + (extent,), F32)
        return lax.dynamic_update_slice_in_dim(base, part, at, part.ndim - 1)

    conv_all = jnp.concatenate(
        [
            placed(conv_part[:, :inner_cols], DI, rank * inner_cols),
            placed(conv_part[:, inner_cols:], 2 * NS, rank * bc_cols),
        ],
        1,
    )
    conv_bias_all = jnp.concatenate(
        [
            placed(conv_bias_part[:inner_cols], DI, rank * inner_cols),
            placed(conv_bias_part[inner_cols:], 2 * NS, rank * bc_cols),
        ],
        0,
    )
    gain_all = placed(gain_part, DI, rank * inner_cols)
    step_all = placed(step_back, HM, rank * heads)
    step_all = step_all.reshape(sh, ch, sl, 4, drows * HM).swapaxes(1, 2)
    per_head = jnp.concatenate(
        [placed(v, HM, rank * heads) for v in (bias_part, decay_part, skip_part)]
    )
    sent = jnp.concatenate(
        [
            conv_all.reshape(KC, world, conv_own).swapaxes(0, 1).reshape(world, -1),
            conv_bias_all.reshape(world, -1),
            gain_all.reshape(world, -1),
            step_all.reshape(world, -1),
            jnp.broadcast_to(per_head[None], (world, 3 * HM)),
        ],
        1,
    )
    got = jnp.sum(
        lax.all_to_all(sent, WORLD, split_axis=0, concat_axis=0, tiled=True), axis=0
    )
    at = 0
    conv_out = got[at : at + KC * conv_own].reshape(KC, conv_own)
    at += KC * conv_own
    conv_bias_out = got[at : at + conv_own]
    at += conv_own
    gain_out = got[at : at + gain_own]
    at += gain_own
    step_core = got[at : at + drows * HM].reshape(drows, HM)
    at += drows * HM
    bias_out, decay_out, skip_out = (got[at + i * HM : at + (i + 1) * HM] for i in range(3))

    def against(weight, grad):
        return jnp.sum(weight.astype(F32) * grad, axis=1)

    inner_core = to_columns(inner_back[:, :, :inner_cols])
    state_core = to_columns(inner_back[:, :, inner_cols:conv_cols])
    key_value_core = to_columns(inner_back[:, :, conv_cols:]).reshape(drows, HK, 2, 2 * kv_cols)
    key_core = key_value_core[:, :, 0].reshape(drows, HK * HD)
    value_core = key_value_core[:, :, 1].reshape(drows, HK * HD)
    gating_core = to_columns(gating_back[:, :, :inner_cols])
    query_core = to_columns(gating_back[:, :, inner_cols:])
    gate_core, lift_core = to_columns(gate_back), to_columns(lift_back)
    norm_out = (
        against(gating_weight, gating_core)
        + against(inner_weight, inner_core)
        + against(state_weight, state_core)
        + against(step_weight, step_core)
        + against(query_weight, query_core)
        + against(key_weight, key_core)
        + against(value_weight, value_core)
    )
    feed_out = against(gate_matrix, gate_core) + against(lift_matrix, lift_core)
    norm_scale = norm_gain.astype(F32)[:, None]
    feed_scale = feed_gain.astype(F32)[:, None]
    mixer_out_out = out_back[:, :, :inner_cols].transpose(0, 2, 1).reshape(DI, drows)
    output_out = out_back[:, :, inner_cols:].transpose(0, 2, 1).reshape(HA * HD, drows)
    drop_out = drop_back.transpose(0, 2, 1).reshape(-1, drows)
    return (
        unshuffled(layer_output, sh, sl, ch),
        unshuffled(tokens_grad, sh, sl, ch),
        norm_out,
        gating_core * norm_scale,
        inner_core * norm_scale,
        state_core * norm_scale,
        step_core * norm_scale,
        conv_out,
        conv_bias_out,
        gain_out,
        mixer_out_out,
        query_core * norm_scale,
        key_core * norm_scale,
        value_core * norm_scale,
        output_out,
        feed_out,
        gate_core * feed_scale,
        lift_core * feed_scale,
        drop_out,
        bias_out,
        decay_out,
        skip_out,
    )


def solution(mesh):
    seq, ctx = mesh.shape["seq"], mesh.shape["ctx"]
    fine = Mesh(mesh.devices.reshape(seq // 2, 2, ctx // 4, 2, 2), WORLD)
    lead, vector, tail = P(WORLD, None), P(WORLD), P(None, WORLD)
    in_specs = (
        lead,
        lead,
        vector,
        lead,
        lead,
        lead,
        lead,
        tail,
        vector,
        vector,
        tail,
        lead,
        lead,
        lead,
        tail,
        vector,
        lead,
        lead,
        tail,
        P(),
        P(),
        P(),
    )
    out_specs = (
        lead,
        lead,
        vector,
        lead,
        lead,
        lead,
        lead,
        tail,
        vector,
        vector,
        tail,
        lead,
        lead,
        lead,
        tail,
        vector,
        lead,
        lead,
        tail,
        P(),
        P(),
        P(),
    )
    return jax.shard_map(local, mesh=fine, in_specs=in_specs, out_specs=out_specs, check_vma=False)
```

```python
import jax
import jax.numpy as jnp
from jax import lax
from jax.experimental import pallas as pl
from jax.experimental.pallas import tpu as pltpu
from jax.sharding import Mesh
from jax.sharding import PartitionSpec as P

DI = 3072
HM = 48
PM = 64
NS = 256
KC = 4
HA = 8
HK = 2
HD = 128
FF = 4096
BLOCK = 128

epsilon = 1e-06
negative = -1e30
BF = jnp.bfloat16
F32 = jnp.float32

TEAM = ("sl", "zl", "core")
PEERS = ("sh", "ch")
WORLD = ("sh", "sl", "ch", "zl", "core")
RANKS = 8


def swap(value, axis):
    return lax.ppermute(value, axis, [(0, 1), (1, 0)])


def paired(mine, theirs, axis_name, dim):
    bit = lax.axis_index(axis_name)
    return jnp.where(bit == 0, jnp.stack([mine, theirs], dim), jnp.stack([theirs, mine], dim))


def kept(value, axis_name, dim):
    return lax.dynamic_index_in_dim(value, lax.axis_index(axis_name), dim, False)


def given(value, axis_name, dim):
    return lax.dynamic_index_in_dim(value, 1 - lax.axis_index(axis_name), dim, False)


def added(mine, theirs):
    return mine.astype(F32) + theirs.astype(F32)


def team_order():
    s, z, c = (lax.axis_index(axis) for axis in TEAM)
    blocks = [
        ((s ^ sl) * 2 + (z ^ zl)) * 2 + (c ^ core)
        for core in (0, 1)
        for zl in (0, 1)
        for sl in (0, 1)
    ]
    return jnp.stack(blocks).astype(jnp.int32)


def team_gather(rows):
    half = rows.shape[1] // 2
    left, right = rows[:, :half], rows[:, half:]
    left = jnp.stack([left, swap(left, "sl")])
    right = jnp.stack([right, swap(right, "zl")])
    left_z = swap(left, "zl")
    right_x = swap(right, "sl")
    left = jnp.concatenate([left, left_z], 0)
    right = jnp.stack([right[0], right_x[0], right[1], right_x[1]])
    return left, right, swap(left, "core"), swap(right, "core")


def team_scatter(parts):
    left, right, left_given, right_given = parts
    left_got, right_got = swap(left_given, "core"), swap(right_given, "core")
    left_z = swap(added(left[2:], left_got[2:]).astype(BF), "zl")
    right_x = swap(added(right[1::2], right_got[1::2]).astype(BF), "sl")
    left = added(left[:2], left_got[:2]) + left_z.astype(F32)
    right = added(right[0::2], right_got[0::2]) + right_x.astype(F32)
    left_x = swap(left[1].astype(BF), "sl")
    right_z = swap(right[1].astype(BF), "zl")
    return jnp.concatenate([added(left[0], left_x), added(right[0], right_z)], 1)


def team_sum(value):
    for axis in TEAM[::-1]:
        value = value + swap(value, axis)
    return value


def relative(value, axis_name, dim):
    if lax.axis_size(axis_name) != 2:
        return value
    return jnp.where(lax.axis_index(axis_name) == 0, value, jnp.flip(value, dim))


def peers_gather(part):
    size = lax.axis_size("ch")
    if size == 2:
        part = jnp.concatenate([part, swap(part, "ch")], 0)
    elif size > 2:
        part = lax.all_gather(part, "ch", axis=0, tiled=True)
    return part, swap(part, "sh")


def ranks_exchange(pack):
    mixed = lax.all_to_all(pack, TEAM, split_axis=0, concat_axis=0, tiled=True)
    return mixed.reshape(-1, pack.shape[2])


def peers_sum(mine, theirs):
    part = added(mine, theirs)
    if lax.axis_size("ch") == 2:
        half = part.shape[0] // 2
        part = added(part[:half], swap(part[half:].astype(BF), "ch"))
    elif lax.axis_size("ch") > 2:
        part = lax.psum_scatter(part.astype(BF), "ch", scatter_dimension=0, tiled=True)
    return part.astype(BF)


def ranks_return(parts, rows):
    pack = jnp.concatenate([p.reshape(RANKS, rows, -1) for p in parts], 2)
    return lax.all_to_all(pack, TEAM, split_axis=0, concat_axis=0, tiled=True)


def by_rank(weight):
    rows = weight.shape[0]
    return weight.reshape(rows, RANKS, -1).transpose(1, 0, 2)


def to_columns(pieces):
    return pieces.transpose(1, 0, 2).reshape(pieces.shape[1], -1)


def shuffled(rows, sh, sl, ch):
    count, width = rows.shape
    rows = rows.reshape(count, sh, sl, ch, -1).swapaxes(2, 3)
    return relative(relative(rows, "sh", 1), "ch", 2).reshape(count, width)


def unshuffled(rows, sh, sl, ch):
    count, width = rows.shape
    rows = relative(relative(rows.reshape(count, sh, ch, sl, -1), "sh", 1), "ch", 2)
    return rows.swapaxes(2, 3).reshape(count, width)


def shifted(value, steps):
    count = lax.axis_size("ch")
    if count == 1:
        return jnp.zeros_like(value)
    leading, last = max(0, -steps), min(count, count - steps)
    return lax.ppermute(value, "ch", [(at, at + steps) for at in range(leading, last)])


def entering(decay, state, reverse):
    count = lax.axis_size("ch")
    if count == 1:
        return jnp.zeros_like(state)
    if count == 2:
        return shifted(state, -1 if reverse else 1)
    place = lax.axis_index("ch")
    ahead = count - 1 - place if reverse else place
    decays = lax.all_gather(decay, "ch")
    states = lax.all_gather(state, "ch")

    def one(step, run):
        source = count - 1 - step if reverse else step
        factor = lax.dynamic_index_in_dim(decays, source, 0, False)
        return factor[:, None] * run + lax.dynamic_index_in_dim(states, source, 0, False).astype(
            F32
        )

    return lax.fori_loop(0, ahead, one, jnp.zeros(state.shape, F32)).astype(state.dtype)


def inverse_root(values):
    return lax.rsqrt(jnp.mean(values * values, axis=-1, keepdims=True) + epsilon)


def norm_back(values, scaled, upstream):
    normed = values * scaled
    return scaled * (upstream - normed * jnp.mean(upstream * normed, axis=-1, keepdims=True))


def silu_value(values):
    return values * jax.nn.sigmoid(values)


def silu_slope(values):
    sigmoid_part = jax.nn.sigmoid(values)
    return sigmoid_part * (1.0 + values * (1.0 - sigmoid_part))


def dot(operand, against, at, precision=None):
    return lax.dot_general(
        operand, against, (((at[0],), (at[1],)), ((), ())), precision=precision, preferred_element_type=F32
    )


def exact(operand, against, at):
    return dot(operand, against, at, lax.Precision.HIGHEST)


TILE = 2 * BLOCK
EDGE = 16
LANES = 512
INNER = DI // RANKS
HEADS = HM // RANKS
SIDE = 2 * NS // RANKS
CONV = INNER + SIDE


def call(kernel, grid, in_specs, out_specs, out_shape, scratch=(), scalars=0):
    return pl.pallas_call(
        kernel,
        grid_spec=pltpu.PrefetchScalarGridSpec(
            num_scalar_prefetch=scalars,
            grid=grid,
            in_specs=in_specs,
            out_specs=out_specs,
            scratch_shapes=list(scratch),
        ),
        out_shape=out_shape,
        compiler_params=pltpu.CompilerParams(vmem_limit_bytes=48 * 1024 * 1024),
        cost_estimate=pl.CostEstimate(flops=10**9, bytes_accessed=10**6, transcendentals=0),
    )


def shape(dims, dtype=F32):
    return jax.ShapeDtypeStruct(dims, dtype)


def full(array):
    return pl.BlockSpec(array.shape, lambda *at: (0,) * array.ndim)


def tiled(width, rows=TILE):
    return pl.BlockSpec((rows, width), lambda i, *at: (i, 0))


def place_rows(scalars, gathered, rows):
    left, right, left_other, right_other = gathered
    half = left.shape[2]
    own = pl.multiple_of(scalars[0] * BLOCK, BLOCK)
    other = pl.multiple_of((1 - scalars[0]) * BLOCK, BLOCK)
    rows[pl.ds(own, BLOCK), :half] = left[0]
    rows[pl.ds(own, BLOCK), half:] = right[0]
    rows[pl.ds(other, BLOCK), :half] = left_other[0]
    rows[pl.ds(other, BLOCK), half:] = right_other[0]


def gathered_specs(gathered):
    spec = pl.BlockSpec((1,) + gathered[0].shape[1:], lambda i, s: (s[1 + i], 0, 0))
    return [spec] * 4


def halves_product(rows, mine, theirs):
    half = mine.shape[0]
    return dot(rows[:, :half], mine[...], (1, 0)) + dot(rows[:, half:], theirs[...], (1, 0))


def row_root(rows):
    values = rows.astype(F32)
    return lax.rsqrt(jnp.mean(values * values, axis=-1, keepdims=True) + epsilon)


def project_inner_kernel(tiles, scalars, l, r, lo, ro, mine, theirs, halo, taps, steps, pre_ref, conv_ref, side_ref, step_ref, root_ref, edge_ref, rows, line):
    i = pl.program_id(0)
    place_rows(scalars, (l, r, lo, ro), rows)
    values = rows[...]
    root = row_root(values)
    root_ref[...] = root
    pre = halves_product(values, mine, theirs) * root
    pre_ref[...] = pre
    step_ref[...] = dot(values, steps[...], (1, 1)) * root

    @pl.when(i % tiles == 0)
    def _():
        before = halo[0]
        edge = halves_product(before, mine, theirs) * row_root(before)
        edge_ref[0] = edge
        line[:EDGE] = edge

    @pl.when(i % tiles != 0)
    def _():
        line[:EDGE] = line[TILE:]

    line[EDGE:] = pre
    conv = taps[KC : KC + 1, :]
    for k in range(KC):
        conv = conv + taps[k : k + 1, :] * line[EDGE - (KC - 1) + k : EDGE - (KC - 1) + k + TILE, :]
    conv_ref[...] = conv
    last = conv[:, INNER:]
    lane = lax.broadcasted_iota(jnp.int32, last.shape, 1)
    side_ref[...] = jnp.where(lane < SIDE, silu_value(last), last).astype(BF)


def project_inner(scalars, gathered, weight, halo, taps, steps):
    seqs = halo.shape[0]
    total = 2 * 4 * gathered[0].shape[1]
    tiles = total // TILE // seqs
    width = 2 * gathered[0].shape[2]
    return call(
        lambda *refs: project_inner_kernel(tiles, *refs),
        (total // TILE,),
        gathered_specs(gathered)
        + [full(weight[0]), full(weight[1])]
        + [pl.BlockSpec((1, EDGE, width), lambda i, s: (i // tiles, 0, 0)), full(taps), full(steps)],
        [
            tiled(LANES),
            tiled(LANES),
            tiled(2 * SIDE),
            tiled(8),
            tiled(1),
            pl.BlockSpec((1, EDGE, LANES), lambda i, s: (i // tiles, 0, 0)),
        ],
        [
            shape((total, LANES)),
            shape((total, LANES)),
            shape((total, 2 * SIDE), BF),
            shape((total, 8)),
            shape((total, 1)),
            shape((seqs, EDGE, LANES)),
        ],
        [pltpu.VMEM((TILE, width), BF), pltpu.VMEM((EDGE + TILE, LANES), F32)],
        1,
    )(scalars, *gathered, *weight, halo, taps, steps)


def project_gating_kernel(scalars, l, r, lo, ro, mine, theirs, root, gating_ref, query_ref, rows):
    place_rows(scalars, (l, r, lo, ro), rows)
    product = halves_product(rows[...], mine, theirs) * root[...]
    gating_ref[...] = product[:, :INNER]
    query_ref[...] = product[:, INNER:].astype(BF)


def project_gating(scalars, gathered, weight, root):
    total, width = root.shape[0], 2 * gathered[0].shape[2]
    return call(
        project_gating_kernel,
        (total // TILE,),
        gathered_specs(gathered) + [full(weight[0]), full(weight[1]), tiled(1)],
        [tiled(INNER), tiled(HD)],
        [shape((total, INNER)), shape((total, HD), BF)],
        [pltpu.VMEM((TILE, width), BF)],
        1,
    )(scalars, *gathered, *weight, root)


def rows_back_kernel(scalars, l, r, lo, ro, mine, theirs, ssm, gating, root, gain, mixer_ref, attn_ref, along_ref, gain_ref, rows):
    place_rows(scalars, (l, r, lo, ro), rows)
    product = halves_product(rows[...], mine, theirs)
    mixer = product[:, :INNER]
    mixer_ref[...] = mixer
    attn_ref[...] = product[:, INNER:].astype(BF)
    norm = ssm[...] * silu_value(gating[...]) * root[...]
    together = mixer * norm
    along_ref[0] = exact(jnp.ones((8, INNER), F32), together * gain[...], (1, 1))

    @pl.when(pl.program_id(0) == 0)
    def _():
        gain_ref[...] = jnp.zeros_like(gain_ref)

    gain_ref[...] += jnp.sum(together, axis=0, keepdims=True)


def rows_back(scalars, gathered, weight, ssm, gating, root, gain):
    total, width = root.shape[0], 2 * gathered[0].shape[2]
    tiles = total // TILE
    return call(
        rows_back_kernel,
        (tiles,),
        gathered_specs(gathered)
        + [full(weight[0]), full(weight[1]), tiled(INNER), tiled(INNER), tiled(1), full(gain)],
        [
            tiled(INNER),
            tiled(HD),
            pl.BlockSpec((1, 8, TILE), lambda i, s: (i, 0, 0)),
            pl.BlockSpec((1, INNER), lambda i, s: (0, 0)),
        ],
        [
            shape((total, INNER)),
            shape((total, HD), BF),
            shape((tiles, 8, TILE)),
            shape((1, INNER)),
        ],
        [pltpu.VMEM((TILE, width), BF)],
        1,
    )(scalars, *gathered, *weight, ssm, gating, root, gain)


def back_dot_kernel(terms, halves, scalars, *refs):
    ins, outs = refs[: terms * 4], refs[terms * 4 :]
    i = pl.program_id(0)
    for half in range(2):
        product = None
        for t in range(terms):
            first, second = ins[4 * t], ins[4 * t + 1]
            weight = ins[4 * t + 2 + half]
            rows = jnp.concatenate([first[...], second[...]], 0)
            at = (1, 1) if weight.shape[1] == rows.shape[1] else (1, 0)
            one = dot(rows, weight[...], at)
            product = one if product is None else product + one
        product = product.reshape(outs[half].shape)

        @pl.when(i < halves)
        def _():
            outs[2 + half][...] = product.astype(BF)

        @pl.when(i >= halves)
        def _():
            outs[half][...] = product


def back_dot(order, terms):
    total = terms[0][0].shape[0]
    half = terms[0][1][0].shape[0]
    halves = total // TILE // 2
    specs, arrays = [], []
    for rows, weights in terms:
        width = rows.shape[1]
        specs += [
            pl.BlockSpec((BLOCK, width), lambda i, s: (s[(2 * i + 4) % 8], 0)),
            pl.BlockSpec((BLOCK, width), lambda i, s: (s[(2 * i + 5) % 8], 0)),
            full(weights[0]),
            full(weights[1]),
        ]
        arrays += [rows, rows, *weights]
    kept_spec = pl.BlockSpec((2, BLOCK, half), lambda i, s: (jnp.maximum(i - halves, 0), 0, 0))
    given_spec = pl.BlockSpec((2, BLOCK, half), lambda i, s: (jnp.minimum(i, halves - 1), 0, 0))
    blocks = total // BLOCK // 2
    return call(
        lambda *refs: back_dot_kernel(len(terms), halves, *refs),
        (2 * halves,),
        specs,
        [kept_spec, kept_spec, given_spec, given_spec],
        [shape((blocks, BLOCK, half))] * 2 + [shape((blocks, BLOCK, half), BF)] * 2,
        (),
        1,
    )(order, *arrays)


def grad_dot_kernel(scalars, own, other, against, *refs):
    out, ordered = refs[-2], refs[-1]

    @pl.when(pl.program_id(0) == 0)
    def _():
        for k in range(8):
            start = pl.multiple_of(scalars[k] * BLOCK, BLOCK)
            ordered[k * BLOCK : (k + 1) * BLOCK] = against[pl.ds(start, BLOCK), :]

    tile = own.shape[2]
    rows = own.shape[0] * own.shape[1]
    product = dot(own[...].reshape(rows, tile), ordered[:rows], (0, 0))
    product = product + dot(other[...].reshape(rows, tile), ordered[rows:], (0, 0))
    out[...] = product.astype(out.dtype)


def grad_dot(order, own, other, against, dtype):
    half = own.shape[2]
    total, width = against.shape
    tile = 512
    spec = pl.BlockSpec((own.shape[0], own.shape[1], tile), lambda i, s: (0, 0, i))
    return call(
        grad_dot_kernel,
        (half // tile,),
        [spec, spec, full(against)],
        pl.BlockSpec((tile, width), lambda i, s: (i, 0)),
        shape((half, width), dtype),
        [pltpu.VMEM((total, width), BF)],
        1,
    )(order, own, other, against)


def peers_half(order, gathered, against):
    left, right, left_other, right_other = gathered
    theirs = swap(grad_dot(order, right, right_other, against, BF), "sh")
    return grad_dot(order, left, left_other, against, F32), theirs


def feed_kernel(parts, l, r, lo, ro, cl, cr, clo, cro, gm, gt, lm, lt, dm, dt, active_ref, gate_ref, lift_ref):
    i = pl.program_id(0)

    def run(left, right, cleft, cright):
        half = left.shape[2]

        def product(a, b, mine, theirs):
            return dot(a[...].reshape(TILE, half), mine[...], (1, 0)) + dot(
                b[...].reshape(TILE, half), theirs[...], (1, 0)
            )

        gate = product(left, right, gm, gt)
        lift = product(left, right, lm, lt)
        grad = product(cleft, cright, dm, dt)
        sigmoid_part = jax.nn.sigmoid(gate)
        swish = gate * sigmoid_part
        active_ref[...] = (swish * lift).astype(BF)
        gate_ref[...] = (
            grad * lift * sigmoid_part * (1.0 + gate * (1.0 - sigmoid_part))
        ).astype(BF)
        lift_ref[...] = (grad * swish).astype(BF)

    @pl.when(i < parts)
    def _():
        run(l, r, cl, cr)

    @pl.when(i >= parts)
    def _():
        run(lo, ro, clo, cro)


def feed_block(rows, cotangent, gate, lift, drop):
    blocks, count, half = rows[0].shape
    total = 2 * blocks * count
    parts = total // TILE // 2
    own = pl.BlockSpec((2, count, half), lambda i: (jnp.minimum(i, parts - 1), 0, 0))
    other = pl.BlockSpec((2, count, half), lambda i: (jnp.maximum(i - parts, 0), 0, 0))
    weights = [*gate, *lift, *drop]
    return call(
        lambda *refs: feed_kernel(parts, *refs),
        (2 * parts,),
        [own, own, other, other] * 2 + [full(w) for w in weights],
        [tiled(LANES)] * 3,
        [shape((total, LANES), BF)] * 3,
    )(*rows, *cotangent, *weights)


def scores_of(place, queries, keys):
    count, whole = queries.shape[0], keys.shape[0]
    scores = dot(queries, keys, (1, 1)) * HD**-0.5
    row = place + pl.program_id(1) * count + lax.broadcasted_iota(jnp.int32, (count, whole), 0)
    column = lax.broadcasted_iota(jnp.int32, (count, whole), 1)
    return scores, row >= column


def attend_kernel(place, queries, key_value, out_ref, log_ref):
    keys, values = key_value[0, :, :HD], key_value[0, :, HD:]
    scores, visible = scores_of(place[0], queries[...], keys)
    scores = jnp.where(visible, scores, negative)
    top = jnp.max(scores, axis=-1, keepdims=True)
    weights = jnp.exp(scores - top)
    total = jnp.sum(weights, axis=-1, keepdims=True)
    log_ref[...] = top + jnp.log(total)
    out_ref[...] = dot(weights.astype(BF), values, (1, 0)) / total


def attend_specs(seqs, total):
    tiles = total // TILE // seqs
    rows = lambda width: pl.BlockSpec((TILE, width), lambda n, i, s: (n * tiles + i, 0))
    return (seqs, tiles), rows


def attend(place, queries, key_value):
    seqs, whole, width = key_value.shape
    total = queries.shape[0]
    grid, rows = attend_specs(seqs, total)
    return call(
        attend_kernel,
        grid,
        [rows(HD), pl.BlockSpec((1, whole, width), lambda n, i, s: (n, 0, 0))],
        [rows(HD), rows(1)],
        [shape((total, HD)), shape((total, 1))],
        (),
        1,
    )(place, queries, key_value)


def attend_back_kernel(place, queries, grads, attended, logs, root, key_value, query_ref, sum_ref):
    keys, values = key_value[0, :, :HD], key_value[0, :, HD:]
    scores, visible = scores_of(place[0], queries[...], keys)
    probs = jnp.where(visible, jnp.exp(scores - logs[...]), 0.0)
    grad = grads[...]
    delta = jnp.sum(grad.astype(F32) * attended[...], axis=-1, keepdims=True)
    scores_grad = (probs * (dot(grad, values, (1, 1)) - delta)).astype(BF)
    query_ref[...] = (dot(scores_grad, keys, (1, 0)) * (HD**-0.5 * root[...])).astype(BF)

    @pl.when(pl.program_id(1) == 0)
    def _():
        sum_ref[...] = jnp.zeros_like(sum_ref)

    sum_ref[0, :, :HD] += dot(scores_grad, queries[...], (0, 0)) * HD**-0.5
    sum_ref[0, :, HD:] += dot(probs.astype(BF), grad, (0, 0))


def attend_back(place, queries, grads, attended, logs, root, key_value):
    seqs, whole, width = key_value.shape
    total = queries.shape[0]
    grid, rows = attend_specs(seqs, total)
    sums = pl.BlockSpec((1, whole, width), lambda n, i, s: (n, 0, 0))
    return call(
        attend_back_kernel,
        grid,
        [rows(HD), rows(HD), rows(HD), rows(1), rows(1), sums],
        [rows(HD), sums],
        [shape((total, HD), BF), shape((seqs, whole, width))],
        (),
        1,
    )(place, queries, grads, attended, logs, root, key_value)


def over_heads(values):
    rows = values.shape[0]
    return jnp.concatenate(
        [jnp.broadcast_to(values[:, h : h + 1], (rows, PM)) for h in range(HEADS)], 1
    )


def head_sums(values):
    channel = lax.broadcasted_iota(jnp.int32, (INNER, 8), 0)
    head = lax.broadcasted_iota(jnp.int32, (INNER, 8), 1)
    return exact(values, jnp.where(channel // PM == head, 1.0, 0.0), (1, 0))


def triangle():
    row = lax.broadcasted_iota(jnp.int32, (BLOCK, BLOCK), 0)
    column = lax.broadcasted_iota(jnp.int32, (BLOCK, BLOCK), 1)
    return row, column


def block_steps(step_pre, head):
    arg = step_pre[...] + head[0:1, :]
    size = jnp.maximum(arg, 0.0) + jnp.log1p(jnp.exp(-jnp.abs(arg)))
    row, column = triangle()
    cum = exact(jnp.where(row >= column, 1.0, 0.0), size * head[1:2, :], (1, 0))
    return arg, size, cum


def as_rows(values):
    row, column = triangle()
    return exact(values, jnp.where(row == column, 1.0, 0.0), (0, 0))


def as_columns(values):
    row, column = triangle()
    return exact(jnp.where(row == column, 1.0, 0.0), values, (1, 1))


def states_kernel(blocks, step_pre, head, conv, io, out_ref, decay_ref, run):
    i = pl.program_id(0)
    _, size, cum = block_steps(step_pre, head)
    last = cum[BLOCK - 1 :, :]
    feeding = jnp.exp(last - cum) * size
    inner = silu_value(conv[:, :INNER])
    fresh = dot(io[:, :NS], (over_heads(feeding) * inner).astype(BF), (0, 0))
    decay = over_heads(jnp.exp(last))

    @pl.when(i % blocks == 0)
    def _():
        run[...] = fresh
        decay_ref[0] = decay

    @pl.when(i % blocks != 0)
    def _():
        run[...] = decay * run[...] + fresh
        decay_ref[0] = decay_ref[0] * decay

    @pl.when(i % blocks == blocks - 1)
    def _():
        out_ref[0] = run[...].astype(BF)


def states(seqs, step_pre, head, conv, io):
    total = conv.shape[0]
    blocks = total // BLOCK // seqs
    return call(
        lambda *refs: states_kernel(blocks, *refs),
        (total // BLOCK,),
        [tiled(8, BLOCK), full(head), tiled(LANES, BLOCK), tiled(2 * NS, BLOCK)],
        [
            pl.BlockSpec((1, NS, INNER), lambda i: (i // blocks, 0, 0)),
            pl.BlockSpec((1, 1, INNER), lambda i: (i // blocks, 0, 0)),
        ],
        [shape((seqs, NS, INNER), BF), shape((seqs, 1, INNER))],
        [pltpu.VMEM((NS, INNER), F32)],
    )(step_pre, head, conv, io)


def fading_of(cum, cum_rows, h):
    row, column = triangle()
    span = cum[:, h : h + 1] - cum_rows[h : h + 1, :]
    return jnp.where(row >= column, jnp.exp(jnp.minimum(span, 0.0)), 0.0)


def ssm_kernel(blocks, step_pre, head, conv, io, gating, entry, ssm_ref, carried_ref, square_ref, run):
    i = pl.program_id(0)

    @pl.when(i % blocks == 0)
    def _():
        run[...] = entry[0].astype(F32)

    _, size, cum = block_steps(step_pre, head)
    size_rows, cum_rows = as_rows(size), as_rows(cum)
    last = cum[BLOCK - 1 :, :]
    inner = silu_value(conv[:, :INNER])
    inner_low = inner.astype(BF)
    in_state, out_state = io[:, :NS], io[:, NS:]
    carried = run[...].astype(BF)
    carried_ref[0] = carried
    pairing = dot(out_state, in_state, (1, 1))
    within = []
    for h in range(HEADS):
        mixing = fading_of(cum, cum_rows, h) * pairing * size_rows[h : h + 1, :]
        within.append(dot(mixing.astype(BF), inner_low[:, h * PM : (h + 1) * PM], (1, 0)))
    readout = dot(out_state, carried, (1, 0))
    ssm = (
        jnp.concatenate(within, 1)
        + over_heads(jnp.exp(cum)) * readout
        + over_heads(head[2:3, :]) * inner
    )
    ssm_ref[...] = ssm
    gated = ssm * silu_value(gating[...])
    square_ref[0] = exact(jnp.ones((8, INNER), F32), gated * gated, (1, 1))
    feeding = jnp.exp(last - cum) * size
    fresh = dot(in_state, (over_heads(feeding) * inner).astype(BF), (0, 0))
    run[...] = over_heads(jnp.exp(last)) * run[...] + fresh


def ssm_block(seqs, step_pre, head, conv, io, gating, entry):
    total = conv.shape[0]
    blocks = total // BLOCK // seqs
    return call(
        lambda *refs: ssm_kernel(blocks, *refs),
        (total // BLOCK,),
        [
            tiled(8, BLOCK),
            full(head),
            tiled(LANES, BLOCK),
            tiled(2 * NS, BLOCK),
            tiled(INNER, BLOCK),
            pl.BlockSpec((1, NS, INNER), lambda i: (i // blocks, 0, 0)),
        ],
        [
            tiled(INNER, BLOCK),
            pl.BlockSpec((1, NS, INNER), lambda i: (i, 0, 0)),
            pl.BlockSpec((1, 8, BLOCK), lambda i: (i, 0, 0)),
        ],
        [
            shape((total, INNER)),
            shape((total // BLOCK, NS, INNER), BF),
            shape((total // BLOCK, 8, BLOCK)),
        ],
        [pltpu.VMEM((NS, INNER), F32)],
    )(step_pre, head, conv, io, gating, entry)


def states_back_kernel(blocks, step_pre, head, io, mixer, ssm, gating, mixer_root, along, gain, root, grad_ref, gating_ref, out_ref, run):
    i = pl.program_id(0)
    _, _, cum = block_steps(step_pre, head)
    gate = gating[...]
    sigmoid_part = jax.nn.sigmoid(gate)
    act = gate * sigmoid_part
    values = ssm[...]
    norm = values * act * mixer_root[...]
    gated_grad = mixer_root[...] * (mixer[...] * gain[...] - norm * along[...])
    grad = gated_grad * act
    grad_ref[...] = grad
    slope = sigmoid_part * (1.0 + gate * (1.0 - sigmoid_part))
    gating_ref[...] = (gated_grad * values * slope * root[...]).astype(BF)
    grown = (over_heads(jnp.exp(cum)) * grad).astype(BF)
    fresh = dot(io[:, NS:], grown, (0, 0))
    decay = over_heads(jnp.exp(cum[BLOCK - 1 :, :]))

    @pl.when(i % blocks == 0)
    def _():
        run[...] = fresh

    @pl.when(i % blocks != 0)
    def _():
        run[...] = decay * run[...] + fresh

    @pl.when(i % blocks == blocks - 1)
    def _():
        out_ref[0] = run[...].astype(BF)


def states_back(seqs, step_pre, head, io, mixer, ssm, gating, mixer_root, along, gain, root):
    total = ssm.shape[0]
    many = total // BLOCK
    blocks = many // seqs
    back = lambda width: pl.BlockSpec((BLOCK, width), lambda i: (many - 1 - i, 0))
    return call(
        lambda *refs: states_back_kernel(blocks, *refs),
        (many,),
        [back(8), full(head), back(2 * NS), back(INNER), back(INNER), back(INNER)]
        + [back(1), back(1), full(gain), back(1)],
        [
            back(INNER),
            back(INNER),
            pl.BlockSpec((1, NS, INNER), lambda i: (seqs - 1 - i // blocks, 0, 0)),
        ],
        [shape((total, INNER)), shape((total, INNER), BF), shape((seqs, NS, INNER), BF)],
        [pltpu.VMEM((NS, INNER), F32)],
    )(step_pre, head, io, mixer, ssm, gating, mixer_root, along, gain, root)


def ssm_back_kernel(blocks, side, step_pre, head, conv, io, grads, carried_ref, entry, key_value, root, conv_ref, parts_ref, step_ref, sums_ref, later):
    i = pl.program_id(0)

    @pl.when(i % blocks == 0)
    def _():
        later[...] = entry[0].astype(F32)

    @pl.when(i == 0)
    def _():
        sums_ref[...] = jnp.zeros_like(sums_ref)

    arg, size, cum = block_steps(step_pre, head)
    size_rows, cum_rows = as_rows(size), as_rows(cum)
    last = cum[BLOCK - 1 :, :]
    growth, to_end, decay = jnp.exp(cum), jnp.exp(last - cum), jnp.exp(last)
    feeding = to_end * size
    conv_sum = conv[:, :INNER]
    inner = silu_value(conv_sum)
    inner_low = inner.astype(BF)
    in_state, out_state = io[:, :NS], io[:, NS:]
    carried = carried_ref[0]
    after = later[...]
    after_low = after.astype(BF)
    grad = grads[...]
    grad_low = grad.astype(BF)
    pairing = dot(out_state, in_state, (1, 1))
    readout = dot(out_state, carried, (1, 0))
    spread = dot(in_state, after_low, (1, 0))
    grown = (over_heads(growth) * grad).astype(BF)
    feeding_wide = over_heads(feeding)
    fed_inner = (feeding_wide * inner).astype(BF)
    pairing_grad = jnp.zeros((BLOCK, BLOCK), F32)
    inner_parts, flows, step_rows = [], [], []
    for h in range(HEADS):
        at = slice(h * PM, (h + 1) * PM)
        fading = fading_of(cum, cum_rows, h)
        sized = size_rows[h : h + 1, :]
        mixing = (fading * pairing * sized).astype(BF)
        faded = dot(grad_low[:, at], inner_low[:, at], (1, 1)) * fading
        pairing_grad = pairing_grad + faded * sized
        stepwise = faded * pairing
        step_rows.append(jnp.sum(stepwise, axis=0, keepdims=True))
        flows.append(jnp.sum(stepwise * sized, axis=1, keepdims=True))
        inner_parts.append(dot(mixing, grad_low[:, at], (0, 0)))
    empty_row, empty_column = jnp.zeros((2, BLOCK), F32), jnp.zeros((BLOCK, 2), F32)
    step_rows = jnp.concatenate(step_rows + [empty_row], 0)
    flow = jnp.concatenate(flows + [empty_column], 1)
    pairing_low = pairing_grad.astype(BF)
    out_grad = dot(pairing_low, in_state, (1, 0)) + dot(grown, carried, (1, 1))
    in_grad = dot(pairing_low, out_state, (0, 0)) + dot(fed_inner, after_low, (1, 1))
    inner_grad = (
        jnp.concatenate(inner_parts, 1) + over_heads(head[2:3, :]) * grad + feeding_wide * spread
    )
    conv_ref[...] = inner_grad * silu_slope(conv_sum)
    for rank in range(RANKS):
        source = in_grad if rank < RANKS // 2 else out_grad
        at = (rank % 4) * SIDE
        own = jnp.where(side[0] == rank // 4, 1.0, 0.0)
        parts_ref[rank] = jnp.concatenate(
            [source[:, at : at + SIDE], key_value[:, at : at + SIDE] * own], 1
        ).astype(BF)
    feeding_grad = head_sums(spread * inner)
    fed = feeding_grad * feeding
    through = jnp.sum(after * carried.astype(F32), axis=0, keepdims=True)
    through = head_sums(jnp.broadcast_to(through, (8, INNER)))[:1]
    last_grad = jnp.sum(fed, axis=0, keepdims=True) + through * decay
    cum_grad = flow - as_columns(step_rows * size_rows) + head_sums(grad * readout) * growth - fed
    row, column = triangle()
    increment = exact(jnp.where(column >= row, 1.0, 0.0), cum_grad, (1, 0)) + last_grad
    rates = head[1:2, :]
    step_grad = as_columns(step_rows) + feeding_grad * to_end + increment * rates
    arg_grad = step_grad * jax.nn.sigmoid(arg)
    step_ref[...] = (arg_grad * root[...]).astype(BF)
    skip = jnp.broadcast_to(jnp.sum(grad * inner, axis=0, keepdims=True), (8, INNER))
    sums_ref[0:1, :] += jnp.sum(arg_grad, axis=0, keepdims=True)
    sums_ref[1:2, :] += jnp.sum(increment * size, axis=0, keepdims=True) * rates
    sums_ref[2:3, :] += head_sums(skip)[:1]
    later[...] = over_heads(decay) * after + dot(out_state, grown, (0, 0))


def ssm_back(side, seqs, step_pre, head, conv, io, grads, carried, entry, key_value, root):
    total = conv.shape[0]
    many = total // BLOCK
    blocks = many // seqs
    back = lambda width: pl.BlockSpec((BLOCK, width), lambda i, s: (many - 1 - i, 0))
    return call(
        lambda *refs: ssm_back_kernel(blocks, *refs),
        (many,),
        [back(8), full(head), back(LANES), back(2 * NS), back(INNER)]
        + [
            pl.BlockSpec((1, NS, INNER), lambda i, s: (many - 1 - i, 0, 0)),
            pl.BlockSpec((1, NS, INNER), lambda i, s: (seqs - 1 - i // blocks, 0, 0)),
            back(2 * HD),
            back(1),
        ],
        [
            back(INNER),
            pl.BlockSpec((RANKS, BLOCK, 2 * SIDE), lambda i, s: (0, many - 1 - i, 0)),
            back(8),
            pl.BlockSpec((8, 8), lambda i, s: (0, 0)),
        ],
        [
            shape((total, INNER)),
            shape((RANKS, total, 2 * SIDE), BF),
            shape((total, 8), BF),
            shape((8, 8)),
        ],
        [pltpu.VMEM((NS, INNER), F32)],
        1,
    )(side, step_pre, head, conv, io, grads, carried, entry, key_value, root)


def conv_back_kernel(tiles, inner, parts, conv, pre, edge, grad_ref, sums_ref, line):
    i = pl.program_id(0)
    got = jnp.sum(parts[...].astype(F32), axis=0)
    lane = lax.broadcasted_iota(jnp.int32, got.shape, 1)
    got = jnp.where(lane < SIDE, got * silu_slope(conv[:, INNER:]), got)
    grad = jnp.concatenate([inner[...], got], 1)
    grad_ref[...] = grad

    @pl.when(i % tiles == 0)
    def _():
        line[:EDGE] = edge[0]

    @pl.when(i % tiles != 0)
    def _():
        line[:EDGE] = line[TILE:]

    @pl.when(i == 0)
    def _():
        sums_ref[...] = jnp.zeros_like(sums_ref)

    line[EDGE:] = pre[...]
    for k in range(KC):
        before = line[EDGE - (KC - 1) + k : EDGE - (KC - 1) + k + TILE, :]
        sums_ref[k : k + 1, :] += jnp.sum(grad * before, axis=0, keepdims=True)
    sums_ref[KC : KC + 1, :] += jnp.sum(grad, axis=0, keepdims=True)


def conv_back(inner, parts, conv, pre, edge):
    total = conv.shape[0]
    tiles = total // TILE // edge.shape[0]
    return call(
        lambda *refs: conv_back_kernel(tiles, *refs),
        (total // TILE,),
        [
            tiled(INNER),
            pl.BlockSpec((RANKS, TILE, 2 * SIDE), lambda i: (0, i, 0)),
            tiled(LANES),
            tiled(LANES),
            pl.BlockSpec((1, EDGE, LANES), lambda i: (i // tiles, 0, 0)),
        ],
        [tiled(LANES), pl.BlockSpec((8, LANES), lambda i: (0, 0))],
        [shape((total, LANES)), shape((8, LANES))],
        [pltpu.VMEM((EDGE + TILE, LANES), F32)],
    )(inner, parts, conv, pre, edge)


def pre_back_kernel(tiles, grad, after, follow, taps, root, out_ref, line):
    i = pl.program_id(0)
    line[:TILE] = grad[...]

    @pl.when(i % tiles == tiles - 1)
    def _():
        line[TILE:] = follow[0]

    @pl.when(i % tiles != tiles - 1)
    def _():
        line[TILE:] = after[...]

    total = taps[KC - 1 : KC, :] * line[:TILE, :]
    for k in range(KC - 1):
        total = total + taps[k : k + 1, :] * line[KC - 1 - k : KC - 1 - k + TILE, :]
    out_ref[...] = (total * root[...]).astype(BF)


def pre_back(grad, follow, taps, root):
    total = grad.shape[0]
    tiles = total // TILE // follow.shape[0]
    last = total // EDGE - 1
    return call(
        lambda *refs: pre_back_kernel(tiles, *refs),
        (total // TILE,),
        [
            tiled(LANES),
            pl.BlockSpec((EDGE, LANES), lambda i: (jnp.minimum((i + 1) * (TILE // EDGE), last), 0)),
            pl.BlockSpec((1, EDGE, LANES), lambda i: (i // tiles, 0, 0)),
            full(taps),
            tiled(1),
        ],
        tiled(LANES),
        shape((total, LANES), BF),
        [pltpu.VMEM((TILE + EDGE, LANES), F32)],
    )(grad, grad, follow, taps, root)


def local(
    tokens,
    cotangent,
    norm_gain,
    gating_weight,
    inner_weight,
    state_weight,
    step_weight,
    conv_weight,
    conv_bias,
    mixer_gain,
    mixer_out,
    query_weight,
    key_weight,
    value_weight,
    output_weight,
    feed_gain,
    gate_matrix,
    lift_matrix,
    drop_matrix,
    step_bias,
    decay_log,
    skip_scale,
):
    sh, sl, ch = lax.axis_size("sh"), lax.axis_size("sl"), lax.axis_size("ch")
    world = sh * sl * ch * 4
    rows, width = tokens.shape
    drows = norm_gain.shape[0]
    my_sl, my_zl, my_core = (lax.axis_index(axis) for axis in TEAM)
    rank = (my_sl * 2 + my_zl) * 2 + my_core
    total = RANKS * rows
    count = 4 * rows
    whole = ch * count

    order = team_order()
    straight = jnp.arange(8, dtype=jnp.int32)
    tiles = [((z ^ my_zl) * 2 + (s ^ my_sl)) for s in (0, 1) for z in (0, 1)]
    scalars = jnp.stack([my_core, *tiles]).astype(jnp.int32)
    place = (lax.axis_index("ch") * count).astype(jnp.int32).reshape(1)
    side_index = my_sl.astype(jnp.int32).reshape(1)

    def scaled(weight, gain):
        return (weight.astype(F32) * gain.astype(F32)[:, None]).astype(BF)

    key_value = jnp.stack(
        [key_weight.reshape(drows, HK, 2, SIDE), value_weight.reshape(drows, HK, 2, SIDE)], 2
    ).reshape(drows, RANKS * SIDE)
    pack_in = jnp.concatenate(
        [
            by_rank(scaled(w, norm_gain))
            for w in (inner_weight, state_weight, key_value, gating_weight, query_weight)
        ],
        2,
    )
    own_tokens = shuffled(tokens, sh, sl, ch)
    own_cotangent = shuffled(cotangent, sh, sl, ch)
    mixed_in = ranks_exchange(pack_in)
    team_tokens = team_gather(own_tokens)
    w_inner = peers_gather(mixed_in[:, :LANES])
    w_gating = peers_gather(mixed_in[:, LANES:])

    conv_own, gain_own = conv_weight.shape[1], mixer_gain.shape[0]
    step_sent = jnp.broadcast_to(
        scaled(step_weight, norm_gain).T.reshape(1, sl, 1, 4, HEADS * drows),
        (sh, sl, ch, 4, HEADS * drows),
    ).reshape(world, HEADS * drows)
    shared = jnp.concatenate([conv_weight.reshape(-1), conv_bias, mixer_gain])
    small = lax.all_to_all(
        jnp.concatenate([jnp.broadcast_to(shared[None], (world, shared.shape[0])), step_sent], 1),
        WORLD,
        split_axis=0,
        concat_axis=0,
        tiled=True,
    )
    at = (KC + 1) * conv_own
    wide_conv = small[:, :at].reshape(world, KC + 1, conv_own)
    wide_conv = wide_conv.transpose(1, 0, 2).reshape(KC + 1, -1).astype(F32)
    wide_gain = small[:, at : at + gain_own].reshape(1, -1).astype(F32)
    own_step = small[:, at + gain_own :].reshape(sh, sl, ch, 4, HEADS, drows).swapaxes(1, 2)
    own_step = relative(relative(own_step, "sh", 0), "ch", 1)
    own_step = own_step.reshape(-1, HEADS, drows).swapaxes(0, 1).reshape(HEADS, width)
    own_step = jnp.pad(own_step, ((0, 8 - HEADS), (0, 0)))
    taps = jnp.concatenate(
        [
            lax.dynamic_slice_in_dim(wide_conv, rank * INNER, INNER, 1),
            lax.dynamic_slice_in_dim(wide_conv, DI + rank * SIDE, SIDE, 1),
            jnp.zeros((KC + 1, LANES - CONV), F32).at[KC - 1].set(1.0),
        ],
        1,
    )
    taps = jnp.pad(taps, ((0, 8 - KC - 1), (0, 0)))
    own_gain = lax.dynamic_slice_in_dim(wide_gain, rank * INNER, INNER, 1)
    head = jnp.stack([step_bias, -jnp.exp(decay_log), skip_scale])
    head = lax.dynamic_slice_in_dim(head, rank * HEADS, HEADS, 1)
    head = jnp.pad(head, ((0, 5), (0, 8 - HEADS)))

    ends = []
    for seq in range(sl):
        at_block = 2 * (1 - my_zl) + (seq ^ my_sl)
        halves = []
        for own, other in ((team_tokens[0], team_tokens[2]), (team_tokens[1], team_tokens[3])):
            own = lax.dynamic_index_in_dim(own[:, rows - EDGE :], at_block, 0, False)
            other = lax.dynamic_index_in_dim(other[:, rows - EDGE :], at_block, 0, False)
            halves.append(jnp.where(my_core == 1, own, other))
        ends.append(jnp.concatenate(halves, 1))
    halo = shifted(jnp.stack(ends), 1)
    if ch == 2:
        halo = jnp.flip(halo.reshape(sl, EDGE, sh, ch, -1), 3).reshape(sl, EDGE, width)

    pre, conv, side, step_pre, root, edge = project_inner(
        scalars, team_tokens, w_inner, halo, taps, own_step
    )
    sides = lax.all_gather(side, TEAM)
    gating, queries = project_gating(scalars, team_tokens, w_gating, root)
    io = sides[:, :, :SIDE].transpose(1, 0, 2).reshape(total, 2 * NS)
    key_value_rows = lax.dynamic_slice_in_dim(sides[:, :, SIDE:], my_sl * 4, 4, 0)
    key_value_rows = key_value_rows.transpose(1, 0, 2).reshape(sl, count, 2 * HD)
    if ch == 2:
        key_value_rows = paired(key_value_rows, swap(key_value_rows, "ch"), "ch", 1)
        key_value_rows = key_value_rows.reshape(sl, whole, 2 * HD)
    elif ch > 2:
        key_value_rows = lax.all_gather(key_value_rows, "ch", axis=1, tiled=True)
    leaving, piece_decay = states(sl, step_pre, head, conv, io)
    entry = entering(piece_decay[:, 0], leaving, False)
    attended, logs = attend(place, queries, key_value_rows)
    ssm, carried, square = ssm_block(sl, step_pre, head, conv, io, gating, entry)
    mixer_root = lax.rsqrt(team_sum(square[:, 0]) / DI + epsilon).reshape(total, 1)
    branch_rows = jnp.concatenate(
        [(ssm * silu_value(gating) * mixer_root * own_gain).astype(BF), attended.astype(BF)], 1
    )

    pack_rest = jnp.concatenate(
        [by_rank(mixer_out.T), by_rank(output_weight.T)]
        + [by_rank(scaled(w, feed_gain)) for w in (gate_matrix, lift_matrix)]
        + [by_rank(drop_matrix.T)],
        2,
    )
    mixed_rest = ranks_exchange(pack_rest)
    w_out = peers_gather(mixed_rest[:, :LANES])
    w_gate = peers_gather(mixed_rest[:, LANES : 2 * LANES])
    w_lift = peers_gather(mixed_rest[:, 2 * LANES : 3 * LANES])
    w_drop = peers_gather(mixed_rest[:, 3 * LANES :])
    team_cotangent = team_gather(own_cotangent)

    branch = team_scatter(back_dot(order, [(branch_rows, w_out)]))

    residual = own_tokens.astype(F32) + branch
    feed_root = inverse_root(residual)
    feed_rows = team_gather((residual * feed_root).astype(BF))
    active, gate_rows_grad, lift_rows_grad = feed_block(
        feed_rows, team_cotangent, w_gate, w_lift, w_drop
    )
    feed_grad = team_scatter(
        back_dot(straight, [(gate_rows_grad, w_gate), (lift_rows_grad, w_lift)])
    )
    residual_grad = own_cotangent.astype(F32) + norm_back(residual, feed_root, feed_grad)
    branch_grad = team_gather(residual_grad.astype(BF))
    drop_half = peers_half(straight, team_cotangent, active)
    gate_half = peers_half(straight, feed_rows, gate_rows_grad)
    lift_half = peers_half(straight, feed_rows, lift_rows_grad)
    active, drop_half, gate_half, lift_half, branch_grad = lax.optimization_barrier(
        (active, drop_half, gate_half, lift_half, branch_grad)
    )
    feed_back = ranks_return(
        [peers_sum(*drop_half), peers_sum(*gate_half), peers_sum(*lift_half)], drows
    ).astype(F32)
    drop_back = feed_back[:, :, :LANES]
    gate_back = feed_back[:, :, LANES : 2 * LANES]
    lift_back = feed_back[:, :, 2 * LANES :]
    layer_output = (residual + team_scatter(back_dot(straight, [(active, w_drop)]))).astype(BF)

    mixer_rows_grad, attn_grad, along, gain_part = rows_back(
        scalars, branch_grad, w_out, ssm, gating, mixer_root, own_gain
    )
    along = team_sum(along[:, 0]).reshape(total, 1) / DI
    query_grad, key_value_part = attend_back(
        place, queries, attn_grad, attended, logs, root, key_value_rows
    )
    if ch == 1:
        key_value_grad = key_value_part
    elif ch == 2:
        halves = key_value_part.reshape(sl, ch, count, 2 * HD)
        key_value_grad = added(
            kept(halves, "ch", 1), swap(given(halves, "ch", 1).astype(BF), "ch")
        )
    else:
        key_value_grad = lax.psum_scatter(
            key_value_part.astype(BF), "ch", scatter_dimension=1, tiled=True
        ).astype(F32)
    ssm_grad, gating_grad, leaving_back = states_back(
        sl, step_pre, head, io, mixer_rows_grad, ssm, gating, mixer_root, along, own_gain, root
    )
    entry_back = entering(piece_decay[:, 0], leaving_back, True)
    inner_conv_grad, parts, step_rows_grad, sums = ssm_back(
        side_index,
        sl,
        step_pre,
        head,
        conv,
        io,
        ssm_grad,
        carried,
        entry_back,
        key_value_grad.reshape(total, 2 * HD),
        root,
    )
    parts = lax.all_to_all(parts, TEAM, split_axis=0, concat_axis=0, tiled=True)
    gating_rows_grad = jnp.concatenate([gating_grad, query_grad], 1)
    gating_half = peers_half(order, team_tokens, gating_rows_grad)
    out_half = peers_half(order, branch_grad, branch_rows)
    conv_grad, conv_sums = conv_back(inner_conv_grad, parts, conv, pre, edge)
    follow = shifted(conv_grad.reshape(sl, count, LANES)[:, :EDGE], -1)
    inner_rows_grad = pre_back(conv_grad, follow, taps, root)
    step_halves = (own_step[:, : width // 2], own_step[:, width // 2 :])
    hidden_grad = team_scatter(
        back_dot(
            order,
            [
                (inner_rows_grad, w_inner),
                (gating_rows_grad, w_gating),
                (step_rows_grad, step_halves),
            ],
        )
    )
    inner_half = peers_half(order, team_tokens, inner_rows_grad)
    mixer_back = ranks_return(
        [peers_sum(*out_half), peers_sum(*gating_half), peers_sum(*inner_half)], drows
    ).astype(F32)
    out_back = mixer_back[:, :, :LANES]
    gating_back = mixer_back[:, :, LANES : 2 * LANES]
    inner_back = mixer_back[:, :, 2 * LANES :]
    token_values = own_tokens.astype(F32)
    token_root = inverse_root(token_values)
    tokens_grad = residual_grad + norm_back(token_values, token_root, hidden_grad / token_root)
    left, right, left_other, right_other = team_tokens
    step_back = jnp.concatenate(
        [
            grad_dot(order, left, left_other, step_rows_grad, F32),
            grad_dot(order, right, right_other, step_rows_grad, F32),
        ],
        0,
    )[:, :HEADS].T

    def placed(part, extent, at):
        base = jnp.zeros(part.shape[:-1] + (extent,), F32)
        return lax.dynamic_update_slice_in_dim(base, part, at, part.ndim - 1)

    conv_all = jnp.concatenate(
        [
            placed(conv_sums[: KC + 1, :INNER], DI, rank * INNER),
            placed(conv_sums[: KC + 1, INNER:CONV], 2 * NS, rank * SIDE),
        ],
        1,
    )
    gain_all = placed(gain_part[0], DI, rank * INNER)
    step_all = step_back.reshape(HEADS, -1, drows).swapaxes(0, 1)
    step_all = step_all.reshape(sh, ch, sl, 4, HEADS * drows)
    step_all = relative(relative(step_all, "sh", 0), "ch", 1).swapaxes(1, 2)
    per_head = jnp.concatenate(
        [placed(sums[at, :HEADS], HM, rank * HEADS) for at in range(3)]
    )
    sent = jnp.concatenate(
        [
            conv_all.reshape(KC + 1, world, conv_own).swapaxes(0, 1).reshape(world, -1),
            gain_all.reshape(world, -1),
            step_all.reshape(world, -1),
            jnp.broadcast_to(per_head[None], (world, 3 * HM)),
        ],
        1,
    )
    got_all = lax.all_to_all(sent, WORLD, split_axis=0, concat_axis=0, tiled=True)
    at = KC * conv_own + conv_own + gain_own
    step_core = got_all[:, at : at + HEADS * drows].reshape(sh, sl, ch, 4, HEADS, drows)
    step_core = jnp.sum(step_core, axis=(0, 2)).reshape(HM, drows).T
    got = jnp.sum(got_all, axis=0)
    at = 0
    conv_out = got[at : at + KC * conv_own].reshape(KC, conv_own)
    at += KC * conv_own
    conv_bias_out = got[at : at + conv_own]
    at += conv_own
    gain_out = got[at : at + gain_own]
    at += gain_own + HEADS * drows
    bias_out, decay_out, skip_out = (got[at + i * HM : at + (i + 1) * HM] for i in range(3))

    def against(weight, grad):
        return jnp.sum(weight.astype(F32) * grad, axis=1)

    inner_core = to_columns(inner_back[:, :, :INNER])
    state_core = to_columns(inner_back[:, :, INNER:CONV])
    key_value_core = to_columns(inner_back[:, :, CONV:]).reshape(drows, HK, 2, 2 * SIDE)
    key_core = key_value_core[:, :, 0].reshape(drows, HK * HD)
    value_core = key_value_core[:, :, 1].reshape(drows, HK * HD)
    gating_core = to_columns(gating_back[:, :, :INNER])
    query_core = to_columns(gating_back[:, :, INNER:])
    gate_core, lift_core = to_columns(gate_back), to_columns(lift_back)
    norm_out = (
        against(gating_weight, gating_core)
        + against(inner_weight, inner_core)
        + against(state_weight, state_core)
        + against(step_weight, step_core)
        + against(query_weight, query_core)
        + against(key_weight, key_core)
        + against(value_weight, value_core)
    )
    feed_out = against(gate_matrix, gate_core) + against(lift_matrix, lift_core)
    norm_scale = norm_gain.astype(F32)[:, None]
    feed_scale = feed_gain.astype(F32)[:, None]
    mixer_out_out = out_back[:, :, :INNER].transpose(0, 2, 1).reshape(DI, drows)
    output_out = out_back[:, :, INNER:].transpose(0, 2, 1).reshape(HA * HD, drows)
    drop_out = drop_back.transpose(0, 2, 1).reshape(-1, drows)
    return (
        unshuffled(layer_output, sh, sl, ch),
        unshuffled(tokens_grad, sh, sl, ch),
        norm_out,
        gating_core * norm_scale,
        inner_core * norm_scale,
        state_core * norm_scale,
        step_core * norm_scale,
        conv_out,
        conv_bias_out,
        gain_out,
        mixer_out_out,
        query_core * norm_scale,
        key_core * norm_scale,
        value_core * norm_scale,
        output_out,
        feed_out,
        gate_core * feed_scale,
        lift_core * feed_scale,
        drop_out,
        bias_out,
        decay_out,
        skip_out,
    )


def solution(mesh):
    seq, ctx = mesh.shape["seq"], mesh.shape["ctx"]
    fine = Mesh(mesh.devices.reshape(seq // 2, 2, ctx // 4, 2, 2), WORLD)
    lead, vector, tail = P(WORLD, None), P(WORLD), P(None, WORLD)
    in_specs = (
        lead,
        lead,
        vector,
        lead,
        lead,
        lead,
        lead,
        tail,
        vector,
        vector,
        tail,
        lead,
        lead,
        lead,
        tail,
        vector,
        lead,
        lead,
        tail,
        P(),
        P(),
        P(),
    )
    out_specs = (
        lead,
        lead,
        vector,
        lead,
        lead,
        lead,
        lead,
        tail,
        vector,
        vector,
        tail,
        lead,
        lead,
        lead,
        tail,
        vector,
        lead,
        lead,
        tail,
        P(),
        P(),
        P(),
    )
    return jax.shard_map(local, mesh=fine, in_specs=in_specs, out_specs=out_specs, check_vma=False)
```

```python
import jax
import jax.numpy as jnp
from jax import lax
from jax.experimental import pallas as pl
from jax.experimental.pallas import tpu as pltpu
from jax.sharding import Mesh
from jax.sharding import PartitionSpec as P

DI = 3072
HM = 48
PM = 64
NS = 256
KC = 4
HA = 8
HK = 2
HD = 128
FF = 4096
BLOCK = 128

epsilon = 1e-06
negative = -1e30
BF = jnp.bfloat16
F32 = jnp.float32

TEAM = ("sl", "zl", "core")
PEERS = ("sh", "ch")
WORLD = ("sh", "sl", "ch", "zl", "core")
RANKS = 8


def swap(value, axis):
    return lax.ppermute(value, axis, [(0, 1), (1, 0)])


def paired(mine, theirs, axis_name, dim):
    bit = lax.axis_index(axis_name)
    return jnp.where(bit == 0, jnp.stack([mine, theirs], dim), jnp.stack([theirs, mine], dim))


def kept(value, axis_name, dim):
    return lax.dynamic_index_in_dim(value, lax.axis_index(axis_name), dim, False)


def given(value, axis_name, dim):
    return lax.dynamic_index_in_dim(value, 1 - lax.axis_index(axis_name), dim, False)


def added(mine, theirs):
    return mine.astype(F32) + theirs.astype(F32)


def team_order():
    s, z, c = (lax.axis_index(axis) for axis in TEAM)
    blocks = [
        ((s ^ sl) * 2 + (z ^ zl)) * 2 + (c ^ core)
        for core in (0, 1)
        for zl in (0, 1)
        for sl in (0, 1)
    ]
    return jnp.stack(blocks).astype(jnp.int32)


def team_gather(rows):
    half = rows.shape[1] // 2
    left, right = rows[:, :half], rows[:, half:]
    left = jnp.stack([left, swap(left, "sl")])
    right = jnp.stack([right, swap(right, "zl")])
    left_z = swap(left, "zl")
    right_x = swap(right, "sl")
    left = jnp.concatenate([left, left_z], 0)
    right = jnp.stack([right[0], right_x[0], right[1], right_x[1]])
    return left, right, swap(left, "core"), swap(right, "core")


def team_scatter(parts):
    left, right, left_given, right_given = parts
    left_got, right_got = swap(left_given, "core"), swap(right_given, "core")
    left_z = swap(added(left[2:], left_got[2:]).astype(BF), "zl")
    right_x = swap(added(right[1::2], right_got[1::2]).astype(BF), "sl")
    left = added(left[:2], left_got[:2]) + left_z.astype(F32)
    right = added(right[0::2], right_got[0::2]) + right_x.astype(F32)
    left_x = swap(left[1].astype(BF), "sl")
    right_z = swap(right[1].astype(BF), "zl")
    return jnp.concatenate([added(left[0], left_x), added(right[0], right_z)], 1)


def team_sum(value):
    for axis in TEAM[::-1]:
        value = value + swap(value, axis)
    return value


def relative(value, axis_name, dim):
    if lax.axis_size(axis_name) != 2:
        return value
    return jnp.where(lax.axis_index(axis_name) == 0, value, jnp.flip(value, dim))


def together(*values):
    return lax.optimization_barrier(values)


def along_ch(part):
    size = lax.axis_size("ch")
    if size == 2:
        return jnp.concatenate([part, swap(part, "ch")], 0)
    return lax.all_gather(part, "ch", axis=0, tiled=True)


def peers_gather(parts):
    out = []
    ready = along_ch(parts[0])
    for part in parts[1:]:
        mine = ready
        theirs, ready = together(swap(mine, "sh"), along_ch(part))
        out.append((mine, theirs))
    return out + [(ready, swap(ready, "sh"))]


def ranks_exchange(pack):
    mixed = lax.all_to_all(pack, TEAM, split_axis=0, concat_axis=0, tiled=True)
    return mixed.reshape(-1, pack.shape[2])


def ch_part(part):
    size = lax.axis_size("ch")
    if size == 2:
        half = part.shape[0] // 2
        part = added(part[:half], swap(part[half:].astype(BF), "ch"))
    elif size > 2:
        part = lax.psum_scatter(part.astype(BF), "ch", scatter_dimension=0, tiled=True)
    return part.astype(BF)


def ranks_return(parts, rows):
    pack = jnp.concatenate([p.reshape(RANKS, rows, -1) for p in parts], 2)
    return lax.all_to_all(pack, TEAM, split_axis=0, concat_axis=0, tiled=True)


def by_rank(weight):
    rows = weight.shape[0]
    return weight.reshape(rows, RANKS, -1).transpose(1, 0, 2)


def to_columns(pieces):
    return pieces.transpose(1, 0, 2).reshape(pieces.shape[1], -1)


def shuffled(rows, sh, sl, ch):
    count, width = rows.shape
    rows = rows.reshape(count, sh, sl, ch, -1).swapaxes(2, 3)
    return relative(relative(rows, "sh", 1), "ch", 2).reshape(count, width)


def unshuffled(rows, sh, sl, ch):
    count, width = rows.shape
    rows = relative(relative(rows.reshape(count, sh, ch, sl, -1), "sh", 1), "ch", 2)
    return rows.swapaxes(2, 3).reshape(count, width)


def shifted(value, steps):
    count = lax.axis_size("ch")
    if count == 1:
        return jnp.zeros_like(value)
    leading, last = max(0, -steps), min(count, count - steps)
    return lax.ppermute(value, "ch", [(at, at + steps) for at in range(leading, last)])


def entering(decay, state, reverse):
    count = lax.axis_size("ch")
    if count == 1:
        return jnp.zeros_like(state)
    if count == 2:
        return shifted(state, -1 if reverse else 1)
    place = lax.axis_index("ch")
    ahead = count - 1 - place if reverse else place
    decays = lax.all_gather(decay, "ch")
    states = lax.all_gather(state, "ch")

    def one(step, run):
        source = count - 1 - step if reverse else step
        factor = lax.dynamic_index_in_dim(decays, source, 0, False)
        return factor[:, None] * run + lax.dynamic_index_in_dim(states, source, 0, False).astype(
            F32
        )

    return lax.fori_loop(0, ahead, one, jnp.zeros(state.shape, F32)).astype(state.dtype)


def inverse_root(values):
    return lax.rsqrt(jnp.mean(values * values, axis=-1, keepdims=True) + epsilon)


def norm_back(values, scaled, upstream):
    normed = values * scaled
    return scaled * (upstream - normed * jnp.mean(upstream * normed, axis=-1, keepdims=True))


def silu_value(values):
    return values * jax.nn.sigmoid(values)


def silu_slope(values):
    sigmoid_part = jax.nn.sigmoid(values)
    return sigmoid_part * (1.0 + values * (1.0 - sigmoid_part))


def dot(operand, against, at, precision=None):
    return lax.dot_general(
        operand, against, (((at[0],), (at[1],)), ((), ())), precision=precision, preferred_element_type=F32
    )


def exact(operand, against, at):
    return dot(operand, against, at, lax.Precision.HIGHEST)


TILE = 2 * BLOCK
EDGE = 16
LANES = 512
INNER = DI // RANKS
HEADS = HM // RANKS
SIDE = 2 * NS // RANKS
CONV = INNER + SIDE


def call(kernel, grid, in_specs, out_specs, out_shape, scratch=(), scalars=0):
    return pl.pallas_call(
        kernel,
        grid_spec=pltpu.PrefetchScalarGridSpec(
            num_scalar_prefetch=scalars,
            grid=grid,
            in_specs=in_specs,
            out_specs=out_specs,
            scratch_shapes=list(scratch),
        ),
        out_shape=out_shape,
        compiler_params=pltpu.CompilerParams(vmem_limit_bytes=48 * 1024 * 1024),
        cost_estimate=pl.CostEstimate(flops=10**9, bytes_accessed=10**6, transcendentals=0),
    )


def shape(dims, dtype=F32):
    return jax.ShapeDtypeStruct(dims, dtype)


def full(array):
    return pl.BlockSpec(array.shape, lambda *at: (0,) * array.ndim)


def tiled(width, rows=TILE):
    return pl.BlockSpec((rows, width), lambda i, *at: (i, 0))


def place_rows(scalars, gathered, rows):
    left, right, left_other, right_other = gathered
    half = left.shape[2]
    own = pl.multiple_of(scalars[0] * BLOCK, BLOCK)
    other = pl.multiple_of((1 - scalars[0]) * BLOCK, BLOCK)
    rows[pl.ds(own, BLOCK), :half] = left[0]
    rows[pl.ds(own, BLOCK), half:] = right[0]
    rows[pl.ds(other, BLOCK), :half] = left_other[0]
    rows[pl.ds(other, BLOCK), half:] = right_other[0]


def gathered_specs(gathered):
    spec = pl.BlockSpec((1,) + gathered[0].shape[1:], lambda i, s: (s[1 + i], 0, 0))
    return [spec] * 4


def halves_product(rows, mine, theirs):
    half = mine.shape[0]
    return dot(rows[:, :half], mine[...], (1, 0)) + dot(rows[:, half:], theirs[...], (1, 0))


def row_root(rows):
    values = rows.astype(F32)
    return lax.rsqrt(jnp.mean(values * values, axis=-1, keepdims=True) + epsilon)


def project_inner_kernel(tiles, scalars, l, r, lo, ro, mine, theirs, halo, taps, steps, pre_ref, conv_ref, side_ref, step_ref, root_ref, edge_ref, rows, line):
    i = pl.program_id(0)
    place_rows(scalars, (l, r, lo, ro), rows)
    values = rows[...]
    root = row_root(values)
    root_ref[...] = root
    pre = halves_product(values, mine, theirs) * root
    pre_ref[...] = pre
    step_ref[...] = dot(values, steps[...], (1, 1)) * root

    @pl.when(i % tiles == 0)
    def _():
        before = halo[0]
        edge = halves_product(before, mine, theirs) * row_root(before)
        edge_ref[0] = edge
        line[:EDGE] = edge

    @pl.when(i % tiles != 0)
    def _():
        line[:EDGE] = line[TILE:]

    line[EDGE:] = pre
    conv = taps[KC : KC + 1, :]
    for k in range(KC):
        conv = conv + taps[k : k + 1, :] * line[EDGE - (KC - 1) + k : EDGE - (KC - 1) + k + TILE, :]
    conv_ref[...] = conv
    last = conv[:, INNER:]
    lane = lax.broadcasted_iota(jnp.int32, last.shape, 1)
    side_ref[...] = jnp.where(lane < SIDE, silu_value(last), last).astype(BF)


def project_inner(scalars, gathered, weight, halo, taps, steps):
    seqs = halo.shape[0]
    total = 2 * 4 * gathered[0].shape[1]
    tiles = total // TILE // seqs
    width = 2 * gathered[0].shape[2]
    return call(
        lambda *refs: project_inner_kernel(tiles, *refs),
        (total // TILE,),
        gathered_specs(gathered)
        + [full(weight[0]), full(weight[1])]
        + [pl.BlockSpec((1, EDGE, width), lambda i, s: (i // tiles, 0, 0)), full(taps), full(steps)],
        [
            tiled(LANES),
            tiled(LANES),
            tiled(2 * SIDE),
            tiled(8),
            tiled(1),
            pl.BlockSpec((1, EDGE, LANES), lambda i, s: (i // tiles, 0, 0)),
        ],
        [
            shape((total, LANES)),
            shape((total, LANES)),
            shape((total, 2 * SIDE), BF),
            shape((total, 8)),
            shape((total, 1)),
            shape((seqs, EDGE, LANES)),
        ],
        [pltpu.VMEM((TILE, width), BF), pltpu.VMEM((EDGE + TILE, LANES), F32)],
        1,
    )(scalars, *gathered, *weight, halo, taps, steps)


def project_gating_kernel(scalars, l, r, lo, ro, mine, theirs, root, gating_ref, query_ref, rows):
    place_rows(scalars, (l, r, lo, ro), rows)
    product = halves_product(rows[...], mine, theirs) * root[...]
    gating_ref[...] = product[:, :INNER]
    query_ref[...] = product[:, INNER:].astype(BF)


def project_gating(scalars, gathered, weight, root):
    total, width = root.shape[0], 2 * gathered[0].shape[2]
    return call(
        project_gating_kernel,
        (total // TILE,),
        gathered_specs(gathered) + [full(weight[0]), full(weight[1]), tiled(1)],
        [tiled(INNER), tiled(HD)],
        [shape((total, INNER)), shape((total, HD), BF)],
        [pltpu.VMEM((TILE, width), BF)],
        1,
    )(scalars, *gathered, *weight, root)


def rows_back_kernel(scalars, l, r, lo, ro, mine, theirs, ssm, gating, root, gain, mixer_ref, attn_ref, along_ref, gain_ref, rows):
    place_rows(scalars, (l, r, lo, ro), rows)
    product = halves_product(rows[...], mine, theirs)
    mixer = product[:, :INNER]
    mixer_ref[...] = mixer
    attn_ref[...] = product[:, INNER:].astype(BF)
    norm = ssm[...] * silu_value(gating[...]) * root[...]
    together = mixer * norm
    along_ref[0] = exact(jnp.ones((8, INNER), F32), together * gain[...], (1, 1))

    @pl.when(pl.program_id(0) == 0)
    def _():
        gain_ref[...] = jnp.zeros_like(gain_ref)

    gain_ref[...] += jnp.sum(together, axis=0, keepdims=True)


def rows_back(scalars, gathered, weight, ssm, gating, root, gain):
    total, width = root.shape[0], 2 * gathered[0].shape[2]
    tiles = total // TILE
    return call(
        rows_back_kernel,
        (tiles,),
        gathered_specs(gathered)
        + [full(weight[0]), full(weight[1]), tiled(INNER), tiled(INNER), tiled(1), full(gain)],
        [
            tiled(INNER),
            tiled(HD),
            pl.BlockSpec((1, 8, TILE), lambda i, s: (i, 0, 0)),
            pl.BlockSpec((1, INNER), lambda i, s: (0, 0)),
        ],
        [
            shape((total, INNER)),
            shape((total, HD), BF),
            shape((tiles, 8, TILE)),
            shape((1, INNER)),
        ],
        [pltpu.VMEM((TILE, width), BF)],
        1,
    )(scalars, *gathered, *weight, ssm, gating, root, gain)


def back_dot_kernel(terms, halves, scalars, *refs):
    ins, outs = refs[: terms * 4], refs[terms * 4 :]
    i = pl.program_id(0)
    for half in range(2):
        product = None
        for t in range(terms):
            first, second = ins[4 * t], ins[4 * t + 1]
            weight = ins[4 * t + 2 + half]
            rows = jnp.concatenate([first[...], second[...]], 0)
            at = (1, 1) if weight.shape[1] == rows.shape[1] else (1, 0)
            one = dot(rows, weight[...], at)
            product = one if product is None else product + one
        product = product.reshape(outs[half].shape)

        @pl.when(i < halves)
        def _():
            outs[2 + half][...] = product.astype(BF)

        @pl.when(i >= halves)
        def _():
            outs[half][...] = product


def back_dot(order, terms):
    total = terms[0][0].shape[0]
    half = terms[0][1][0].shape[0]
    halves = total // TILE // 2
    specs, arrays = [], []
    for rows, weights in terms:
        width = rows.shape[1]
        specs += [
            pl.BlockSpec((BLOCK, width), lambda i, s: (s[(2 * i + 4) % 8], 0)),
            pl.BlockSpec((BLOCK, width), lambda i, s: (s[(2 * i + 5) % 8], 0)),
            full(weights[0]),
            full(weights[1]),
        ]
        arrays += [rows, rows, *weights]
    kept_spec = pl.BlockSpec((2, BLOCK, half), lambda i, s: (jnp.maximum(i - halves, 0), 0, 0))
    given_spec = pl.BlockSpec((2, BLOCK, half), lambda i, s: (jnp.minimum(i, halves - 1), 0, 0))
    blocks = total // BLOCK // 2
    return call(
        lambda *refs: back_dot_kernel(len(terms), halves, *refs),
        (2 * halves,),
        specs,
        [kept_spec, kept_spec, given_spec, given_spec],
        [shape((blocks, BLOCK, half))] * 2 + [shape((blocks, BLOCK, half), BF)] * 2,
        (),
        1,
    )(order, *arrays)


def grad_dot_kernel(scalars, own, other, against, *refs):
    out, ordered = refs[-2], refs[-1]

    @pl.when(pl.program_id(0) == 0)
    def _():
        for k in range(8):
            start = pl.multiple_of(scalars[k] * BLOCK, BLOCK)
            ordered[k * BLOCK : (k + 1) * BLOCK] = against[pl.ds(start, BLOCK), :]

    tile = own.shape[2]
    rows = own.shape[0] * own.shape[1]
    product = dot(own[...].reshape(rows, tile), ordered[:rows], (0, 0))
    product = product + dot(other[...].reshape(rows, tile), ordered[rows:], (0, 0))
    out[...] = product.astype(out.dtype)


def grad_dot(order, own, other, against, dtype):
    half = own.shape[2]
    total, width = against.shape
    tile = 512
    spec = pl.BlockSpec((own.shape[0], own.shape[1], tile), lambda i, s: (0, 0, i))
    return call(
        grad_dot_kernel,
        (half // tile,),
        [spec, spec, full(against)],
        pl.BlockSpec((tile, width), lambda i, s: (i, 0)),
        shape((half, width), dtype),
        [pltpu.VMEM((total, width), BF)],
        1,
    )(order, own, other, against)


def grad_halves(order, gathered, against):
    left, right, left_other, right_other = gathered
    theirs = grad_dot(order, right, right_other, against, BF)
    return grad_dot(order, left, left_other, against, F32), theirs


def feed_kernel(parts, l, r, lo, ro, cl, cr, clo, cro, gm, gt, lm, lt, dm, dt, active_ref, gate_ref, lift_ref):
    i = pl.program_id(0)

    def run(left, right, cleft, cright):
        half = left.shape[2]

        def product(a, b, mine, theirs):
            return dot(a[...].reshape(TILE, half), mine[...], (1, 0)) + dot(
                b[...].reshape(TILE, half), theirs[...], (1, 0)
            )

        gate = product(left, right, gm, gt)
        lift = product(left, right, lm, lt)
        grad = product(cleft, cright, dm, dt)
        sigmoid_part = jax.nn.sigmoid(gate)
        swish = gate * sigmoid_part
        active_ref[...] = (swish * lift).astype(BF)
        gate_ref[...] = (
            grad * lift * sigmoid_part * (1.0 + gate * (1.0 - sigmoid_part))
        ).astype(BF)
        lift_ref[...] = (grad * swish).astype(BF)

    @pl.when(i < parts)
    def _():
        run(l, r, cl, cr)

    @pl.when(i >= parts)
    def _():
        run(lo, ro, clo, cro)


def feed_block(rows, cotangent, gate, lift, drop):
    blocks, count, half = rows[0].shape
    total = 2 * blocks * count
    parts = total // TILE // 2
    own = pl.BlockSpec((2, count, half), lambda i: (jnp.minimum(i, parts - 1), 0, 0))
    other = pl.BlockSpec((2, count, half), lambda i: (jnp.maximum(i - parts, 0), 0, 0))
    weights = [*gate, *lift, *drop]
    return call(
        lambda *refs: feed_kernel(parts, *refs),
        (2 * parts,),
        [own, own, other, other] * 2 + [full(w) for w in weights],
        [tiled(LANES)] * 3,
        [shape((total, LANES), BF)] * 3,
    )(*rows, *cotangent, *weights)


def scores_of(place, queries, keys):
    count, whole = queries.shape[0], keys.shape[0]
    scores = dot(queries, keys, (1, 1)) * HD**-0.5
    row = place + pl.program_id(1) * count + lax.broadcasted_iota(jnp.int32, (count, whole), 0)
    column = lax.broadcasted_iota(jnp.int32, (count, whole), 1)
    return scores, row >= column


def attend_kernel(place, queries, key_value, out_ref, log_ref):
    keys, values = key_value[0, :, :HD], key_value[0, :, HD:]
    scores, visible = scores_of(place[0], queries[...], keys)
    scores = jnp.where(visible, scores, negative)
    top = jnp.max(scores, axis=-1, keepdims=True)
    weights = jnp.exp(scores - top)
    total = jnp.sum(weights, axis=-1, keepdims=True)
    log_ref[...] = top + jnp.log(total)
    out_ref[...] = dot(weights.astype(BF), values, (1, 0)) / total


def attend_specs(seqs, total):
    tiles = total // TILE // seqs
    rows = lambda width: pl.BlockSpec((TILE, width), lambda n, i, s: (n * tiles + i, 0))
    return (seqs, tiles), rows


def attend(place, queries, key_value):
    seqs, whole, width = key_value.shape
    total = queries.shape[0]
    grid, rows = attend_specs(seqs, total)
    return call(
        attend_kernel,
        grid,
        [rows(HD), pl.BlockSpec((1, whole, width), lambda n, i, s: (n, 0, 0))],
        [rows(HD), rows(1)],
        [shape((total, HD)), shape((total, 1))],
        (),
        1,
    )(place, queries, key_value)


def attend_back_kernel(place, queries, grads, attended, logs, root, key_value, query_ref, sum_ref):
    keys, values = key_value[0, :, :HD], key_value[0, :, HD:]
    scores, visible = scores_of(place[0], queries[...], keys)
    probs = jnp.where(visible, jnp.exp(scores - logs[...]), 0.0)
    grad = grads[...]
    delta = jnp.sum(grad.astype(F32) * attended[...], axis=-1, keepdims=True)
    scores_grad = (probs * (dot(grad, values, (1, 1)) - delta)).astype(BF)
    query_ref[...] = (dot(scores_grad, keys, (1, 0)) * (HD**-0.5 * root[...])).astype(BF)

    @pl.when(pl.program_id(1) == 0)
    def _():
        sum_ref[...] = jnp.zeros_like(sum_ref)

    sum_ref[0, :, :HD] += dot(scores_grad, queries[...], (0, 0)) * HD**-0.5
    sum_ref[0, :, HD:] += dot(probs.astype(BF), grad, (0, 0))


def attend_back(place, queries, grads, attended, logs, root, key_value):
    seqs, whole, width = key_value.shape
    total = queries.shape[0]
    grid, rows = attend_specs(seqs, total)
    sums = pl.BlockSpec((1, whole, width), lambda n, i, s: (n, 0, 0))
    return call(
        attend_back_kernel,
        grid,
        [rows(HD), rows(HD), rows(HD), rows(1), rows(1), sums],
        [rows(HD), sums],
        [shape((total, HD), BF), shape((seqs, whole, width))],
        (),
        1,
    )(place, queries, grads, attended, logs, root, key_value)


def over_heads(values):
    rows = values.shape[0]
    return jnp.concatenate(
        [jnp.broadcast_to(values[:, h : h + 1], (rows, PM)) for h in range(HEADS)], 1
    )


def head_sums(values):
    channel = lax.broadcasted_iota(jnp.int32, (INNER, 8), 0)
    head = lax.broadcasted_iota(jnp.int32, (INNER, 8), 1)
    return exact(values, jnp.where(channel // PM == head, 1.0, 0.0), (1, 0))


def triangle():
    row = lax.broadcasted_iota(jnp.int32, (BLOCK, BLOCK), 0)
    column = lax.broadcasted_iota(jnp.int32, (BLOCK, BLOCK), 1)
    return row, column


def block_steps(step_pre, head):
    arg = step_pre[...] + head[0:1, :]
    size = jnp.maximum(arg, 0.0) + jnp.log1p(jnp.exp(-jnp.abs(arg)))
    row, column = triangle()
    cum = exact(jnp.where(row >= column, 1.0, 0.0), size * head[1:2, :], (1, 0))
    return arg, size, cum


def as_rows(values):
    row, column = triangle()
    return exact(values, jnp.where(row == column, 1.0, 0.0), (0, 0))


def as_columns(values):
    row, column = triangle()
    return exact(jnp.where(row == column, 1.0, 0.0), values, (1, 1))


def states_kernel(blocks, step_pre, head, conv, io, out_ref, decay_ref, run):
    i = pl.program_id(0)
    _, size, cum = block_steps(step_pre, head)
    last = cum[BLOCK - 1 :, :]
    feeding = jnp.exp(last - cum) * size
    inner = silu_value(conv[:, :INNER])
    fresh = dot(io[:, :NS], (over_heads(feeding) * inner).astype(BF), (0, 0))
    decay = over_heads(jnp.exp(last))

    @pl.when(i % blocks == 0)
    def _():
        run[...] = fresh
        decay_ref[0] = decay

    @pl.when(i % blocks != 0)
    def _():
        run[...] = decay * run[...] + fresh
        decay_ref[0] = decay_ref[0] * decay

    @pl.when(i % blocks == blocks - 1)
    def _():
        out_ref[0] = run[...].astype(BF)


def states(seqs, step_pre, head, conv, io):
    total = conv.shape[0]
    blocks = total // BLOCK // seqs
    return call(
        lambda *refs: states_kernel(blocks, *refs),
        (total // BLOCK,),
        [tiled(8, BLOCK), full(head), tiled(LANES, BLOCK), tiled(2 * NS, BLOCK)],
        [
            pl.BlockSpec((1, NS, INNER), lambda i: (i // blocks, 0, 0)),
            pl.BlockSpec((1, 1, INNER), lambda i: (i // blocks, 0, 0)),
        ],
        [shape((seqs, NS, INNER), BF), shape((seqs, 1, INNER))],
        [pltpu.VMEM((NS, INNER), F32)],
    )(step_pre, head, conv, io)


def fading_of(cum, cum_rows, h):
    row, column = triangle()
    span = cum[:, h : h + 1] - cum_rows[h : h + 1, :]
    return jnp.where(row >= column, jnp.exp(jnp.minimum(span, 0.0)), 0.0)


def ssm_kernel(blocks, step_pre, head, conv, io, gating, entry, ssm_ref, carried_ref, square_ref, run):
    i = pl.program_id(0)

    @pl.when(i % blocks == 0)
    def _():
        run[...] = entry[0].astype(F32)

    _, size, cum = block_steps(step_pre, head)
    size_rows, cum_rows = as_rows(size), as_rows(cum)
    last = cum[BLOCK - 1 :, :]
    inner = silu_value(conv[:, :INNER])
    inner_low = inner.astype(BF)
    in_state, out_state = io[:, :NS], io[:, NS:]
    carried = run[...].astype(BF)
    carried_ref[0] = carried
    pairing = dot(out_state, in_state, (1, 1))
    within = []
    for h in range(HEADS):
        mixing = fading_of(cum, cum_rows, h) * pairing * size_rows[h : h + 1, :]
        within.append(dot(mixing.astype(BF), inner_low[:, h * PM : (h + 1) * PM], (1, 0)))
    readout = dot(out_state, carried, (1, 0))
    ssm = (
        jnp.concatenate(within, 1)
        + over_heads(jnp.exp(cum)) * readout
        + over_heads(head[2:3, :]) * inner
    )
    ssm_ref[...] = ssm
    gated = ssm * silu_value(gating[...])
    square_ref[0] = exact(jnp.ones((8, INNER), F32), gated * gated, (1, 1))
    feeding = jnp.exp(last - cum) * size
    fresh = dot(in_state, (over_heads(feeding) * inner).astype(BF), (0, 0))
    run[...] = over_heads(jnp.exp(last)) * run[...] + fresh


def ssm_block(seqs, step_pre, head, conv, io, gating, entry):
    total = conv.shape[0]
    blocks = total // BLOCK // seqs
    return call(
        lambda *refs: ssm_kernel(blocks, *refs),
        (total // BLOCK,),
        [
            tiled(8, BLOCK),
            full(head),
            tiled(LANES, BLOCK),
            tiled(2 * NS, BLOCK),
            tiled(INNER, BLOCK),
            pl.BlockSpec((1, NS, INNER), lambda i: (i // blocks, 0, 0)),
        ],
        [
            tiled(INNER, BLOCK),
            pl.BlockSpec((1, NS, INNER), lambda i: (i, 0, 0)),
            pl.BlockSpec((1, 8, BLOCK), lambda i: (i, 0, 0)),
        ],
        [
            shape((total, INNER)),
            shape((total // BLOCK, NS, INNER), BF),
            shape((total // BLOCK, 8, BLOCK)),
        ],
        [pltpu.VMEM((NS, INNER), F32)],
    )(step_pre, head, conv, io, gating, entry)


def states_back_kernel(blocks, step_pre, head, io, mixer, ssm, gating, mixer_root, along, gain, root, grad_ref, gating_ref, out_ref, run):
    i = pl.program_id(0)
    _, _, cum = block_steps(step_pre, head)
    gate = gating[...]
    sigmoid_part = jax.nn.sigmoid(gate)
    act = gate * sigmoid_part
    values = ssm[...]
    norm = values * act * mixer_root[...]
    gated_grad = mixer_root[...] * (mixer[...] * gain[...] - norm * along[...])
    grad = gated_grad * act
    grad_ref[...] = grad
    slope = sigmoid_part * (1.0 + gate * (1.0 - sigmoid_part))
    gating_ref[...] = (gated_grad * values * slope * root[...]).astype(BF)
    grown = (over_heads(jnp.exp(cum)) * grad).astype(BF)
    fresh = dot(io[:, NS:], grown, (0, 0))
    decay = over_heads(jnp.exp(cum[BLOCK - 1 :, :]))

    @pl.when(i % blocks == 0)
    def _():
        run[...] = fresh

    @pl.when(i % blocks != 0)
    def _():
        run[...] = decay * run[...] + fresh

    @pl.when(i % blocks == blocks - 1)
    def _():
        out_ref[0] = run[...].astype(BF)


def states_back(seqs, step_pre, head, io, mixer, ssm, gating, mixer_root, along, gain, root):
    total = ssm.shape[0]
    many = total // BLOCK
    blocks = many // seqs
    back = lambda width: pl.BlockSpec((BLOCK, width), lambda i: (many - 1 - i, 0))
    return call(
        lambda *refs: states_back_kernel(blocks, *refs),
        (many,),
        [back(8), full(head), back(2 * NS), back(INNER), back(INNER), back(INNER)]
        + [back(1), back(1), full(gain), back(1)],
        [
            back(INNER),
            back(INNER),
            pl.BlockSpec((1, NS, INNER), lambda i: (seqs - 1 - i // blocks, 0, 0)),
        ],
        [shape((total, INNER)), shape((total, INNER), BF), shape((seqs, NS, INNER), BF)],
        [pltpu.VMEM((NS, INNER), F32)],
    )(step_pre, head, io, mixer, ssm, gating, mixer_root, along, gain, root)


def ssm_back_kernel(blocks, side, step_pre, head, conv, io, grads, carried_ref, entry, key_value, root, conv_ref, parts_ref, step_ref, sums_ref, later):
    i = pl.program_id(0)

    @pl.when(i % blocks == 0)
    def _():
        later[...] = entry[0].astype(F32)

    @pl.when(i == 0)
    def _():
        sums_ref[...] = jnp.zeros_like(sums_ref)

    arg, size, cum = block_steps(step_pre, head)
    size_rows, cum_rows = as_rows(size), as_rows(cum)
    last = cum[BLOCK - 1 :, :]
    growth, to_end, decay = jnp.exp(cum), jnp.exp(last - cum), jnp.exp(last)
    feeding = to_end * size
    conv_sum = conv[:, :INNER]
    inner = silu_value(conv_sum)
    inner_low = inner.astype(BF)
    in_state, out_state = io[:, :NS], io[:, NS:]
    carried = carried_ref[0]
    after = later[...]
    after_low = after.astype(BF)
    grad = grads[...]
    grad_low = grad.astype(BF)
    pairing = dot(out_state, in_state, (1, 1))
    readout = dot(out_state, carried, (1, 0))
    spread = dot(in_state, after_low, (1, 0))
    grown = (over_heads(growth) * grad).astype(BF)
    feeding_wide = over_heads(feeding)
    fed_inner = (feeding_wide * inner).astype(BF)
    pairing_grad = jnp.zeros((BLOCK, BLOCK), F32)
    inner_parts, flows, step_rows = [], [], []
    for h in range(HEADS):
        at = slice(h * PM, (h + 1) * PM)
        fading = fading_of(cum, cum_rows, h)
        sized = size_rows[h : h + 1, :]
        mixing = (fading * pairing * sized).astype(BF)
        faded = dot(grad_low[:, at], inner_low[:, at], (1, 1)) * fading
        pairing_grad = pairing_grad + faded * sized
        stepwise = faded * pairing
        step_rows.append(jnp.sum(stepwise, axis=0, keepdims=True))
        flows.append(jnp.sum(stepwise * sized, axis=1, keepdims=True))
        inner_parts.append(dot(mixing, grad_low[:, at], (0, 0)))
    empty_row, empty_column = jnp.zeros((2, BLOCK), F32), jnp.zeros((BLOCK, 2), F32)
    step_rows = jnp.concatenate(step_rows + [empty_row], 0)
    flow = jnp.concatenate(flows + [empty_column], 1)
    pairing_low = pairing_grad.astype(BF)
    out_grad = dot(pairing_low, in_state, (1, 0)) + dot(grown, carried, (1, 1))
    in_grad = dot(pairing_low, out_state, (0, 0)) + dot(fed_inner, after_low, (1, 1))
    inner_grad = (
        jnp.concatenate(inner_parts, 1) + over_heads(head[2:3, :]) * grad + feeding_wide * spread
    )
    conv_ref[...] = inner_grad * silu_slope(conv_sum)
    for rank in range(RANKS):
        source = in_grad if rank < RANKS // 2 else out_grad
        at = (rank % 4) * SIDE
        own = jnp.where(side[0] == rank // 4, 1.0, 0.0)
        parts_ref[rank] = jnp.concatenate(
            [source[:, at : at + SIDE], key_value[:, at : at + SIDE] * own], 1
        ).astype(BF)
    feeding_grad = head_sums(spread * inner)
    fed = feeding_grad * feeding
    through = jnp.sum(after * carried.astype(F32), axis=0, keepdims=True)
    through = head_sums(jnp.broadcast_to(through, (8, INNER)))[:1]
    last_grad = jnp.sum(fed, axis=0, keepdims=True) + through * decay
    cum_grad = flow - as_columns(step_rows * size_rows) + head_sums(grad * readout) * growth - fed
    row, column = triangle()
    increment = exact(jnp.where(column >= row, 1.0, 0.0), cum_grad, (1, 0)) + last_grad
    rates = head[1:2, :]
    step_grad = as_columns(step_rows) + feeding_grad * to_end + increment * rates
    arg_grad = step_grad * jax.nn.sigmoid(arg)
    step_ref[...] = (arg_grad * root[...]).astype(BF)
    skip = jnp.broadcast_to(jnp.sum(grad * inner, axis=0, keepdims=True), (8, INNER))
    sums_ref[0:1, :] += jnp.sum(arg_grad, axis=0, keepdims=True)
    sums_ref[1:2, :] += jnp.sum(increment * size, axis=0, keepdims=True) * rates
    sums_ref[2:3, :] += head_sums(skip)[:1]
    later[...] = over_heads(decay) * after + dot(out_state, grown, (0, 0))


def ssm_back(side, seqs, step_pre, head, conv, io, grads, carried, entry, key_value, root):
    total = conv.shape[0]
    many = total // BLOCK
    blocks = many // seqs
    back = lambda width: pl.BlockSpec((BLOCK, width), lambda i, s: (many - 1 - i, 0))
    return call(
        lambda *refs: ssm_back_kernel(blocks, *refs),
        (many,),
        [back(8), full(head), back(LANES), back(2 * NS), back(INNER)]
        + [
            pl.BlockSpec((1, NS, INNER), lambda i, s: (many - 1 - i, 0, 0)),
            pl.BlockSpec((1, NS, INNER), lambda i, s: (seqs - 1 - i // blocks, 0, 0)),
            back(2 * HD),
            back(1),
        ],
        [
            back(INNER),
            pl.BlockSpec((RANKS, BLOCK, 2 * SIDE), lambda i, s: (0, many - 1 - i, 0)),
            back(8),
            pl.BlockSpec((8, 8), lambda i, s: (0, 0)),
        ],
        [
            shape((total, INNER)),
            shape((RANKS, total, 2 * SIDE), BF),
            shape((total, 8), BF),
            shape((8, 8)),
        ],
        [pltpu.VMEM((NS, INNER), F32)],
        1,
    )(side, step_pre, head, conv, io, grads, carried, entry, key_value, root)


def conv_back_kernel(tiles, inner, parts, conv, pre, edge, grad_ref, sums_ref, line):
    i = pl.program_id(0)
    got = jnp.sum(parts[...].astype(F32), axis=0)
    lane = lax.broadcasted_iota(jnp.int32, got.shape, 1)
    got = jnp.where(lane < SIDE, got * silu_slope(conv[:, INNER:]), got)
    grad = jnp.concatenate([inner[...], got], 1)
    grad_ref[...] = grad

    @pl.when(i % tiles == 0)
    def _():
        line[:EDGE] = edge[0]

    @pl.when(i % tiles != 0)
    def _():
        line[:EDGE] = line[TILE:]

    @pl.when(i == 0)
    def _():
        sums_ref[...] = jnp.zeros_like(sums_ref)

    line[EDGE:] = pre[...]
    for k in range(KC):
        before = line[EDGE - (KC - 1) + k : EDGE - (KC - 1) + k + TILE, :]
        sums_ref[k : k + 1, :] += jnp.sum(grad * before, axis=0, keepdims=True)
    sums_ref[KC : KC + 1, :] += jnp.sum(grad, axis=0, keepdims=True)


def conv_back(inner, parts, conv, pre, edge):
    total = conv.shape[0]
    tiles = total // TILE // edge.shape[0]
    return call(
        lambda *refs: conv_back_kernel(tiles, *refs),
        (total // TILE,),
        [
            tiled(INNER),
            pl.BlockSpec((RANKS, TILE, 2 * SIDE), lambda i: (0, i, 0)),
            tiled(LANES),
            tiled(LANES),
            pl.BlockSpec((1, EDGE, LANES), lambda i: (i // tiles, 0, 0)),
        ],
        [tiled(LANES), pl.BlockSpec((8, LANES), lambda i: (0, 0))],
        [shape((total, LANES)), shape((8, LANES))],
        [pltpu.VMEM((EDGE + TILE, LANES), F32)],
    )(inner, parts, conv, pre, edge)


def pre_back_kernel(tiles, grad, after, follow, taps, root, out_ref, line):
    i = pl.program_id(0)
    line[:TILE] = grad[...]

    @pl.when(i % tiles == tiles - 1)
    def _():
        line[TILE:] = follow[0]

    @pl.when(i % tiles != tiles - 1)
    def _():
        line[TILE:] = after[...]

    total = taps[KC - 1 : KC, :] * line[:TILE, :]
    for k in range(KC - 1):
        total = total + taps[k : k + 1, :] * line[KC - 1 - k : KC - 1 - k + TILE, :]
    out_ref[...] = (total * root[...]).astype(BF)


def pre_back(grad, follow, taps, root):
    total = grad.shape[0]
    tiles = total // TILE // follow.shape[0]
    last = total // EDGE - 1
    return call(
        lambda *refs: pre_back_kernel(tiles, *refs),
        (total // TILE,),
        [
            tiled(LANES),
            pl.BlockSpec((EDGE, LANES), lambda i: (jnp.minimum((i + 1) * (TILE // EDGE), last), 0)),
            pl.BlockSpec((1, EDGE, LANES), lambda i: (i // tiles, 0, 0)),
            full(taps),
            tiled(1),
        ],
        tiled(LANES),
        shape((total, LANES), BF),
        [pltpu.VMEM((TILE + EDGE, LANES), F32)],
    )(grad, grad, follow, taps, root)


def local(
    tokens,
    cotangent,
    norm_gain,
    gating_weight,
    inner_weight,
    state_weight,
    step_weight,
    conv_weight,
    conv_bias,
    mixer_gain,
    mixer_out,
    query_weight,
    key_weight,
    value_weight,
    output_weight,
    feed_gain,
    gate_matrix,
    lift_matrix,
    drop_matrix,
    step_bias,
    decay_log,
    skip_scale,
):
    sh, sl, ch = lax.axis_size("sh"), lax.axis_size("sl"), lax.axis_size("ch")
    world = sh * sl * ch * 4
    rows, width = tokens.shape
    drows = norm_gain.shape[0]
    my_sl, my_zl, my_core = (lax.axis_index(axis) for axis in TEAM)
    rank = (my_sl * 2 + my_zl) * 2 + my_core
    total = RANKS * rows
    count = 4 * rows
    whole = ch * count

    order = team_order()
    straight = jnp.arange(8, dtype=jnp.int32)
    tiles = [((z ^ my_zl) * 2 + (s ^ my_sl)) for s in (0, 1) for z in (0, 1)]
    scalars = jnp.stack([my_core, *tiles]).astype(jnp.int32)
    place = (lax.axis_index("ch") * count).astype(jnp.int32).reshape(1)
    side_index = my_sl.astype(jnp.int32).reshape(1)

    def scaled(weight, gain):
        return (weight.astype(F32) * gain.astype(F32)[:, None]).astype(BF)

    key_value = jnp.stack(
        [key_weight.reshape(drows, HK, 2, SIDE), value_weight.reshape(drows, HK, 2, SIDE)], 2
    ).reshape(drows, RANKS * SIDE)
    pack_in = jnp.concatenate(
        [
            by_rank(scaled(w, norm_gain))
            for w in (inner_weight, state_weight, key_value, gating_weight, query_weight)
        ],
        2,
    )
    own_tokens = shuffled(tokens, sh, sl, ch)
    own_cotangent = shuffled(cotangent, sh, sl, ch)
    mixed_in = ranks_exchange(pack_in)
    team_tokens = team_gather(own_tokens)
    pack_rest = jnp.concatenate(
        [by_rank(mixer_out.T), by_rank(output_weight.T)]
        + [by_rank(scaled(w, feed_gain)) for w in (gate_matrix, lift_matrix)]
        + [by_rank(drop_matrix.T)],
        2,
    )

    conv_own, gain_own = conv_weight.shape[1], mixer_gain.shape[0]
    step_sent = jnp.broadcast_to(
        scaled(step_weight, norm_gain).T.reshape(1, sl, 1, 4, HEADS * drows),
        (sh, sl, ch, 4, HEADS * drows),
    ).reshape(world, HEADS * drows)
    shared = jnp.concatenate([conv_weight.reshape(-1), conv_bias, mixer_gain])
    small = jnp.concatenate(
        [jnp.broadcast_to(shared[None], (world, shared.shape[0])), step_sent], 1
    )
    small, mixed_in = together(small, mixed_in)
    small = lax.all_to_all(small, WORLD, split_axis=0, concat_axis=0, tiled=True)
    pack_rest, small, team_tokens = together(pack_rest, small, team_tokens)
    mixed_rest = ranks_exchange(pack_rest)
    w_inner, w_gating, w_out, w_gate, w_lift, w_drop = peers_gather(
        [
            mixed_in[:, :LANES],
            mixed_in[:, LANES:],
            *(mixed_rest[:, at * LANES : (at + 1) * LANES] for at in range(4)),
        ]
    )
    at = (KC + 1) * conv_own
    wide_conv = small[:, :at].reshape(world, KC + 1, conv_own)
    wide_conv = wide_conv.transpose(1, 0, 2).reshape(KC + 1, -1).astype(F32)
    wide_gain = small[:, at : at + gain_own].reshape(1, -1).astype(F32)
    own_step = small[:, at + gain_own :].reshape(sh, sl, ch, 4, HEADS, drows).swapaxes(1, 2)
    own_step = relative(relative(own_step, "sh", 0), "ch", 1)
    own_step = own_step.reshape(-1, HEADS, drows).swapaxes(0, 1).reshape(HEADS, width)
    own_step = jnp.pad(own_step, ((0, 8 - HEADS), (0, 0)))
    taps = jnp.concatenate(
        [
            lax.dynamic_slice_in_dim(wide_conv, rank * INNER, INNER, 1),
            lax.dynamic_slice_in_dim(wide_conv, DI + rank * SIDE, SIDE, 1),
            jnp.zeros((KC + 1, LANES - CONV), F32).at[KC - 1].set(1.0),
        ],
        1,
    )
    taps = jnp.pad(taps, ((0, 8 - KC - 1), (0, 0)))
    own_gain = lax.dynamic_slice_in_dim(wide_gain, rank * INNER, INNER, 1)
    head = jnp.stack([step_bias, -jnp.exp(decay_log), skip_scale])
    head = lax.dynamic_slice_in_dim(head, rank * HEADS, HEADS, 1)
    head = jnp.pad(head, ((0, 5), (0, 8 - HEADS)))

    ends = []
    for seq in range(sl):
        at_block = 2 * (1 - my_zl) + (seq ^ my_sl)
        halves = []
        for own, other in ((team_tokens[0], team_tokens[2]), (team_tokens[1], team_tokens[3])):
            own = lax.dynamic_index_in_dim(own[:, rows - EDGE :], at_block, 0, False)
            other = lax.dynamic_index_in_dim(other[:, rows - EDGE :], at_block, 0, False)
            halves.append(jnp.where(my_core == 1, own, other))
        ends.append(jnp.concatenate(halves, 1))
    halo = shifted(jnp.stack(ends), 1)
    if ch == 2:
        halo = jnp.flip(halo.reshape(sl, EDGE, sh, ch, -1), 3).reshape(sl, EDGE, width)

    pre, conv, side, step_pre, root, edge = project_inner(
        scalars, team_tokens, w_inner, halo, taps, own_step
    )
    sides = lax.all_gather(side, TEAM)
    gating, queries = project_gating(scalars, team_tokens, w_gating, root)
    io = sides[:, :, :SIDE].transpose(1, 0, 2).reshape(total, 2 * NS)
    key_value_rows = lax.dynamic_slice_in_dim(sides[:, :, SIDE:], my_sl * 4, 4, 0)
    key_value_rows = key_value_rows.transpose(1, 0, 2).reshape(sl, count, 2 * HD)
    if ch == 2:
        key_value_rows = paired(key_value_rows, swap(key_value_rows, "ch"), "ch", 1)
        key_value_rows = key_value_rows.reshape(sl, whole, 2 * HD)
    elif ch > 2:
        key_value_rows = lax.all_gather(key_value_rows, "ch", axis=1, tiled=True)
    leaving, piece_decay = states(sl, step_pre, head, conv, io)
    entry = entering(piece_decay[:, 0], leaving, False)
    attended, logs = attend(place, queries, key_value_rows)
    team_cotangent = team_gather(own_cotangent)
    entry, *team_cotangent = together(entry, *team_cotangent)
    ssm, carried, square = ssm_block(sl, step_pre, head, conv, io, gating, entry)
    mixer_root = lax.rsqrt(team_sum(square[:, 0]) / DI + epsilon).reshape(total, 1)
    branch_rows = jnp.concatenate(
        [(ssm * silu_value(gating) * mixer_root * own_gain).astype(BF), attended.astype(BF)], 1
    )

    branch = team_scatter(back_dot(order, [(branch_rows, w_out)]))

    residual = own_tokens.astype(F32) + branch
    feed_root = inverse_root(residual)
    feed_rows = team_gather((residual * feed_root).astype(BF))
    active, gate_rows_grad, lift_rows_grad = feed_block(
        feed_rows, team_cotangent, w_gate, w_lift, w_drop
    )
    feed_grad = team_scatter(
        back_dot(straight, [(gate_rows_grad, w_gate), (lift_rows_grad, w_lift)])
    )
    residual_grad = own_cotangent.astype(F32) + norm_back(residual, feed_root, feed_grad)
    branch_grad = team_gather(residual_grad.astype(BF))
    drop_mine, drop_theirs = grad_halves(straight, team_cotangent, active)
    gate_mine, gate_theirs = grad_halves(straight, feed_rows, gate_rows_grad)
    lift_mine, lift_theirs = grad_halves(straight, feed_rows, lift_rows_grad)
    layer_parts = back_dot(straight, [(active, w_drop)])
    drop_theirs = swap(drop_theirs, "sh")
    branch_grad, layer_parts, drop_theirs, gate_theirs, lift_theirs = together(
        branch_grad, layer_parts, drop_theirs, gate_theirs, lift_theirs
    )
    gate_theirs, drop_part = together(
        swap(gate_theirs, "sh"), ch_part(added(drop_mine, drop_theirs))
    )
    layer_output = (residual + team_scatter(layer_parts)).astype(BF)

    mixer_rows_grad, attn_grad, along, gain_part = rows_back(
        scalars, branch_grad, w_out, ssm, gating, mixer_root, own_gain
    )
    along = team_sum(along[:, 0]).reshape(total, 1) / DI
    query_grad, key_value_part = attend_back(
        place, queries, attn_grad, attended, logs, root, key_value_rows
    )
    if ch == 1:
        key_value_grad = key_value_part
    elif ch == 2:
        halves = key_value_part.reshape(sl, ch, count, 2 * HD)
        key_value_grad = added(
            kept(halves, "ch", 1), swap(given(halves, "ch", 1).astype(BF), "ch")
        )
    else:
        key_value_grad = lax.psum_scatter(
            key_value_part.astype(BF), "ch", scatter_dimension=1, tiled=True
        ).astype(F32)
    out_mine, out_theirs = grad_halves(order, branch_grad, branch_rows)
    along, gate_theirs, drop_part, out_theirs = together(
        along, gate_theirs, drop_part, out_theirs
    )
    lift_theirs, gate_part = together(
        swap(lift_theirs, "sh"), ch_part(added(gate_mine, gate_theirs))
    )
    ssm_grad, gating_grad, leaving_back = states_back(
        sl, step_pre, head, io, mixer_rows_grad, ssm, gating, mixer_root, along, own_gain, root
    )
    entry_back = entering(piece_decay[:, 0], leaving_back, True)
    gating_rows_grad = jnp.concatenate([gating_grad, query_grad], 1)
    gating_mine, gating_theirs = grad_halves(order, team_tokens, gating_rows_grad)
    ssm_grad, layer_output, lift_theirs, gate_part, gating_theirs = together(
        ssm_grad, layer_output, lift_theirs, gate_part, gating_theirs
    )
    out_theirs, lift_part = together(
        swap(out_theirs, "sh"), ch_part(added(lift_mine, lift_theirs))
    )
    inner_conv_grad, parts, step_rows_grad, sums = ssm_back(
        side_index,
        sl,
        step_pre,
        head,
        conv,
        io,
        ssm_grad,
        carried,
        entry_back,
        key_value_grad.reshape(total, 2 * HD),
        root,
    )
    parts = lax.all_to_all(parts, TEAM, split_axis=0, concat_axis=0, tiled=True)
    parts, out_theirs, lift_part = together(parts, out_theirs, lift_part)
    gating_theirs, out_part = together(
        swap(gating_theirs, "sh"), ch_part(added(out_mine, out_theirs))
    )
    feed_back = ranks_return([drop_part, gate_part, lift_part], drows).astype(F32)
    drop_back = feed_back[:, :, :LANES]
    gate_back = feed_back[:, :, LANES : 2 * LANES]
    lift_back = feed_back[:, :, 2 * LANES :]
    conv_grad, conv_sums = conv_back(inner_conv_grad, parts, conv, pre, edge)
    follow = shifted(conv_grad.reshape(sl, count, LANES)[:, :EDGE], -1)
    inner_rows_grad = pre_back(conv_grad, follow, taps, root)
    step_halves = (own_step[:, : width // 2], own_step[:, width // 2 :])
    hidden_grad = team_scatter(
        back_dot(
            order,
            [
                (inner_rows_grad, w_inner),
                (gating_rows_grad, w_gating),
                (step_rows_grad, step_halves),
            ],
        )
    )
    inner_mine, inner_theirs = grad_halves(order, team_tokens, inner_rows_grad)
    inner_theirs, gating_part = together(
        swap(inner_theirs, "sh"), ch_part(added(gating_mine, gating_theirs))
    )
    inner_part = ch_part(added(inner_mine, inner_theirs))
    mixer_back = ranks_return([out_part, gating_part, inner_part], drows).astype(F32)
    out_back = mixer_back[:, :, :LANES]
    gating_back = mixer_back[:, :, LANES : 2 * LANES]
    inner_back = mixer_back[:, :, 2 * LANES :]
    token_values = own_tokens.astype(F32)
    token_root = inverse_root(token_values)
    tokens_grad = residual_grad + norm_back(token_values, token_root, hidden_grad / token_root)
    left, right, left_other, right_other = team_tokens
    step_back = jnp.concatenate(
        [
            grad_dot(order, left, left_other, step_rows_grad, F32),
            grad_dot(order, right, right_other, step_rows_grad, F32),
        ],
        0,
    )[:, :HEADS].T

    def placed(part, extent, at):
        base = jnp.zeros(part.shape[:-1] + (extent,), F32)
        return lax.dynamic_update_slice_in_dim(base, part, at, part.ndim - 1)

    conv_all = jnp.concatenate(
        [
            placed(conv_sums[: KC + 1, :INNER], DI, rank * INNER),
            placed(conv_sums[: KC + 1, INNER:CONV], 2 * NS, rank * SIDE),
        ],
        1,
    )
    gain_all = placed(gain_part[0], DI, rank * INNER)
    step_all = step_back.reshape(HEADS, -1, drows).swapaxes(0, 1)
    step_all = step_all.reshape(sh, ch, sl, 4, HEADS * drows)
    step_all = relative(relative(step_all, "sh", 0), "ch", 1).swapaxes(1, 2)
    per_head = jnp.concatenate(
        [placed(sums[at, :HEADS], HM, rank * HEADS) for at in range(3)]
    )
    sent = jnp.concatenate(
        [
            conv_all.reshape(KC + 1, world, conv_own).swapaxes(0, 1).reshape(world, -1),
            gain_all.reshape(world, -1),
            step_all.reshape(world, -1),
            jnp.broadcast_to(per_head[None], (world, 3 * HM)),
        ],
        1,
    )
    got_all = lax.all_to_all(sent, WORLD, split_axis=0, concat_axis=0, tiled=True)
    at = KC * conv_own + conv_own + gain_own
    step_core = got_all[:, at : at + HEADS * drows].reshape(sh, sl, ch, 4, HEADS, drows)
    step_core = jnp.sum(step_core, axis=(0, 2)).reshape(HM, drows).T
    got = jnp.sum(got_all, axis=0)
    at = 0
    conv_out = got[at : at + KC * conv_own].reshape(KC, conv_own)
    at += KC * conv_own
    conv_bias_out = got[at : at + conv_own]
    at += conv_own
    gain_out = got[at : at + gain_own]
    at += gain_own + HEADS * drows
    bias_out, decay_out, skip_out = (got[at + i * HM : at + (i + 1) * HM] for i in range(3))

    def against(weight, grad):
        return jnp.sum(weight.astype(F32) * grad, axis=1)

    inner_core = to_columns(inner_back[:, :, :INNER])
    state_core = to_columns(inner_back[:, :, INNER:CONV])
    key_value_core = to_columns(inner_back[:, :, CONV:]).reshape(drows, HK, 2, 2 * SIDE)
    key_core = key_value_core[:, :, 0].reshape(drows, HK * HD)
    value_core = key_value_core[:, :, 1].reshape(drows, HK * HD)
    gating_core = to_columns(gating_back[:, :, :INNER])
    query_core = to_columns(gating_back[:, :, INNER:])
    gate_core, lift_core = to_columns(gate_back), to_columns(lift_back)
    norm_out = (
        against(gating_weight, gating_core)
        + against(inner_weight, inner_core)
        + against(state_weight, state_core)
        + against(step_weight, step_core)
        + against(query_weight, query_core)
        + against(key_weight, key_core)
        + against(value_weight, value_core)
    )
    feed_out = against(gate_matrix, gate_core) + against(lift_matrix, lift_core)
    norm_scale = norm_gain.astype(F32)[:, None]
    feed_scale = feed_gain.astype(F32)[:, None]
    mixer_out_out = out_back[:, :, :INNER].transpose(0, 2, 1).reshape(DI, drows)
    output_out = out_back[:, :, INNER:].transpose(0, 2, 1).reshape(HA * HD, drows)
    drop_out = drop_back.transpose(0, 2, 1).reshape(-1, drows)
    return (
        unshuffled(layer_output, sh, sl, ch),
        unshuffled(tokens_grad, sh, sl, ch),
        norm_out,
        gating_core * norm_scale,
        inner_core * norm_scale,
        state_core * norm_scale,
        step_core * norm_scale,
        conv_out,
        conv_bias_out,
        gain_out,
        mixer_out_out,
        query_core * norm_scale,
        key_core * norm_scale,
        value_core * norm_scale,
        output_out,
        feed_out,
        gate_core * feed_scale,
        lift_core * feed_scale,
        drop_out,
        bias_out,
        decay_out,
        skip_out,
    )


def solution(mesh):
    seq, ctx = mesh.shape["seq"], mesh.shape["ctx"]
    fine = Mesh(mesh.devices.reshape(seq // 2, 2, ctx // 4, 2, 2), WORLD)
    lead, vector, tail = P(WORLD, None), P(WORLD), P(None, WORLD)
    in_specs = (
        lead,
        lead,
        vector,
        lead,
        lead,
        lead,
        lead,
        tail,
        vector,
        vector,
        tail,
        lead,
        lead,
        lead,
        tail,
        vector,
        lead,
        lead,
        tail,
        P(),
        P(),
        P(),
    )
    out_specs = (
        lead,
        lead,
        vector,
        lead,
        lead,
        lead,
        lead,
        tail,
        vector,
        vector,
        tail,
        lead,
        lead,
        lead,
        tail,
        vector,
        lead,
        lead,
        tail,
        P(),
        P(),
        P(),
    )
    return jax.shard_map(local, mesh=fine, in_specs=in_specs, out_specs=out_specs, check_vma=False)
```

```python
import jax
import jax.numpy as jnp
from jax import lax
from jax.experimental import pallas as pl
from jax.experimental.pallas import tpu as pltpu
from jax.sharding import Mesh
from jax.sharding import PartitionSpec as P

DI = 3072
HM = 48
PM = 64
NS = 256
KC = 4
HA = 8
HK = 2
HD = 128
FF = 4096
BLOCK = 128

epsilon = 1e-06
negative = -1e30
BF = jnp.bfloat16
F32 = jnp.float32

TEAM = ("sl", "zl", "core")
PEERS = ("sh", "ch")
WORLD = ("sh", "sl", "ch", "zl", "core")
RANKS = 8


def swap(value, axis):
    return lax.ppermute(value, axis, [(0, 1), (1, 0)])


def paired(mine, theirs, axis_name, dim):
    bit = lax.axis_index(axis_name)
    return jnp.where(bit == 0, jnp.stack([mine, theirs], dim), jnp.stack([theirs, mine], dim))


def kept(value, axis_name, dim):
    return lax.dynamic_index_in_dim(value, lax.axis_index(axis_name), dim, False)


def given(value, axis_name, dim):
    return lax.dynamic_index_in_dim(value, 1 - lax.axis_index(axis_name), dim, False)


def added(mine, theirs):
    return mine.astype(F32) + theirs.astype(F32)


def team_order():
    s, z, c = (lax.axis_index(axis) for axis in TEAM)
    blocks = [
        ((s ^ sl) * 2 + (z ^ zl)) * 2 + (c ^ core)
        for core in (0, 1)
        for zl in (0, 1)
        for sl in (0, 1)
    ]
    return jnp.stack(blocks).astype(jnp.int32)


def team_gather(left, right):
    left = jnp.stack([left, swap(left, "sl")])
    right = jnp.stack([right, swap(right, "zl")])
    left_z = swap(left, "zl")
    right_x = swap(right, "sl")
    left = jnp.concatenate([left, left_z], 0)
    right = jnp.stack([right[0], right_x[0], right[1], right_x[1]])
    return left, right, swap(left, "core"), swap(right, "core")


def scatter_core(parts):
    left, right, left_given, right_given = parts
    left_got, right_got = swap(left_given, "core"), swap(right_given, "core")
    return (
        added(left[:2], left_got[:2]),
        added(left[2:], left_got[2:]).astype(BF),
        added(right[0::2], right_got[0::2]),
        added(right[1::2], right_got[1::2]).astype(BF),
    )


def scatter_near(parts):
    left, left_given, right, right_given = parts
    left = left + swap(left_given, "zl").astype(F32)
    right = right + swap(right_given, "sl").astype(F32)
    return left[0], left[1].astype(BF), right[0], right[1].astype(BF)


def scatter_last(parts):
    left, left_given, right, right_given = parts
    return left, swap(left_given, "sl"), right, swap(right_given, "zl")


def team_scatter(parts):
    return scatter_last(scatter_near(scatter_core(parts)))


def team_sum(value):
    for axis in TEAM[::-1]:
        value = value + swap(value, axis)
    return value


def relative(value, axis_name, dim):
    if lax.axis_size(axis_name) != 2:
        return value
    return jnp.where(lax.axis_index(axis_name) == 0, value, jnp.flip(value, dim))


def together(*values):
    return lax.optimization_barrier(values)


def along_ch(part):
    size = lax.axis_size("ch")
    if size == 2:
        return jnp.concatenate([part, swap(part, "ch")], 0)
    return lax.all_gather(part, "ch", axis=0, tiled=True)


def peers_gather(parts):
    out = []
    ready = along_ch(parts[0])
    for part in parts[1:]:
        mine = ready
        theirs, ready = together(swap(mine, "sh"), along_ch(part))
        out.append((mine, theirs))
    return out + [(ready, swap(ready, "sh"))]


def ranks_exchange(pack):
    mixed = lax.all_to_all(pack, TEAM, split_axis=0, concat_axis=0, tiled=True)
    return mixed.reshape(-1, pack.shape[2])


def ch_part(part):
    size = lax.axis_size("ch")
    if size == 2:
        half = part.shape[0] // 2
        part = added(part[:half], swap(part[half:].astype(BF), "ch"))
    elif size > 2:
        part = lax.psum_scatter(part.astype(BF), "ch", scatter_dimension=0, tiled=True)
    return part.astype(BF)


def ranks_return(parts, rows):
    pack = jnp.concatenate([p.reshape(RANKS, rows, -1) for p in parts], 2)
    return lax.all_to_all(pack, TEAM, split_axis=0, concat_axis=0, tiled=True)


def by_rank(weight):
    rows = weight.shape[0]
    return weight.reshape(rows, RANKS, -1).transpose(1, 0, 2)


def to_columns(pieces):
    return pieces.transpose(1, 0, 2).reshape(pieces.shape[1], -1)


def column_blocks(sh, sl, ch):
    place = lax.axis_index("sh")
    if ch == 2:
        place = place * 2 + lax.axis_index("ch")
    return place.astype(jnp.int32).reshape(1)


def shifted(value, steps):
    count = lax.axis_size("ch")
    if count == 1:
        return jnp.zeros_like(value)
    leading, last = max(0, -steps), min(count, count - steps)
    return lax.ppermute(value, "ch", [(at, at + steps) for at in range(leading, last)])


def entering(decay, state, reverse):
    count = lax.axis_size("ch")
    if count == 1:
        return jnp.zeros_like(state)
    if count == 2:
        return shifted(state, -1 if reverse else 1)
    place = lax.axis_index("ch")
    ahead = count - 1 - place if reverse else place
    decays = lax.all_gather(decay, "ch")
    states = lax.all_gather(state, "ch")

    def one(step, run):
        source = count - 1 - step if reverse else step
        factor = lax.dynamic_index_in_dim(decays, source, 0, False)
        return factor[:, None] * run + lax.dynamic_index_in_dim(states, source, 0, False).astype(
            F32
        )

    return lax.fori_loop(0, ahead, one, jnp.zeros(state.shape, F32)).astype(state.dtype)


def inverse_root(values):
    return lax.rsqrt(jnp.mean(values * values, axis=-1, keepdims=True) + epsilon)


def norm_back(values, scaled, upstream):
    normed = values * scaled
    return scaled * (upstream - normed * jnp.mean(upstream * normed, axis=-1, keepdims=True))


def silu_value(values):
    return values * jax.nn.sigmoid(values)


def silu_slope(values):
    sigmoid_part = jax.nn.sigmoid(values)
    return sigmoid_part * (1.0 + values * (1.0 - sigmoid_part))


def dot(operand, against, at, precision=None):
    return lax.dot_general(
        operand, against, (((at[0],), (at[1],)), ((), ())), precision=precision, preferred_element_type=F32
    )


def exact(operand, against, at):
    return dot(operand, against, at, lax.Precision.HIGHEST)


TILE = 2 * BLOCK
EDGE = 16
LANES = 512
INNER = DI // RANKS
HEADS = HM // RANKS
SIDE = 2 * NS // RANKS
CONV = INNER + SIDE


COST = 0.4e9


def call(cost, kernel, grid, in_specs, out_specs, out_shape, scratch=(), scalars=0):
    return pl.pallas_call(
        kernel,
        grid_spec=pltpu.PrefetchScalarGridSpec(
            num_scalar_prefetch=scalars,
            grid=grid,
            in_specs=in_specs,
            out_specs=out_specs,
            scratch_shapes=list(scratch),
        ),
        out_shape=out_shape,
        compiler_params=pltpu.CompilerParams(vmem_limit_bytes=48 * 1024 * 1024),
        cost_estimate=pl.CostEstimate(flops=int(cost * COST), bytes_accessed=10**6, transcendentals=0),
    )


def shape(dims, dtype=F32):
    return jax.ShapeDtypeStruct(dims, dtype)


def full(array):
    return pl.BlockSpec(array.shape, lambda *at: (0,) * array.ndim)


def tiled(width, rows=TILE):
    return pl.BlockSpec((rows, width), lambda i, *at: (i, 0))


def place_rows(scalars, gathered, rows):
    left, right, left_other, right_other = gathered
    half = left.shape[2]
    own = pl.multiple_of(scalars[0] * BLOCK, BLOCK)
    other = pl.multiple_of((1 - scalars[0]) * BLOCK, BLOCK)
    rows[pl.ds(own, BLOCK), :half] = left[0]
    rows[pl.ds(own, BLOCK), half:] = right[0]
    rows[pl.ds(other, BLOCK), :half] = left_other[0]
    rows[pl.ds(other, BLOCK), half:] = right_other[0]


def gathered_specs(gathered):
    spec = pl.BlockSpec((1, BLOCK, gathered[0].shape[2]), lambda i, s: (s[1 + i], 0, 0))
    return [spec] * 4


def halves_product(rows, mine, theirs):
    half = mine.shape[0]
    return dot(rows[:, :half], mine[...], (1, 0)) + dot(rows[:, half:], theirs[...], (1, 0))


def row_root(rows):
    values = rows.astype(F32)
    return lax.rsqrt(jnp.mean(values * values, axis=-1, keepdims=True) + epsilon)


def natural_blocks(dims):
    sh, sl, ch, width = dims
    block = width // (sh * sl * ch)
    return [
        (((a * sl + b) * ch + c) * block, ((a * ch + c) * sl + b) * block, block)
        for a in range(sh)
        for b in range(sl)
        for c in range(ch)
    ]


def related(place, start, dims):
    sh, _, ch, width = dims
    unit = width // (sh * ch) if ch == 2 else width // sh
    return pl.multiple_of(lax.bitwise_xor(place, start // unit) * unit + start % unit, 128)


def related_blocks(dims):
    sh, _, ch, width = dims
    unit = width // (sh * ch) if ch == 2 else width // sh
    return range(0, width, unit), unit


def whole_blocks(width):
    return pl.BlockSpec((BLOCK, width), lambda i, s: (0, 0))


def shuffle_kernel(dims, place, rows, out_refs, scratch):
    width = dims[3]
    for natural, start, block in natural_blocks(dims):
        scratch[:, start : start + block] = rows[:, natural : natural + block].astype(F32)
    starts, unit = related_blocks(dims)
    for start in starts:
        at = related(place, start, dims)
        out = out_refs[start // (width // 2)]
        inside = start % (width // 2)
        out[:, inside : inside + unit] = scratch[:, pl.ds(at, unit)].astype(BF)


def arrive_kernel(dims, place, tokens, cotangent, tl, tr, whole, scratch):
    half = dims[3] // 2
    shuffle_kernel(dims, place[0], tokens, (tl, tr), scratch)
    shuffle_kernel(dims, place[0], cotangent, (whole.at[:, :half], whole.at[:, half:]), scratch)


def arrive(dims, place, tokens, cotangent):
    width = dims[3]
    half = shape((BLOCK, width // 2), BF)
    return call(
        2.0,
        lambda *refs: arrive_kernel(dims, *refs),
        (1,),
        [whole_blocks(width)] * 2,
        [whole_blocks(width // 2)] * 2 + [whole_blocks(width)],
        [half] * 2 + [shape((BLOCK, width), BF)],
        [pltpu.VMEM((BLOCK, width), F32)],
        1,
    )(place, tokens, cotangent)


def leave_kernel(dims, added_to, place, rows, *refs):
    out, scratch = refs[-2], refs[-1]
    values = rows[...].astype(F32)
    if added_to:
        values = values + refs[0][...].astype(F32)
    scratch[...] = values
    sh, _, ch, width = dims
    unit = related_blocks(dims)[1]
    for natural, start, block in natural_blocks(dims):
        at = pl.multiple_of(related(place[0], start // unit * unit, dims), 128)
        if block % 128 == 0:
            got = scratch[:, pl.ds(pl.multiple_of(at + start % unit, 128), block)]
        else:
            got = scratch[:, pl.ds(at, unit)][:, start % unit : start % unit + block]
        out[:, natural : natural + block] = got.astype(out.dtype)


def leave(dims, place, rows, ordered, dtype):
    width = dims[3]
    ins = [rows] if ordered is None else [rows, ordered]
    return call(
        1.5,
        lambda *refs: leave_kernel(dims, ordered is not None, *refs),
        (1,),
        [whole_blocks(width)] * len(ins),
        whole_blocks(width),
        shape((BLOCK, width), dtype),
        [pltpu.VMEM((BLOCK, width), F32)],
        1,
    )(place, *ins)


def home_forward_kernel(dims, place, left, left_rest, right, right_rest, tl, tr, residual_ref, root_ref, l_ref, r_ref):
    half = left.shape[1]
    a = tl[...].astype(F32) + left[...] + left_rest[...].astype(F32)
    b = tr[...].astype(F32) + right[...] + right_rest[...].astype(F32)
    square = jnp.sum(a * a, axis=-1, keepdims=True) + jnp.sum(b * b, axis=-1, keepdims=True)
    root = lax.rsqrt(square / (2 * half) + epsilon)
    residual_ref[:, :half] = a
    residual_ref[:, half:] = b
    root_ref[...] = root
    starts, unit = related_blocks(dims)
    for start in starts:
        out, inside = (l_ref, start) if start < half else (r_ref, start - half)
        rows = residual_ref[:, pl.ds(related(place[0], start, dims), unit)]
        out[:, inside : inside + unit] = (rows * root).astype(BF)


def home_forward(dims, place, parts, tokens):
    half = dims[3] // 2
    return call(
        1.4,
        lambda *refs: home_forward_kernel(dims, *refs),
        (1,),
        [whole_blocks(half)] * 6,
        [whole_blocks(2 * half), whole_blocks(1), whole_blocks(half), whole_blocks(half)],
        [
            shape((BLOCK, 2 * half)),
            shape((BLOCK, 1)),
            shape((BLOCK, half), BF),
            shape((BLOCK, half), BF),
        ],
        (),
        1,
    )(place, *parts, *tokens)


def home_back_kernel(dims, place, left, left_rest, right, right_rest, values, root, base, grad_ref, l_ref, r_ref, scratch):
    half = left.shape[1]
    width = 2 * half
    scaled = root[...]
    scratch[:, :half] = left[...] + left_rest[...].astype(F32)
    scratch[:, half:] = right[...] + right_rest[...].astype(F32)
    starts, unit = related_blocks(dims)
    mean = jnp.zeros_like(scaled)
    for start in starts:
        norm = values[:, pl.ds(related(place[0], start, dims), unit)].astype(F32) * scaled
        up = scratch[:, start : start + unit]
        mean = mean + jnp.sum(up * norm, axis=-1, keepdims=True)
    mean = mean / width
    for start in starts:
        at = related(place[0], start, dims)
        norm = values[:, pl.ds(at, unit)].astype(F32) * scaled
        up = scratch[:, start : start + unit]
        grad_ref[:, pl.ds(at, unit)] = base[:, pl.ds(at, unit)].astype(F32) + scaled * (
            up - norm * mean
        )
    l_ref[...] = grad_ref[:, :half].astype(BF)
    r_ref[...] = grad_ref[:, half:].astype(BF)


def home_back(dims, place, parts, values, root, base):
    half = dims[3] // 2
    return call(
        1.4,
        lambda *refs: home_back_kernel(dims, *refs),
        (1,),
        [whole_blocks(half)] * 4 + [whole_blocks(2 * half), whole_blocks(1), whole_blocks(2 * half)],
        [whole_blocks(2 * half), whole_blocks(half), whole_blocks(half)],
        [shape((BLOCK, 2 * half)), shape((BLOCK, half), BF), shape((BLOCK, half), BF)],
        [pltpu.VMEM((BLOCK, 2 * half), F32)],
        1,
    )(place, *parts, values, root, base)


def project_inner_kernel(tiles, scalars, l, r, lo, ro, mine, theirs, halo, taps, steps, pre_ref, conv_ref, side_ref, keys_ref, step_ref, root_ref, edge_ref, rows, line):
    i = pl.program_id(0)
    place_rows(scalars, (l, r, lo, ro), rows)
    values = rows[...]
    root = row_root(values)
    root_ref[...] = root
    pre = halves_product(values, mine, theirs) * root
    pre_ref[...] = pre
    step_ref[...] = dot(values, steps[...], (1, 1)) * root

    @pl.when(i % tiles == 0)
    def _():
        before = halo[0]
        edge = halves_product(before, mine, theirs) * row_root(before)
        edge_ref[0] = edge
        line[:EDGE] = edge

    @pl.when(i % tiles != 0)
    def _():
        line[:EDGE] = line[TILE:]

    line[EDGE:] = pre
    conv = taps[KC : KC + 1, :]
    for k in range(KC):
        conv = conv + taps[k : k + 1, :] * line[EDGE - (KC - 1) + k : EDGE - (KC - 1) + k + TILE, :]
    conv_ref[...] = conv
    side_ref[...] = silu_value(conv[:, INNER:CONV]).astype(BF)
    keys_ref[...] = pre[:, CONV:].astype(BF)


def project_inner(scalars, gathered, weight, halo, taps, steps):
    seqs = halo.shape[0]
    total = 2 * 4 * BLOCK
    tiles = total // TILE // seqs
    width = 2 * gathered[0].shape[2]
    return call(
        10.4,
        lambda *refs: project_inner_kernel(tiles, *refs),
        (total // TILE,),
        gathered_specs(gathered)
        + [full(weight[0]), full(weight[1])]
        + [pl.BlockSpec((1, EDGE, width), lambda i, s: (i // tiles, 0, 0)), full(taps), full(steps)],
        [
            tiled(LANES),
            tiled(LANES),
            tiled(SIDE),
            tiled(SIDE),
            tiled(8),
            tiled(1),
            pl.BlockSpec((1, EDGE, LANES), lambda i, s: (i // tiles, 0, 0)),
        ],
        [
            shape((total, LANES)),
            shape((total, LANES)),
            shape((total, SIDE), BF),
            shape((total, SIDE), BF),
            shape((total, 8)),
            shape((total, 1)),
            shape((seqs, EDGE, LANES)),
        ],
        [pltpu.VMEM((TILE, width), BF), pltpu.VMEM((EDGE + TILE, LANES), F32)],
        1,
    )(scalars, *gathered, *weight, halo, taps, steps)


def project_gating_kernel(scalars, l, r, lo, ro, mine, theirs, root, gating_ref, query_ref, rows):
    place_rows(scalars, (l, r, lo, ro), rows)
    product = halves_product(rows[...], mine, theirs) * root[...]
    gating_ref[...] = product[:, :INNER]
    query_ref[...] = product[:, INNER:].astype(BF)


def project_gating(scalars, gathered, weight, root):
    total, width = root.shape[0], 2 * gathered[0].shape[2]
    return call(
        6.2,
        project_gating_kernel,
        (total // TILE,),
        gathered_specs(gathered) + [full(weight[0]), full(weight[1]), tiled(1)],
        [tiled(INNER), tiled(HD)],
        [shape((total, INNER)), shape((total, HD), BF)],
        [pltpu.VMEM((TILE, width), BF)],
        1,
    )(scalars, *gathered, *weight, root)


def rows_back_kernel(scalars, l, r, lo, ro, mine, theirs, ssm, gating, root, gain, mixer_ref, attn_ref, along_ref, gain_ref, rows):
    place_rows(scalars, (l, r, lo, ro), rows)
    product = halves_product(rows[...], mine, theirs)
    mixer = product[:, :INNER]
    mixer_ref[...] = mixer
    attn_ref[...] = product[:, INNER:].astype(BF)
    norm = ssm[...] * silu_value(gating[...]) * root[...]
    together = mixer * norm
    along_ref[0] = exact(jnp.ones((8, INNER), F32), together * gain[...], (1, 1))

    @pl.when(pl.program_id(0) == 0)
    def _():
        gain_ref[...] = jnp.zeros_like(gain_ref)

    gain_ref[...] += jnp.sum(together, axis=0, keepdims=True)


def rows_back(scalars, gathered, weight, ssm, gating, root, gain):
    total, width = root.shape[0], 2 * gathered[0].shape[2]
    tiles = total // TILE
    return call(
        9.5,
        rows_back_kernel,
        (tiles,),
        gathered_specs(gathered)
        + [full(weight[0]), full(weight[1]), tiled(INNER), tiled(INNER), tiled(1), full(gain)],
        [
            tiled(INNER),
            tiled(HD),
            pl.BlockSpec((1, 8, TILE), lambda i, s: (i, 0, 0)),
            pl.BlockSpec((1, INNER), lambda i, s: (0, 0)),
        ],
        [
            shape((total, INNER)),
            shape((total, HD), BF),
            shape((tiles, 8, TILE)),
            shape((1, INNER)),
        ],
        [pltpu.VMEM((TILE, width), BF)],
        1,
    )(scalars, *gathered, *weight, ssm, gating, root, gain)


def back_dot_kernel(terms, halves, scalars, *refs):
    ins, outs = refs[: terms * 4], refs[terms * 4 :]
    i = pl.program_id(0)
    for half in range(2):
        product = None
        for t in range(terms):
            first, second = ins[4 * t], ins[4 * t + 1]
            weight = ins[4 * t + 2 + half]
            rows = jnp.concatenate([first[...], second[...]], 0)
            at = (1, 1) if weight.shape[1] == rows.shape[1] else (1, 0)
            one = dot(rows, weight[...], at)
            product = one if product is None else product + one
        product = product.reshape(outs[half].shape)

        @pl.when(i < halves)
        def _():
            outs[2 + half][...] = product.astype(BF)

        @pl.when(i >= halves)
        def _():
            outs[half][...] = product


def back_dot(order, terms):
    total = terms[0][0].shape[0]
    half = terms[0][1][0].shape[0]
    halves = total // TILE // 2
    specs, arrays = [], []
    for rows, weights in terms:
        width = rows.shape[1]
        specs += [
            pl.BlockSpec((BLOCK, width), lambda i, s: (s[(2 * i + 4) % 8], 0)),
            pl.BlockSpec((BLOCK, width), lambda i, s: (s[(2 * i + 5) % 8], 0)),
            full(weights[0]),
            full(weights[1]),
        ]
        arrays += [rows, rows, *weights]
    kept_spec = pl.BlockSpec((2, BLOCK, half), lambda i, s: (jnp.maximum(i - halves, 0), 0, 0))
    given_spec = pl.BlockSpec((2, BLOCK, half), lambda i, s: (jnp.minimum(i, halves - 1), 0, 0))
    blocks = total // BLOCK // 2
    return call(
        3.0 + 3.0 * len(terms),
        lambda *refs: back_dot_kernel(len(terms), halves, *refs),
        (2 * halves,),
        specs,
        [kept_spec, kept_spec, given_spec, given_spec],
        [shape((blocks, BLOCK, half))] * 2 + [shape((blocks, BLOCK, half), BF)] * 2,
        (),
        1,
    )(order, *arrays)


def grad_dot_kernel(scalars, own, other, against, *refs):
    out, ordered = refs[-2], refs[-1]

    @pl.when(pl.program_id(0) == 0)
    def _():
        for k in range(8):
            start = pl.multiple_of(scalars[k] * BLOCK, BLOCK)
            ordered[k * BLOCK : (k + 1) * BLOCK] = against[pl.ds(start, BLOCK), :]

    tile = own.shape[2]
    rows = own.shape[0] * own.shape[1]
    product = dot(own[...].reshape(rows, tile), ordered[:rows], (0, 0))
    product = product + dot(other[...].reshape(rows, tile), ordered[rows:], (0, 0))
    out[...] = product.astype(out.dtype)


def grad_dot(order, parts, against, dtype):
    total, width = against.shape
    blocks = total // BLOCK // 2
    tile = 512
    half = parts[0][3]
    specs = [
        pl.BlockSpec((blocks, BLOCK, tile), lambda i, s, at=at, off=off: (at, 0, i + off // tile))
        for _, at, off, _ in parts
    ]
    return call(
        3.1,
        grad_dot_kernel,
        (half // tile,),
        [*specs, full(against)],
        pl.BlockSpec((tile, width), lambda i, s: (i, 0)),
        shape((half, width), dtype),
        [pltpu.VMEM((total, width), BF)],
        1,
    )(order, *(array for array, _, _, _ in parts), against)


def gathered_halves(gathered):
    left, right, left_other, right_other = gathered
    half = left.shape[2]
    return [(left, 0, 0, half), (left_other, 0, 0, half)], [
        (right, 0, 0, half),
        (right_other, 0, 0, half),
    ]


def straight_halves(rows):
    total, width = rows.shape
    rows = rows.reshape(total // BLOCK, BLOCK, width)
    half = width // 2
    return [(rows, 0, 0, half), (rows, 1, 0, half)], [(rows, 0, half, half), (rows, 1, half, half)]


def grad_halves(order, halves, against):
    theirs = grad_dot(order, halves[1], against, BF)
    return grad_dot(order, halves[0], against, F32), theirs


def feed_kernel(scalars, l, r, lo, ro, cotangent, gm, gt, lm, lt, dm, dt, active_ref, gate_ref, lift_ref, rows):
    place_rows(scalars, (l, r, lo, ro), rows)
    values = rows[...]
    gate = halves_product(values, gm, gt)
    lift = halves_product(values, lm, lt)
    grad = halves_product(cotangent[...], dm, dt)
    sigmoid_part = jax.nn.sigmoid(gate)
    swish = gate * sigmoid_part
    active_ref[...] = (swish * lift).astype(BF)
    gate_ref[...] = (grad * lift * sigmoid_part * (1.0 + gate * (1.0 - sigmoid_part))).astype(BF)
    lift_ref[...] = (grad * swish).astype(BF)


def feed_block(scalars, gathered, cotangent, gate, lift, drop):
    total, width = cotangent.shape
    weights = [*gate, *lift, *drop]
    return call(
        11.8,
        feed_kernel,
        (total // TILE,),
        gathered_specs(gathered) + [tiled(width)] + [full(w) for w in weights],
        [tiled(LANES)] * 3,
        [shape((total, LANES), BF)] * 3,
        [pltpu.VMEM((TILE, width), BF)],
        1,
    )(scalars, *gathered, cotangent, *weights)


def forth_dot_kernel(rows, mine, theirs, out):
    half = mine.shape[0]
    out[:, :half] = dot(rows[...], mine[...], (1, 1)).astype(BF)
    out[:, half:] = dot(rows[...], theirs[...], (1, 1)).astype(BF)


def forth_dot(rows, weights):
    total, k = rows.shape
    width = 2 * weights[0].shape[0]
    return call(
        4.2,
        forth_dot_kernel,
        (total // TILE,),
        [tiled(k), full(weights[0]), full(weights[1])],
        tiled(width),
        shape((total, width), BF),
    )(rows, *weights)


def keys_kernel(seqs, parts, out):
    for n in range(seqs):
        out[n] = jnp.concatenate([parts[r][:, n * SIDE : (n + 1) * SIDE] for r in range(4)], 1)


def keys_of(seqs, parts):
    count = parts.shape[1]
    return call(
        1.7,
        lambda *refs: keys_kernel(seqs, *refs),
        (count // TILE,),
        [pl.BlockSpec((4, TILE, seqs * SIDE), lambda i: (0, i, 0))],
        pl.BlockSpec((seqs, TILE, 2 * HD), lambda i: (0, i, 0)),
        shape((seqs, count, 2 * HD), BF),
    )(parts)


def scores_of(place, queries, keys):
    count, whole = queries.shape[0], keys.shape[0]
    scores = dot(queries, keys, (1, 1)) * HD**-0.5
    row = place + pl.program_id(1) * count + lax.broadcasted_iota(jnp.int32, (count, whole), 0)
    column = lax.broadcasted_iota(jnp.int32, (count, whole), 1)
    return scores, row >= column


def attend_kernel(place, queries, key_value, out_ref, log_ref):
    keys, values = key_value[0, :, :HD], key_value[0, :, HD:]
    scores, visible = scores_of(place[0], queries[...], keys)
    scores = jnp.where(visible, scores, negative)
    top = jnp.max(scores, axis=-1, keepdims=True)
    weights = jnp.exp(scores - top)
    total = jnp.sum(weights, axis=-1, keepdims=True)
    log_ref[...] = top + jnp.log(total)
    out_ref[...] = dot(weights.astype(BF), values, (1, 0)) / total


def attend_specs(seqs, total):
    tiles = total // TILE // seqs
    rows = lambda width: pl.BlockSpec((TILE, width), lambda n, i, s: (n * tiles + i, 0))
    return (seqs, tiles), rows


def attend(place, queries, key_value):
    seqs, whole, width = key_value.shape
    total = queries.shape[0]
    grid, rows = attend_specs(seqs, total)
    return call(
        2.8,
        attend_kernel,
        grid,
        [rows(HD), pl.BlockSpec((1, whole, width), lambda n, i, s: (n, 0, 0))],
        [rows(HD), rows(1)],
        [shape((total, HD)), shape((total, 1))],
        (),
        1,
    )(place, queries, key_value)


def attend_back_kernel(place, queries, grads, attended, logs, root, key_value, query_ref, sum_ref):
    keys, values = key_value[0, :, :HD], key_value[0, :, HD:]
    scores, visible = scores_of(place[0], queries[...], keys)
    probs = jnp.where(visible, jnp.exp(scores - logs[...]), 0.0)
    grad = grads[...]
    delta = jnp.sum(grad.astype(F32) * attended[...], axis=-1, keepdims=True)
    scores_grad = (probs * (dot(grad, values, (1, 1)) - delta)).astype(BF)
    query_ref[...] = (dot(scores_grad, keys, (1, 0)) * (HD**-0.5 * root[...])).astype(BF)

    @pl.when((pl.program_id(0) == 0) & (pl.program_id(1) == 0))
    def _():
        sum_ref[...] = jnp.zeros_like(sum_ref)

    key_sum = dot(scores_grad, queries[...], (0, 0)) * HD**-0.5
    value_sum = dot(probs.astype(BF), grad, (0, 0))
    for n in range(sum_ref.shape[2] // SIDE):

        @pl.when(pl.program_id(0) == n)
        def _():
            at = slice(n * SIDE, (n + 1) * SIDE)
            sum_ref[0, :, at] += key_sum[:, :SIDE]
            sum_ref[1, :, at] += key_sum[:, SIDE:]
            sum_ref[2, :, at] += value_sum[:, :SIDE]
            sum_ref[3, :, at] += value_sum[:, SIDE:]


def attend_back(place, queries, grads, attended, logs, root, key_value):
    seqs, whole, width = key_value.shape
    total = queries.shape[0]
    grid, rows = attend_specs(seqs, total)
    sums = pl.BlockSpec((1, whole, width), lambda n, i, s: (n, 0, 0))
    return call(
        5,
        attend_back_kernel,
        grid,
        [rows(HD), rows(HD), rows(HD), rows(1), rows(1), sums],
        [rows(HD), pl.BlockSpec((4, whole, seqs * SIDE), lambda n, i, s: (0, 0, 0))],
        [shape((total, HD), BF), shape((4, whole, seqs * SIDE))],
        (),
        1,
    )(place, queries, grads, attended, logs, root, key_value)


def over_heads(values):
    rows = values.shape[0]
    return jnp.concatenate(
        [jnp.broadcast_to(values[:, h : h + 1], (rows, PM)) for h in range(HEADS)], 1
    )


def head_sums(values):
    channel = lax.broadcasted_iota(jnp.int32, (INNER, 8), 0)
    head = lax.broadcasted_iota(jnp.int32, (INNER, 8), 1)
    return exact(values, jnp.where(channel // PM == head, 1.0, 0.0), (1, 0))


def triangle():
    row = lax.broadcasted_iota(jnp.int32, (BLOCK, BLOCK), 0)
    column = lax.broadcasted_iota(jnp.int32, (BLOCK, BLOCK), 1)
    return row, column


def block_steps(step_pre, head):
    arg = step_pre + head[0:1, :]
    size = jnp.maximum(arg, 0.0) + jnp.log1p(jnp.exp(-jnp.abs(arg)))
    row, column = triangle()
    cum = exact(jnp.where(row >= column, 1.0, 0.0), size * head[1:2, :], (1, 0))
    return arg, size, cum


def as_rows(values):
    row, column = triangle()
    return exact(values, jnp.where(row == column, 1.0, 0.0), (0, 0))


def as_columns(values):
    row, column = triangle()
    return exact(jnp.where(row == column, 1.0, 0.0), values, (1, 1))


def joined(sides, first, n):
    return jnp.concatenate(
        [sides[r][:, n * SIDE : (n + 1) * SIDE] for r in range(first, first + 4)], 1
    )


def pair(seqs, width, back=0):
    if back:
        return pl.BlockSpec((seqs, BLOCK, width), lambda i, *s: (0, back - 1 - i, 0))
    return pl.BlockSpec((seqs, BLOCK, width), lambda i, *s: (0, i, 0))


def by_seq(seqs, *arrays):
    return [a.reshape(*a.shape[:-2], seqs, -1, a.shape[-1]) for a in arrays]


def states_kernel(seqs, blocks, step_pre, head, conv, sides, out_ref, decay_ref, run):
    i = pl.program_id(0)

    @pl.when(i == 0)
    def _():
        run[...] = jnp.zeros_like(run)
        decay_ref[...] = jnp.ones_like(decay_ref)

    for n in range(seqs):
        _, size, cum = block_steps(step_pre[n], head)
        last = cum[BLOCK - 1 :, :]
        feeding = jnp.exp(last - cum) * size
        inner = silu_value(conv[n, :, :INNER])
        in_state = joined(sides, 0, n)
        fresh = dot(in_state, (over_heads(feeding) * inner).astype(BF), (0, 0))
        decay = over_heads(jnp.exp(last))
        run[n] = decay * run[n] + fresh
        decay_ref[n] = decay_ref[n] * decay

    @pl.when(i == blocks - 1)
    def _():
        out_ref[...] = run[...].astype(BF)


def states(seqs, step_pre, head, conv, sides):
    step_pre, conv = by_seq(seqs, step_pre, conv)
    blocks = conv.shape[1] // BLOCK
    return call(
        4.5,
        lambda *refs: states_kernel(seqs, blocks, *refs),
        (blocks,),
        [
            pair(seqs, 8),
            full(head),
            pair(seqs, LANES),
            pl.BlockSpec((4, BLOCK, seqs * SIDE), lambda i: (0, i, 0)),
        ],
        [
            pl.BlockSpec((seqs, NS, INNER), lambda i: (0, 0, 0)),
            pl.BlockSpec((seqs, 1, INNER), lambda i: (0, 0, 0)),
        ],
        [shape((seqs, NS, INNER), BF), shape((seqs, 1, INNER))],
        [pltpu.VMEM((seqs, NS, INNER), F32)],
    )(step_pre, head, conv, sides)


def fading_of(cum, cum_rows, h):
    row, column = triangle()
    span = cum[:, h : h + 1] - cum_rows[h : h + 1, :]
    return jnp.where(row >= column, jnp.exp(jnp.minimum(span, 0.0)), 0.0)


def ssm_kernel(seqs, step_pre, head, conv, sides, gating, entry, ssm_ref, carried_ref, square_ref, run):
    @pl.when(pl.program_id(0) == 0)
    def _():
        run[...] = entry[...].astype(F32)

    for n in range(seqs):
        _, size, cum = block_steps(step_pre[n], head)
        size_rows, cum_rows = as_rows(size), as_rows(cum)
        last = cum[BLOCK - 1 :, :]
        inner = silu_value(conv[n, :, :INNER])
        inner_low = inner.astype(BF)
        in_state, out_state = joined(sides, 0, n), joined(sides, 4, n)
        before = run[n]
        carried = before.astype(BF)
        carried_ref[n, 0] = carried
        pairing = dot(out_state, in_state, (1, 1))
        within = []
        for h in range(HEADS):
            mixing = fading_of(cum, cum_rows, h) * pairing * size_rows[h : h + 1, :]
            within.append(dot(mixing.astype(BF), inner_low[:, h * PM : (h + 1) * PM], (1, 0)))
        readout = dot(out_state, carried, (1, 0))
        ssm = (
            jnp.concatenate(within, 1)
            + over_heads(jnp.exp(cum)) * readout
            + over_heads(head[2:3, :]) * inner
        )
        ssm_ref[n] = ssm
        gated = ssm * silu_value(gating[n])
        square_ref[0, n] = exact(jnp.ones((8, INNER), F32), gated * gated, (1, 1))
        feeding = jnp.exp(last - cum) * size
        fresh = dot(in_state, (over_heads(feeding) * inner).astype(BF), (0, 0))
        run[n] = over_heads(jnp.exp(last)) * before + fresh


def ssm_block(seqs, step_pre, head, conv, sides, gating, entry):
    total = conv.shape[0]
    step_pre, conv, gating = by_seq(seqs, step_pre, conv, gating)
    count = conv.shape[1]
    blocks = count // BLOCK
    ssm, carried, square = call(
        11.2,
        lambda *refs: ssm_kernel(seqs, *refs),
        (blocks,),
        [
            pair(seqs, 8),
            full(head),
            pair(seqs, LANES),
            pl.BlockSpec((RANKS, BLOCK, seqs * SIDE), lambda i: (0, i, 0)),
            pair(seqs, INNER),
            full(entry),
        ],
        [
            pair(seqs, INNER),
            pl.BlockSpec((seqs, 1, NS, INNER), lambda i: (0, i, 0, 0)),
            pl.BlockSpec((1, seqs, 8, BLOCK), lambda i: (i, 0, 0, 0)),
        ],
        [
            shape((seqs, count, INNER)),
            shape((seqs, blocks, NS, INNER), BF),
            shape((blocks, seqs, 8, BLOCK)),
        ],
        [pltpu.VMEM((seqs, NS, INNER), F32)],
    )(step_pre, head, conv, sides, gating, entry)
    square = square[:, :, 0].swapaxes(0, 1).reshape(total // BLOCK, BLOCK)
    return ssm.reshape(total, INNER), carried, square


def states_back_kernel(seqs, blocks, step_pre, head, sides, mixer, ssm, gating, mixer_root, along, gain, root, grad_ref, gating_ref, out_ref, run):
    i = pl.program_id(0)

    @pl.when(i == 0)
    def _():
        run[...] = jnp.zeros_like(run)

    for n in range(seqs):
        _, _, cum = block_steps(step_pre[n], head)
        gate = gating[n]
        sigmoid_part = jax.nn.sigmoid(gate)
        act = gate * sigmoid_part
        values = ssm[n]
        scaled = mixer_root[n]
        norm = values * act * scaled
        gated_grad = scaled * (mixer[n] * gain[...] - norm * along[n])
        grad = gated_grad * act
        grad_ref[n] = grad
        slope = sigmoid_part * (1.0 + gate * (1.0 - sigmoid_part))
        gating_ref[n] = (gated_grad * values * slope * root[n]).astype(BF)
        grown = (over_heads(jnp.exp(cum)) * grad).astype(BF)
        fresh = dot(joined(sides, 0, n), grown, (0, 0))
        run[n] = over_heads(jnp.exp(cum[BLOCK - 1 :, :])) * run[n] + fresh

    @pl.when(i == blocks - 1)
    def _():
        out_ref[...] = run[...].astype(BF)


def states_back(seqs, step_pre, head, sides, mixer, ssm, gating, mixer_root, along, gain, root):
    total = ssm.shape[0]
    step_pre, mixer, ssm, gating, mixer_root, along, root = by_seq(
        seqs, step_pre, mixer, ssm, gating, mixer_root, along, root
    )
    count = ssm.shape[1]
    blocks = count // BLOCK
    back = lambda width: pair(seqs, width, blocks)
    grad, gating_grad, leaving = call(
        6.6,
        lambda *refs: states_back_kernel(seqs, blocks, *refs),
        (blocks,),
        [back(8), full(head)]
        + [pl.BlockSpec((4, BLOCK, seqs * SIDE), lambda i: (1, blocks - 1 - i, 0))]
        + [back(INNER), back(INNER), back(INNER), back(1), back(1), full(gain), back(1)],
        [back(INNER), back(INNER), pl.BlockSpec((seqs, NS, INNER), lambda i: (0, 0, 0))],
        [
            shape((seqs, count, INNER)),
            shape((seqs, count, INNER), BF),
            shape((seqs, NS, INNER), BF),
        ],
        [pltpu.VMEM((seqs, NS, INNER), F32)],
    )(step_pre, head, sides, mixer, ssm, gating, mixer_root, along, gain, root)
    return grad.reshape(total, INNER), gating_grad.reshape(total, INNER), leaving


def ssm_back_one(n, step_pre, head, conv, sides, grads, carried_ref, root, conv_ref, step_ref, sums_ref, later):
    arg, size, cum = block_steps(step_pre[n], head)
    size_rows, cum_rows = as_rows(size), as_rows(cum)
    last = cum[BLOCK - 1 :, :]
    growth, to_end, decay = jnp.exp(cum), jnp.exp(last - cum), jnp.exp(last)
    feeding = to_end * size
    conv_sum = conv[n, :, :INNER]
    inner = silu_value(conv_sum)
    inner_low = inner.astype(BF)
    in_state, out_state = joined(sides, 0, n), joined(sides, 4, n)
    carried = carried_ref[n, 0]
    after = later[n]
    after_low = after.astype(BF)
    grad = grads[n]
    grad_low = grad.astype(BF)
    pairing = dot(out_state, in_state, (1, 1))
    readout = dot(out_state, carried, (1, 0))
    spread = dot(in_state, after_low, (1, 0))
    grown = (over_heads(growth) * grad).astype(BF)
    feeding_wide = over_heads(feeding)
    fed_inner = (feeding_wide * inner).astype(BF)
    pairing_grad = jnp.zeros((BLOCK, BLOCK), F32)
    inner_parts, flows, step_rows = [], [], []
    for h in range(HEADS):
        at = slice(h * PM, (h + 1) * PM)
        fading = fading_of(cum, cum_rows, h)
        sized = size_rows[h : h + 1, :]
        mixing = (fading * pairing * sized).astype(BF)
        faded = dot(grad_low[:, at], inner_low[:, at], (1, 1)) * fading
        pairing_grad = pairing_grad + faded * sized
        stepwise = faded * pairing
        step_rows.append(jnp.sum(stepwise, axis=0, keepdims=True))
        flows.append(jnp.sum(stepwise * sized, axis=1, keepdims=True))
        inner_parts.append(dot(mixing, grad_low[:, at], (0, 0)))
    empty_row, empty_column = jnp.zeros((2, BLOCK), F32), jnp.zeros((BLOCK, 2), F32)
    step_rows = jnp.concatenate(step_rows + [empty_row], 0)
    flow = jnp.concatenate(flows + [empty_column], 1)
    pairing_low = pairing_grad.astype(BF)
    out_grad = dot(pairing_low, in_state, (1, 0)) + dot(grown, carried, (1, 1))
    in_grad = dot(pairing_low, out_state, (0, 0)) + dot(fed_inner, after_low, (1, 1))
    inner_grad = (
        jnp.concatenate(inner_parts, 1) + over_heads(head[2:3, :]) * grad + feeding_wide * spread
    )
    conv_ref[n] = inner_grad * silu_slope(conv_sum)
    feeding_grad = head_sums(spread * inner)
    fed = feeding_grad * feeding
    through = jnp.sum(after * carried.astype(F32), axis=0, keepdims=True)
    through = head_sums(jnp.broadcast_to(through, (8, INNER)))[:1]
    last_grad = jnp.sum(fed, axis=0, keepdims=True) + through * decay
    cum_grad = flow - as_columns(step_rows * size_rows) + head_sums(grad * readout) * growth - fed
    row, column = triangle()
    increment = exact(jnp.where(column >= row, 1.0, 0.0), cum_grad, (1, 0)) + last_grad
    rates = head[1:2, :]
    step_grad = as_columns(step_rows) + feeding_grad * to_end + increment * rates
    arg_grad = step_grad * jax.nn.sigmoid(arg)
    step_ref[n] = (arg_grad * root[n]).astype(BF)
    skip = jnp.broadcast_to(jnp.sum(grad * inner, axis=0, keepdims=True), (8, INNER))
    sums_ref[0:1, :] += jnp.sum(arg_grad, axis=0, keepdims=True)
    sums_ref[1:2, :] += jnp.sum(increment * size, axis=0, keepdims=True) * rates
    sums_ref[2:3, :] += head_sums(skip)[:1]
    later[n] = over_heads(decay) * after + dot(out_state, grown, (0, 0))
    return in_grad, out_grad


def ssm_back_kernel(seqs, step_pre, head, conv, sides, grads, carried, entry, root, conv_ref, parts_ref, step_ref, sums_ref, later):
    @pl.when(pl.program_id(0) == 0)
    def _():
        later[...] = entry[...].astype(F32)
        sums_ref[...] = jnp.zeros_like(sums_ref)

    grad_pairs = [
        ssm_back_one(
            n, step_pre, head, conv, sides, grads, carried, root, conv_ref, step_ref, sums_ref, later
        )
        for n in range(seqs)
    ]
    for rank in range(RANKS):
        at = (rank % 4) * SIDE
        parts_ref[rank] = jnp.concatenate(
            [grad[rank // 4][:, at : at + SIDE] for grad in grad_pairs], 1
        ).astype(BF)


def ssm_back(seqs, step_pre, head, conv, sides, grads, carried, entry, root):
    total = conv.shape[0]
    step_pre, conv, grads, root = by_seq(seqs, step_pre, conv, grads, root)
    count = conv.shape[1]
    blocks = count // BLOCK
    back = lambda width: pair(seqs, width, blocks)
    conv_grad, parts, step_rows, sums = call(
        19,
        lambda *refs: ssm_back_kernel(seqs, *refs),
        (blocks,),
        [
            back(8),
            full(head),
            back(LANES),
            pl.BlockSpec((RANKS, BLOCK, seqs * SIDE), lambda i: (0, blocks - 1 - i, 0)),
            back(INNER),
            pl.BlockSpec((seqs, 1, NS, INNER), lambda i: (0, blocks - 1 - i, 0, 0)),
            full(entry),
            back(1),
        ],
        [
            back(INNER),
            pl.BlockSpec((RANKS, BLOCK, seqs * SIDE), lambda i: (0, blocks - 1 - i, 0)),
            back(8),
            pl.BlockSpec((8, 8), lambda i: (0, 0)),
        ],
        [
            shape((seqs, count, INNER)),
            shape((RANKS, count, seqs * SIDE), BF),
            shape((seqs, count, 8), BF),
            shape((8, 8)),
        ],
        [pltpu.VMEM((seqs, NS, INNER), F32)],
    )(step_pre, head, conv, sides, grads, carried, entry, root)
    return conv_grad.reshape(total, INNER), parts, step_rows.reshape(total, 8), sums


def conv_back_kernel(tiles, inner, parts, keys, conv, pre, edge, grad_ref, sums_ref, line):
    i = pl.program_id(0)
    first = i < tiles
    got = jnp.sum(parts[...].astype(F32), axis=0)
    got = jnp.where(first, got[:, :SIDE], got[:, SIDE:]) * silu_slope(conv[:, INNER:CONV])
    keys_got = keys[...]
    keys_got = jnp.where(first, keys_got[:, :SIDE], keys_got[:, SIDE:])
    got = jnp.concatenate([got, keys_got], 1)
    grad = jnp.concatenate([inner[...], got], 1)
    grad_ref[...] = grad

    @pl.when(i % tiles == 0)
    def _():
        line[:EDGE] = edge[0]

    @pl.when(i % tiles != 0)
    def _():
        line[:EDGE] = line[TILE:]

    @pl.when(i == 0)
    def _():
        sums_ref[...] = jnp.zeros_like(sums_ref)

    line[EDGE:] = pre[...]
    for k in range(KC):
        before = line[EDGE - (KC - 1) + k : EDGE - (KC - 1) + k + TILE, :]
        sums_ref[k : k + 1, :] += jnp.sum(grad * before, axis=0, keepdims=True)
    sums_ref[KC : KC + 1, :] += jnp.sum(grad, axis=0, keepdims=True)


def conv_back(inner, parts, keys, conv, pre, edge):
    total = conv.shape[0]
    tiles = total // TILE // edge.shape[0]
    return call(
        4.8,
        lambda *refs: conv_back_kernel(tiles, *refs),
        (total // TILE,),
        [
            tiled(INNER),
            pl.BlockSpec((RANKS, TILE, 2 * SIDE), lambda i: (0, i % tiles, 0)),
            pl.BlockSpec((TILE, 2 * SIDE), lambda i: (i % tiles, 0)),
            tiled(LANES),
            tiled(LANES),
            pl.BlockSpec((1, EDGE, LANES), lambda i: (i // tiles, 0, 0)),
        ],
        [tiled(LANES), pl.BlockSpec((8, LANES), lambda i: (0, 0))],
        [shape((total, LANES)), shape((8, LANES))],
        [pltpu.VMEM((EDGE + TILE, LANES), F32)],
    )(inner, parts, keys, conv, pre, edge)


def pre_back_kernel(tiles, grad, after, follow, taps, root, out_ref, line):
    i = pl.program_id(0)
    line[:TILE] = grad[...]

    @pl.when(i % tiles == tiles - 1)
    def _():
        line[TILE:] = follow[0]

    @pl.when(i % tiles != tiles - 1)
    def _():
        line[TILE:] = after[...]

    total = taps[KC - 1 : KC, :] * line[:TILE, :]
    for k in range(KC - 1):
        total = total + taps[k : k + 1, :] * line[KC - 1 - k : KC - 1 - k + TILE, :]
    out_ref[...] = (total * root[...]).astype(BF)


def pre_back(grad, follow, taps, root):
    total = grad.shape[0]
    tiles = total // TILE // follow.shape[0]
    last = total // EDGE - 1
    return call(
        1.4,
        lambda *refs: pre_back_kernel(tiles, *refs),
        (total // TILE,),
        [
            tiled(LANES),
            pl.BlockSpec((EDGE, LANES), lambda i: (jnp.minimum((i + 1) * (TILE // EDGE), last), 0)),
            pl.BlockSpec((1, EDGE, LANES), lambda i: (i // tiles, 0, 0)),
            full(taps),
            tiled(1),
        ],
        tiled(LANES),
        shape((total, LANES), BF),
        [pltpu.VMEM((TILE + EDGE, LANES), F32)],
    )(grad, grad, follow, taps, root)


def local(
    tokens,
    cotangent,
    norm_gain,
    gating_weight,
    inner_weight,
    state_weight,
    step_weight,
    conv_weight,
    conv_bias,
    mixer_gain,
    mixer_out,
    query_weight,
    key_weight,
    value_weight,
    output_weight,
    feed_gain,
    gate_matrix,
    lift_matrix,
    drop_matrix,
    step_bias,
    decay_log,
    skip_scale,
):
    sh, sl, ch = lax.axis_size("sh"), lax.axis_size("sl"), lax.axis_size("ch")
    world = sh * sl * ch * 4
    rows, width = tokens.shape
    drows = norm_gain.shape[0]
    my_sl, my_zl, my_core = (lax.axis_index(axis) for axis in TEAM)
    rank = (my_sl * 2 + my_zl) * 2 + my_core
    total = RANKS * rows
    count = 4 * rows
    whole = ch * count

    order = team_order()
    straight = jnp.arange(8, dtype=jnp.int32)
    tiles = [((z ^ my_zl) * 2 + (s ^ my_sl)) for s in (0, 1) for z in (0, 1)]
    scalars = jnp.stack([my_core, *tiles]).astype(jnp.int32)
    place = (lax.axis_index("ch") * count).astype(jnp.int32).reshape(1)
    dims = (sh, sl, ch, width)
    home = column_blocks(sh, sl, ch)
    nowhere = jnp.zeros_like(home)

    def scaled(weight, gain):
        return (weight.astype(F32) * gain.astype(F32)[:, None]).astype(BF)

    key_value = jnp.stack(
        [key_weight.reshape(drows, HK, 2, SIDE), value_weight.reshape(drows, HK, 2, SIDE)], 2
    ).reshape(drows, RANKS * SIDE)
    pack_in = jnp.concatenate(
        [
            by_rank(scaled(w, norm_gain))
            for w in (inner_weight, state_weight, key_value, gating_weight, query_weight)
        ],
        2,
    )
    conv_own, gain_own = conv_weight.shape[1], mixer_gain.shape[0]
    step_sent = jnp.broadcast_to(
        scaled(step_weight, norm_gain).T.reshape(1, sl, 1, 4, HEADS * drows),
        (sh, sl, ch, 4, HEADS * drows),
    ).reshape(world, HEADS * drows)
    shared = jnp.concatenate([conv_weight.reshape(-1), conv_bias, mixer_gain])
    small = jnp.concatenate(
        [jnp.broadcast_to(shared[None], (world, shared.shape[0])), step_sent], 1
    )
    with jax.named_scope("small_exchange"):
        small = lax.all_to_all(small, WORLD, split_axis=0, concat_axis=0, tiled=True)
    small, pack_in = together(small, pack_in)
    with jax.named_scope("weights_in"):
        mixed_in = ranks_exchange(pack_in)
    *own_tokens, own_cotangent = arrive(dims, home, tokens, cotangent)
    with jax.named_scope("tokens_gather"):
        before = jnp.stack([part[rows - EDGE :] for part in own_tokens])
        before = shifted(before, 1)
        if ch == 2:
            before = jnp.flip(before.reshape(2, EDGE, sh // 2, ch, -1), 3)
            before = before.reshape(2, EDGE, width // 2)
        team_tokens = list(
            team_gather(*(jnp.concatenate([own_tokens[h], before[h]], 0) for h in range(2)))
        )
    ends = []
    for seq in range(sl):
        at_block = 2 * (1 - my_zl) + (seq ^ my_sl)
        halves = []
        for own, other in ((team_tokens[0], team_tokens[2]), (team_tokens[1], team_tokens[3])):
            own = lax.dynamic_index_in_dim(own[:, rows:], at_block, 0, False)
            other = lax.dynamic_index_in_dim(other[:, rows:], at_block, 0, False)
            halves.append(jnp.where(my_core == 1, own, other))
        ends.append(jnp.concatenate(halves, 1))
    halo = jnp.stack(ends)
    with jax.named_scope("weights_first"):
        ready = along_ch(mixed_in[:, :LANES])
    pack_rest = jnp.concatenate(
        [by_rank(mixer_out.T), by_rank(output_weight.T)]
        + [by_rank(scaled(w, feed_gain)) for w in (gate_matrix, lift_matrix)]
        + [by_rank(drop_matrix.T)],
        2,
    )
    pack_rest, sent_cotangent, *team_tokens = together(pack_rest, own_cotangent, *team_tokens)
    with jax.named_scope("weights_rest"):
        mixed_rest = ranks_exchange(pack_rest)
    team_cotangent = lax.all_gather(sent_cotangent, TEAM, axis=0, tiled=True)
    with jax.named_scope("weights_inner"):
        theirs, gating_ready, mixed_rest = together(
            swap(ready, "sh"), along_ch(mixed_in[:, LANES:]), mixed_rest
        )
    w_inner = (ready, theirs)

    at = (KC + 1) * conv_own
    wide_conv = small[:, :at].reshape(world, KC + 1, conv_own)
    wide_conv = wide_conv.transpose(1, 0, 2).reshape(KC + 1, -1).astype(F32)
    wide_gain = small[:, at : at + gain_own].reshape(1, -1).astype(F32)
    own_step = small[:, at + gain_own :].reshape(sh, sl, ch, 4, HEADS, drows).swapaxes(1, 2)
    own_step = relative(relative(own_step, "sh", 0), "ch", 1)
    own_step = own_step.reshape(-1, HEADS, drows).swapaxes(0, 1).reshape(HEADS, width)
    own_step = jnp.pad(own_step, ((0, 8 - HEADS), (0, 0)))
    taps = jnp.concatenate(
        [
            lax.dynamic_slice_in_dim(wide_conv, rank * INNER, INNER, 1),
            lax.dynamic_slice_in_dim(wide_conv, DI + rank * SIDE, SIDE, 1),
            jnp.zeros((KC + 1, LANES - CONV), F32).at[KC - 1].set(1.0),
        ],
        1,
    )
    taps = jnp.pad(taps, ((0, 8 - KC - 1), (0, 0)))
    own_gain = lax.dynamic_slice_in_dim(wide_gain, rank * INNER, INNER, 1)
    head = jnp.stack([step_bias, -jnp.exp(decay_log), skip_scale])
    head = lax.dynamic_slice_in_dim(head, rank * HEADS, HEADS, 1)
    head = jnp.pad(head, ((0, 5), (0, 8 - HEADS)))

    pre, conv, side, own_keys, step_pre, root, edge = project_inner(
        scalars, team_tokens, w_inner, halo, taps, own_step
    )
    def packed(values):
        return values.reshape(sl, count, SIDE).swapaxes(0, 1).reshape(count, sl * SIDE)

    sides = lax.all_gather(packed(side), TEAM)
    with jax.named_scope("keys_exchange"):
        own_keys = packed(own_keys)[None]
        if ch == 2:
            own_keys = paired(own_keys[0], swap(own_keys[0], "ch"), "ch", 0)
        elif ch > 2:
            own_keys = lax.all_gather(own_keys[0], "ch")
        own_keys = paired(own_keys, swap(own_keys, "zl"), "zl", 0)
        own_keys = paired(own_keys, swap(own_keys, "core"), "core", 1)
        key_value_rows = keys_of(sl, own_keys.reshape(4, whole, sl * SIDE))
    with jax.named_scope("weights_gating"):
        theirs, out_ready = together(
            swap(gating_ready, "sh"), along_ch(mixed_rest[:, :LANES])
        )
    w_gating = (gating_ready, theirs)
    gating, queries = project_gating(scalars, team_tokens, w_gating, root)
    rest = [mixed_rest[:, at * LANES : (at + 1) * LANES] for at in range(1, 4)]
    with jax.named_scope("weights_out"):
        theirs, gate_ready = together(swap(out_ready, "sh"), along_ch(rest[0]))
    w_out = (out_ready, theirs)
    leaving, piece_decay = states(sl, step_pre, head, conv, sides)
    with jax.named_scope("state_exchange"):
        entry = entering(piece_decay[:, 0], leaving, False)
    entry, gate_ready = together(entry, gate_ready)
    with jax.named_scope("weights_gate"):
        theirs, lift_ready = together(swap(gate_ready, "sh"), along_ch(rest[1]))
    w_gate = (gate_ready, theirs)
    attended, logs = attend(place, queries, key_value_rows)
    ssm, carried, square = ssm_block(sl, step_pre, head, conv, sides, gating, entry)
    with jax.named_scope("square_sum"):
        square = team_sum(square)
    mixer_root = lax.rsqrt(square / DI + epsilon).reshape(total, 1)
    branch_rows = jnp.concatenate(
        [(ssm * silu_value(gating) * mixer_root * own_gain).astype(BF), attended.astype(BF)], 1
    )
    branch_rows, lift_ready = together(branch_rows, lift_ready)
    with jax.named_scope("weights_lift"):
        theirs, drop_ready = together(swap(lift_ready, "sh"), along_ch(rest[2]))
    w_lift = (lift_ready, theirs)
    branch_parts = back_dot(order, [(branch_rows, w_out)])
    with jax.named_scope("branch_scatter"):
        branch = team_scatter(branch_parts)
    branch = list(branch)
    drop_ready, branch[0] = together(drop_ready, branch[0])
    with jax.named_scope("weights_drop"):
        w_drop = (drop_ready, swap(drop_ready, "sh"))
    residual, feed_root, *feed_halves = home_forward(dims, nowhere, branch, own_tokens)
    with jax.named_scope("feed_gather"):
        feed_rows = team_gather(*feed_halves)
    active, gate_rows_grad, lift_rows_grad = feed_block(
        scalars, feed_rows, team_cotangent, w_gate, w_lift, w_drop
    )
    feed_parts = back_dot(order, [(gate_rows_grad, w_gate), (lift_rows_grad, w_lift)])
    with jax.named_scope("feed_scatter"):
        feed_grad = team_scatter(feed_parts)
    gate_mine, gate_theirs = grad_halves(order, gathered_halves(feed_rows), gate_rows_grad)
    with jax.named_scope("gate_back"):
        gate_theirs = swap(gate_theirs, "sh")
    feed_grad = list(feed_grad)
    feed_grad[0], gate_theirs, active = together(feed_grad[0], gate_theirs, active)
    lift_mine, lift_theirs = grad_halves(order, gathered_halves(feed_rows), lift_rows_grad)
    straight = jnp.arange(8, dtype=jnp.int32)
    drop_mine, drop_theirs = grad_halves(straight, straight_halves(team_cotangent), active)
    layer_part = forth_dot(active, w_drop)
    with jax.named_scope("lift_back"):
        lift_theirs, gate_part = together(
            swap(lift_theirs, "sh"), ch_part(added(gate_mine, gate_theirs))
        )
    residual_grad, *branch_halves = home_back(
        dims, nowhere, feed_grad, residual, feed_root, own_cotangent
    )
    with jax.named_scope("branch_gather"):
        branch_grad = team_gather(*branch_halves)
    layer_part, *branch_grad = together(layer_part, *branch_grad)
    layer_part = lax.psum_scatter(layer_part, TEAM, scatter_dimension=0, tiled=True)

    mixer_rows_grad, attn_grad, along, gain_part = rows_back(
        scalars, branch_grad, w_out, ssm, gating, mixer_root, own_gain
    )
    mixer_rows_grad, lift_theirs, gate_part = together(mixer_rows_grad, lift_theirs, gate_part)
    with jax.named_scope("drop_back"):
        drop_theirs, lift_part = together(
            swap(drop_theirs, "sh"), ch_part(added(lift_mine, lift_theirs))
        )
    with jax.named_scope("along_sum"):
        along = team_sum(along[:, 0]).reshape(total, 1) / DI
    query_grad, key_parts = attend_back(
        place, queries, attn_grad, attended, logs, root, key_value_rows
    )
    with jax.named_scope("keys_back"):
        key_parts = lax.all_to_all(
            key_parts.astype(BF), ("zl", "core"), split_axis=0, concat_axis=0, tiled=True
        )
        key_parts = jnp.sum(key_parts.astype(F32), axis=0).reshape(ch, count, sl * SIDE)
        if ch == 1:
            key_grad = key_parts[0]
        elif ch == 2:
            key_grad = added(
                kept(key_parts, "ch", 0), swap(given(key_parts, "ch", 0).astype(BF), "ch")
            )
        else:
            key_grad = lax.psum_scatter(
                key_parts.astype(BF), "ch", scatter_dimension=0, tiled=False
            ).astype(F32)
    out_mine, out_theirs = grad_halves(order, gathered_halves(branch_grad), branch_rows)
    along, drop_theirs, lift_part, out_theirs = together(
        along, drop_theirs, lift_part, out_theirs
    )
    with jax.named_scope("out_back"):
        out_theirs, drop_part = together(
            swap(out_theirs, "sh"), ch_part(added(drop_mine, drop_theirs))
        )
    ssm_grad, gating_grad, leaving_back = states_back(
        sl, step_pre, head, sides, mixer_rows_grad, ssm, gating, mixer_root, along, own_gain, root
    )
    with jax.named_scope("state_back"):
        entry_back = entering(piece_decay[:, 0], leaving_back, True)
    gating_rows_grad = jnp.concatenate([gating_grad, query_grad], 1)
    gating_mine, gating_theirs = grad_halves(order, gathered_halves(team_tokens), gating_rows_grad)
    entry_back, out_theirs, drop_part = together(entry_back, out_theirs, drop_part)
    inner_conv_grad, parts, step_rows_grad, sums = ssm_back(
        sl, step_pre, head, conv, sides, ssm_grad, carried, entry_back, root
    )
    parts, key_grad = together(parts, key_grad)
    with jax.named_scope("parts_exchange"):
        parts = lax.all_to_all(parts, TEAM, split_axis=0, concat_axis=0, tiled=True)
    parts, drop_part = together(parts, drop_part)
    with jax.named_scope("first_return"):
        first_back = ranks_return([gate_part, lift_part, drop_part], drows)
    with jax.named_scope("gating_back"):
        gating_theirs, out_part = together(
            swap(gating_theirs, "sh"), ch_part(added(out_mine, out_theirs))
        )
    conv_grad, conv_sums = conv_back(inner_conv_grad, parts, key_grad, conv, pre, edge)
    with jax.named_scope("follow"):
        follow = shifted(conv_grad.reshape(sl, count, LANES)[:, :EDGE], -1)
    inner_rows_grad = pre_back(conv_grad, follow, taps, root)
    inner_rows_grad, gating_theirs, out_part = together(inner_rows_grad, gating_theirs, out_part)
    inner_theirs = grad_dot(order, gathered_halves(team_tokens)[1], inner_rows_grad, BF)
    inner_mine = grad_dot(order, gathered_halves(team_tokens)[0], inner_rows_grad, F32)
    half = width // 2
    step_halves = (own_step[:, : width // 2], own_step[:, width // 2 :])
    hidden_parts = back_dot(
        order,
        [
            (inner_rows_grad, w_inner),
            (gating_rows_grad, w_gating),
            (step_rows_grad, step_halves),
        ],
    )
    with jax.named_scope("inner_back"):
        inner_theirs = swap(inner_theirs, "sh")
    with jax.named_scope("hidden_scatter"):
        hidden_parts = scatter_core(hidden_parts)
    with jax.named_scope("gating_part"):
        gating_part = ch_part(added(gating_mine, gating_theirs))
    inner_theirs, gating_part, first_back, *hidden_parts = together(
        inner_theirs, gating_part, first_back, *hidden_parts
    )
    with jax.named_scope("hidden_scatter"):
        hidden_parts = scatter_near(hidden_parts)
    with jax.named_scope("inner_part"):
        inner_part = ch_part(added(inner_mine, inner_theirs))
    inner_part, *hidden_parts = together(inner_part, *hidden_parts)
    with jax.named_scope("third_return"):
        third_back = ranks_return([out_part, gating_part, inner_part], drows).astype(F32)
    with jax.named_scope("hidden_scatter"):
        hidden_parts = scatter_last(hidden_parts)
    first_back = first_back.astype(F32)
    gate_back = first_back[:, :, :LANES]
    lift_back = first_back[:, :, LANES : 2 * LANES]
    drop_back = first_back[:, :, 2 * LANES : 3 * LANES]
    out_back = third_back[:, :, :LANES]
    gating_back = third_back[:, :, LANES : 2 * LANES]
    inner_back = third_back[:, :, 2 * LANES :]
    token_values = jnp.concatenate(own_tokens, 1)
    token_root = inverse_root(token_values.astype(F32))
    hidden_parts = [part.astype(F32) / token_root for part in hidden_parts]
    half = width // 2
    tokens_grad, _, _ = home_back(
        dims, nowhere, hidden_parts, token_values, token_root, residual_grad
    )
    tokens_out = leave(dims, home, tokens_grad, None, F32)
    layer_output = leave(dims, home, residual, layer_part, BF)
    token_left, token_right = gathered_halves(team_tokens)
    step_back = jnp.concatenate(
        [
            grad_dot(order, token_left, step_rows_grad, F32),
            grad_dot(order, token_right, step_rows_grad, F32),
        ],
        0,
    )[:, :HEADS].T

    def placed(part, extent, at):
        base = jnp.zeros(part.shape[:-1] + (extent,), F32)
        return lax.dynamic_update_slice_in_dim(base, part, at, part.ndim - 1)

    conv_all = jnp.concatenate(
        [
            placed(conv_sums[: KC + 1, :INNER], DI, rank * INNER),
            placed(conv_sums[: KC + 1, INNER:CONV], 2 * NS, rank * SIDE),
        ],
        1,
    )
    gain_all = placed(gain_part[0], DI, rank * INNER)
    step_all = step_back.reshape(HEADS, -1, drows).swapaxes(0, 1)
    step_all = step_all.reshape(sh, ch, sl, 4, HEADS * drows)
    step_all = relative(relative(step_all, "sh", 0), "ch", 1).swapaxes(1, 2)
    per_head = jnp.concatenate(
        [placed(sums[at, :HEADS], HM, rank * HEADS) for at in range(3)]
    )
    sent = jnp.concatenate(
        [
            conv_all.reshape(KC + 1, world, conv_own).swapaxes(0, 1).reshape(world, -1),
            gain_all.reshape(world, -1),
            step_all.reshape(world, -1),
            jnp.broadcast_to(per_head[None], (world, 3 * HM)),
        ],
        1,
    )
    got_all = lax.all_to_all(sent, WORLD, split_axis=0, concat_axis=0, tiled=True)
    at = KC * conv_own + conv_own + gain_own
    step_core = got_all[:, at : at + HEADS * drows].reshape(sh, sl, ch, 4, HEADS, drows)
    step_core = jnp.sum(step_core, axis=(0, 2)).reshape(HM, drows).T
    got = jnp.sum(got_all, axis=0)
    at = 0
    conv_out = got[at : at + KC * conv_own].reshape(KC, conv_own)
    at += KC * conv_own
    conv_bias_out = got[at : at + conv_own]
    at += conv_own
    gain_out = got[at : at + gain_own]
    at += gain_own + HEADS * drows
    bias_out, decay_out, skip_out = (got[at + i * HM : at + (i + 1) * HM] for i in range(3))

    def against(weight, grad):
        return jnp.sum(weight.astype(F32) * grad, axis=1)

    inner_core = to_columns(inner_back[:, :, :INNER])
    state_core = to_columns(inner_back[:, :, INNER:CONV])
    key_value_core = to_columns(inner_back[:, :, CONV:]).reshape(drows, HK, 2, 2 * SIDE)
    key_core = key_value_core[:, :, 0].reshape(drows, HK * HD)
    value_core = key_value_core[:, :, 1].reshape(drows, HK * HD)
    gating_core = to_columns(gating_back[:, :, :INNER])
    query_core = to_columns(gating_back[:, :, INNER:])
    gate_core, lift_core = to_columns(gate_back), to_columns(lift_back)
    norm_out = (
        against(gating_weight, gating_core)
        + against(inner_weight, inner_core)
        + against(state_weight, state_core)
        + against(step_weight, step_core)
        + against(query_weight, query_core)
        + against(key_weight, key_core)
        + against(value_weight, value_core)
    )
    feed_out = against(gate_matrix, gate_core) + against(lift_matrix, lift_core)
    norm_scale = norm_gain.astype(F32)[:, None]
    feed_scale = feed_gain.astype(F32)[:, None]
    mixer_out_out = out_back[:, :, :INNER].transpose(0, 2, 1).reshape(DI, drows)
    output_out = out_back[:, :, INNER:].transpose(0, 2, 1).reshape(HA * HD, drows)
    drop_out = drop_back.transpose(0, 2, 1).reshape(-1, drows)
    return (
        layer_output,
        tokens_out,
        norm_out,
        gating_core * norm_scale,
        inner_core * norm_scale,
        state_core * norm_scale,
        step_core * norm_scale,
        conv_out,
        conv_bias_out,
        gain_out,
        mixer_out_out,
        query_core * norm_scale,
        key_core * norm_scale,
        value_core * norm_scale,
        output_out,
        feed_out,
        gate_core * feed_scale,
        lift_core * feed_scale,
        drop_out,
        bias_out,
        decay_out,
        skip_out,
    )


def solution(mesh):
    seq, ctx = mesh.shape["seq"], mesh.shape["ctx"]
    fine = Mesh(mesh.devices.reshape(seq // 2, 2, ctx // 4, 2, 2), WORLD)
    lead, vector, tail = P(WORLD, None), P(WORLD), P(None, WORLD)
    in_specs = (
        lead,
        lead,
        vector,
        lead,
        lead,
        lead,
        lead,
        tail,
        vector,
        vector,
        tail,
        lead,
        lead,
        lead,
        tail,
        vector,
        lead,
        lead,
        tail,
        P(),
        P(),
        P(),
    )
    out_specs = (
        lead,
        lead,
        vector,
        lead,
        lead,
        lead,
        lead,
        tail,
        vector,
        vector,
        tail,
        lead,
        lead,
        lead,
        tail,
        vector,
        lead,
        lead,
        tail,
        P(),
        P(),
        P(),
    )
    return jax.shard_map(local, mesh=fine, in_specs=in_specs, out_specs=out_specs, check_vma=False)
```

```python
import jax
import jax.numpy as jnp
from jax import lax
from jax.experimental import pallas as pl
from jax.experimental.pallas import tpu as pltpu
from jax.sharding import Mesh
from jax.sharding import PartitionSpec as P

DI = 3072
HM = 48
PM = 64
NS = 256
KC = 4
HA = 8
HK = 2
HD = 128
FF = 4096
BLOCK = 128

epsilon = 1e-06
negative = -1e30
BF = jnp.bfloat16
F32 = jnp.float32

TEAM = ("sl", "zl", "core")
PEERS = ("sh", "ch")
WORLD = ("sh", "sl", "ch", "zl", "core")
RANKS = 8


def swap(value, axis):
    return lax.ppermute(value, axis, [(0, 1), (1, 0)])


def paired(mine, theirs, axis_name, dim):
    bit = lax.axis_index(axis_name)
    return jnp.where(bit == 0, jnp.stack([mine, theirs], dim), jnp.stack([theirs, mine], dim))


def kept(value, axis_name, dim):
    return lax.dynamic_index_in_dim(value, lax.axis_index(axis_name), dim, False)


def given(value, axis_name, dim):
    return lax.dynamic_index_in_dim(value, 1 - lax.axis_index(axis_name), dim, False)


def added(mine, theirs):
    return mine.astype(F32) + theirs.astype(F32)


def team_order():
    s, z, c = (lax.axis_index(axis) for axis in TEAM)
    blocks = [
        ((s ^ sl) * 2 + (z ^ zl)) * 2 + (c ^ core)
        for core in (0, 1)
        for zl in (0, 1)
        for sl in (0, 1)
    ]
    return jnp.stack(blocks).astype(jnp.int32)


def team_gather(left, right):
    left = jnp.stack([left, swap(left, "sl")])
    right = jnp.stack([right, swap(right, "zl")])
    left_z = swap(left, "zl")
    right_x = swap(right, "sl")
    left = jnp.concatenate([left, left_z], 0)
    right = jnp.stack([right[0], right_x[0], right[1], right_x[1]])
    return left, right, swap(left, "core"), swap(right, "core")


def scatter_core(parts):
    left, right, left_given, right_given = parts
    left_got, right_got = swap(left_given, "core"), swap(right_given, "core")
    return (
        added(left[:2], left_got[:2]),
        added(left[2:], left_got[2:]).astype(BF),
        added(right[0::2], right_got[0::2]),
        added(right[1::2], right_got[1::2]).astype(BF),
    )


def scatter_near(parts):
    left, left_given, right, right_given = parts
    left = left + swap(left_given, "zl").astype(F32)
    right = right + swap(right_given, "sl").astype(F32)
    return left[0], left[1].astype(BF), right[0], right[1].astype(BF)


def scatter_last(parts):
    left, left_given, right, right_given = parts
    return left, swap(left_given, "sl"), right, swap(right_given, "zl")


def team_scatter(parts):
    return scatter_last(scatter_near(scatter_core(parts)))


def team_sum(value):
    for axis in TEAM[::-1]:
        value = value + swap(value, axis)
    return value


def relative(value, axis_name, dim):
    if lax.axis_size(axis_name) != 2:
        return value
    return jnp.where(lax.axis_index(axis_name) == 0, value, jnp.flip(value, dim))


def together(*values):
    return lax.optimization_barrier(values)


def along_ch(part):
    size = lax.axis_size("ch")
    if size == 2:
        return jnp.concatenate([part, swap(part, "ch")], 0)
    return lax.all_gather(part, "ch", axis=0, tiled=True)


def peers_gather(parts):
    out = []
    ready = along_ch(parts[0])
    for part in parts[1:]:
        mine = ready
        theirs, ready = together(swap(mine, "sh"), along_ch(part))
        out.append((mine, theirs))
    return out + [(ready, swap(ready, "sh"))]


def ranks_exchange(pack):
    mixed = lax.all_to_all(pack, TEAM, split_axis=0, concat_axis=0, tiled=True)
    return mixed.reshape(-1, pack.shape[2])


def ch_part(part):
    size = lax.axis_size("ch")
    if size == 2:
        half = part.shape[0] // 2
        part = added(part[:half], swap(part[half:].astype(BF), "ch"))
    elif size > 2:
        part = lax.psum_scatter(part.astype(BF), "ch", scatter_dimension=0, tiled=True)
    return part.astype(BF)


def ranks_return(parts, rows):
    pack = jnp.concatenate([p.reshape(RANKS, rows, -1) for p in parts], 2)
    return lax.all_to_all(pack, TEAM, split_axis=0, concat_axis=0, tiled=True)


def by_rank(weight):
    rows = weight.shape[0]
    return weight.reshape(rows, RANKS, -1).transpose(1, 0, 2)


def to_columns(pieces):
    return pieces.transpose(1, 0, 2).reshape(pieces.shape[1], -1)


def column_blocks(sh, sl, ch):
    place = lax.axis_index("sh")
    if ch == 2:
        place = place * 2 + lax.axis_index("ch")
    return place.astype(jnp.int32).reshape(1)


def shifted(value, steps):
    count = lax.axis_size("ch")
    if count == 1:
        return jnp.zeros_like(value)
    leading, last = max(0, -steps), min(count, count - steps)
    return lax.ppermute(value, "ch", [(at, at + steps) for at in range(leading, last)])


def entering(decay, state, reverse):
    count = lax.axis_size("ch")
    if count == 1:
        return jnp.zeros_like(state)
    if count == 2:
        return shifted(state, -1 if reverse else 1)
    place = lax.axis_index("ch")
    ahead = count - 1 - place if reverse else place
    decays = lax.all_gather(decay, "ch")
    states = lax.all_gather(state, "ch")

    def one(step, run):
        source = count - 1 - step if reverse else step
        factor = lax.dynamic_index_in_dim(decays, source, 0, False)
        return factor[:, None] * run + lax.dynamic_index_in_dim(states, source, 0, False).astype(
            F32
        )

    return lax.fori_loop(0, ahead, one, jnp.zeros(state.shape, F32)).astype(state.dtype)


def inverse_root(values):
    return lax.rsqrt(jnp.mean(values * values, axis=-1, keepdims=True) + epsilon)


def norm_back(values, scaled, upstream):
    normed = values * scaled
    return scaled * (upstream - normed * jnp.mean(upstream * normed, axis=-1, keepdims=True))


def silu_value(values):
    return values * jax.nn.sigmoid(values)


def silu_slope(values):
    sigmoid_part = jax.nn.sigmoid(values)
    return sigmoid_part * (1.0 + values * (1.0 - sigmoid_part))


def dot(operand, against, at, precision=None):
    return lax.dot_general(
        operand, against, (((at[0],), (at[1],)), ((), ())), precision=precision, preferred_element_type=F32
    )


def exact(operand, against, at):
    return dot(operand, against, at, lax.Precision.HIGHEST)


TILE = 2 * BLOCK
EDGE = 16
LANES = 512
INNER = DI // RANKS
HEADS = HM // RANKS
SIDE = 2 * NS // RANKS
CONV = INNER + SIDE


def call(cost, kernel, grid, in_specs, out_specs, out_shape, scratch=(), scalars=0):
    return pl.pallas_call(
        kernel,
        grid_spec=pltpu.PrefetchScalarGridSpec(
            num_scalar_prefetch=scalars,
            grid=grid,
            in_specs=in_specs,
            out_specs=out_specs,
            scratch_shapes=list(scratch),
        ),
        out_shape=out_shape,
        compiler_params=pltpu.CompilerParams(vmem_limit_bytes=48 * 1024 * 1024),
        cost_estimate=pl.CostEstimate(flops=int(cost * 10**9), bytes_accessed=10**6, transcendentals=0),
    )


def shape(dims, dtype=F32):
    return jax.ShapeDtypeStruct(dims, dtype)


def full(array):
    return pl.BlockSpec(array.shape, lambda *at: (0,) * array.ndim)


def tiled(width, rows=TILE):
    return pl.BlockSpec((rows, width), lambda i, *at: (i, 0))


def place_rows(scalars, gathered, rows):
    left, right, left_other, right_other = gathered
    half = left.shape[2]
    own = pl.multiple_of(scalars[0] * BLOCK, BLOCK)
    other = pl.multiple_of((1 - scalars[0]) * BLOCK, BLOCK)
    rows[pl.ds(own, BLOCK), :half] = left[0]
    rows[pl.ds(own, BLOCK), half:] = right[0]
    rows[pl.ds(other, BLOCK), :half] = left_other[0]
    rows[pl.ds(other, BLOCK), half:] = right_other[0]


def gathered_specs(gathered):
    spec = pl.BlockSpec((1, BLOCK, gathered[0].shape[2]), lambda i, s: (s[1 + i], 0, 0))
    return [spec] * 4


def halves_product(rows, mine, theirs):
    half = mine.shape[0]
    return dot(rows[:, :half], mine[...], (1, 0)) + dot(rows[:, half:], theirs[...], (1, 0))


def row_root(rows):
    values = rows.astype(F32)
    return lax.rsqrt(jnp.mean(values * values, axis=-1, keepdims=True) + epsilon)


def natural_blocks(dims):
    sh, sl, ch, width = dims
    block = width // (sh * sl * ch)
    return [
        (((a * sl + b) * ch + c) * block, ((a * ch + c) * sl + b) * block, block)
        for a in range(sh)
        for b in range(sl)
        for c in range(ch)
    ]


def related(place, start, dims):
    sh, _, ch, width = dims
    unit = width // (sh * ch) if ch == 2 else width // sh
    return pl.multiple_of(lax.bitwise_xor(place, start // unit) * unit + start % unit, 128)


def related_blocks(dims):
    sh, _, ch, width = dims
    unit = width // (sh * ch) if ch == 2 else width // sh
    return range(0, width, unit), unit


def whole_blocks(width):
    return pl.BlockSpec((BLOCK, width), lambda i, s: (0, 0))


def shuffle_kernel(dims, place, rows, out_refs, scratch):
    width = dims[3]
    for natural, start, block in natural_blocks(dims):
        scratch[:, start : start + block] = rows[:, natural : natural + block].astype(F32)
    starts, unit = related_blocks(dims)
    for start in starts:
        at = related(place, start, dims)
        out = out_refs[start // (width // 2)]
        inside = start % (width // 2)
        out[:, inside : inside + unit] = scratch[:, pl.ds(at, unit)].astype(BF)


def arrive_kernel(dims, place, tokens, cotangent, tl, tr, whole, scratch):
    half = dims[3] // 2
    shuffle_kernel(dims, place[0], tokens, (tl, tr), scratch)
    shuffle_kernel(dims, place[0], cotangent, (whole.at[:, :half], whole.at[:, half:]), scratch)


def arrive(dims, place, tokens, cotangent):
    width = dims[3]
    half = shape((BLOCK, width // 2), BF)
    return call(
        2,
        lambda *refs: arrive_kernel(dims, *refs),
        (1,),
        [whole_blocks(width)] * 2,
        [whole_blocks(width // 2)] * 2 + [whole_blocks(width)],
        [half] * 2 + [shape((BLOCK, width), BF)],
        [pltpu.VMEM((BLOCK, width), F32)],
        1,
    )(place, tokens, cotangent)


def leave_kernel(dims, added_to, place, rows, *refs):
    out, scratch = refs[-2], refs[-1]
    values = rows[...].astype(F32)
    if added_to:
        values = values + refs[0][...].astype(F32)
    scratch[...] = values
    sh, _, ch, width = dims
    unit = related_blocks(dims)[1]
    for natural, start, block in natural_blocks(dims):
        at = pl.multiple_of(related(place[0], start // unit * unit, dims), 128)
        if block % 128 == 0:
            got = scratch[:, pl.ds(pl.multiple_of(at + start % unit, 128), block)]
        else:
            got = scratch[:, pl.ds(at, unit)][:, start % unit : start % unit + block]
        out[:, natural : natural + block] = got.astype(out.dtype)


def leave(dims, place, rows, ordered, dtype):
    width = dims[3]
    ins = [rows] if ordered is None else [rows, ordered]
    return call(
        1.5,
        lambda *refs: leave_kernel(dims, ordered is not None, *refs),
        (1,),
        [whole_blocks(width)] * len(ins),
        whole_blocks(width),
        shape((BLOCK, width), dtype),
        [pltpu.VMEM((BLOCK, width), F32)],
        1,
    )(place, *ins)


def home_forward_kernel(dims, place, left, left_rest, right, right_rest, tl, tr, residual_ref, root_ref, l_ref, r_ref):
    half = left.shape[1]
    a = tl[...].astype(F32) + left[...] + left_rest[...].astype(F32)
    b = tr[...].astype(F32) + right[...] + right_rest[...].astype(F32)
    square = jnp.sum(a * a, axis=-1, keepdims=True) + jnp.sum(b * b, axis=-1, keepdims=True)
    root = lax.rsqrt(square / (2 * half) + epsilon)
    residual_ref[:, :half] = a
    residual_ref[:, half:] = b
    root_ref[...] = root
    starts, unit = related_blocks(dims)
    for start in starts:
        out, inside = (l_ref, start) if start < half else (r_ref, start - half)
        rows = residual_ref[:, pl.ds(related(place[0], start, dims), unit)]
        out[:, inside : inside + unit] = (rows * root).astype(BF)


def home_forward(dims, place, parts, tokens):
    half = dims[3] // 2
    return call(
        1.4,
        lambda *refs: home_forward_kernel(dims, *refs),
        (1,),
        [whole_blocks(half)] * 6,
        [whole_blocks(2 * half), whole_blocks(1), whole_blocks(half), whole_blocks(half)],
        [
            shape((BLOCK, 2 * half)),
            shape((BLOCK, 1)),
            shape((BLOCK, half), BF),
            shape((BLOCK, half), BF),
        ],
        (),
        1,
    )(place, *parts, *tokens)


def home_back_kernel(dims, place, left, left_rest, right, right_rest, values, root, base, grad_ref, l_ref, r_ref, scratch):
    half = left.shape[1]
    width = 2 * half
    scaled = root[...]
    scratch[:, :half] = left[...] + left_rest[...].astype(F32)
    scratch[:, half:] = right[...] + right_rest[...].astype(F32)
    starts, unit = related_blocks(dims)
    mean = jnp.zeros_like(scaled)
    for start in starts:
        norm = values[:, pl.ds(related(place[0], start, dims), unit)].astype(F32) * scaled
        up = scratch[:, start : start + unit]
        mean = mean + jnp.sum(up * norm, axis=-1, keepdims=True)
    mean = mean / width
    for start in starts:
        at = related(place[0], start, dims)
        norm = values[:, pl.ds(at, unit)].astype(F32) * scaled
        up = scratch[:, start : start + unit]
        grad_ref[:, pl.ds(at, unit)] = base[:, pl.ds(at, unit)].astype(F32) + scaled * (
            up - norm * mean
        )
    l_ref[...] = grad_ref[:, :half].astype(BF)
    r_ref[...] = grad_ref[:, half:].astype(BF)


def home_back(dims, place, parts, values, root, base):
    half = dims[3] // 2
    return call(
        1.6,
        lambda *refs: home_back_kernel(dims, *refs),
        (1,),
        [whole_blocks(half)] * 4 + [whole_blocks(2 * half), whole_blocks(1), whole_blocks(2 * half)],
        [whole_blocks(2 * half), whole_blocks(half), whole_blocks(half)],
        [shape((BLOCK, 2 * half)), shape((BLOCK, half), BF), shape((BLOCK, half), BF)],
        [pltpu.VMEM((BLOCK, 2 * half), F32)],
        1,
    )(place, *parts, values, root, base)


def project_inner_kernel(tiles, scalars, l, r, lo, ro, mine, theirs, halo, taps, steps, pre_ref, conv_ref, side_ref, keys_ref, step_ref, root_ref, edge_ref, rows, line):
    i = pl.program_id(0)
    place_rows(scalars, (l, r, lo, ro), rows)
    values = rows[...]
    root = row_root(values)
    root_ref[...] = root
    pre = halves_product(values, mine, theirs) * root
    pre_ref[...] = pre
    step_ref[...] = dot(values, steps[...], (1, 1)) * root

    @pl.when(i % tiles == 0)
    def _():
        before = halo[0]
        edge = halves_product(before, mine, theirs) * row_root(before)
        edge_ref[0] = edge
        line[:EDGE] = edge

    @pl.when(i % tiles != 0)
    def _():
        line[:EDGE] = line[TILE:]

    line[EDGE:] = pre
    conv = taps[KC : KC + 1, :]
    for k in range(KC):
        conv = conv + taps[k : k + 1, :] * line[EDGE - (KC - 1) + k : EDGE - (KC - 1) + k + TILE, :]
    conv_ref[...] = conv
    side_ref[...] = silu_value(conv[:, INNER:CONV]).astype(BF)
    keys_ref[...] = pre[:, CONV:].astype(BF)


def project_inner(scalars, gathered, weight, halo, taps, steps):
    seqs = halo.shape[0]
    total = 2 * 4 * BLOCK
    tiles = total // TILE // seqs
    width = 2 * gathered[0].shape[2]
    return call(
        10.4,
        lambda *refs: project_inner_kernel(tiles, *refs),
        (total // TILE,),
        gathered_specs(gathered)
        + [full(weight[0]), full(weight[1])]
        + [pl.BlockSpec((1, EDGE, width), lambda i, s: (i // tiles, 0, 0)), full(taps), full(steps)],
        [
            tiled(LANES),
            tiled(LANES),
            tiled(SIDE),
            tiled(SIDE),
            tiled(8),
            tiled(1),
            pl.BlockSpec((1, EDGE, LANES), lambda i, s: (i // tiles, 0, 0)),
        ],
        [
            shape((total, LANES)),
            shape((total, LANES)),
            shape((total, SIDE), BF),
            shape((total, SIDE), BF),
            shape((total, 8)),
            shape((total, 1)),
            shape((seqs, EDGE, LANES)),
        ],
        [pltpu.VMEM((TILE, width), BF), pltpu.VMEM((EDGE + TILE, LANES), F32)],
        1,
    )(scalars, *gathered, *weight, halo, taps, steps)


def project_gating_kernel(scalars, l, r, lo, ro, mine, theirs, root, gating_ref, query_ref, rows):
    place_rows(scalars, (l, r, lo, ro), rows)
    product = halves_product(rows[...], mine, theirs) * root[...]
    gating_ref[...] = product[:, :INNER]
    query_ref[...] = product[:, INNER:].astype(BF)


def project_gating(scalars, gathered, weight, root):
    total, width = root.shape[0], 2 * gathered[0].shape[2]
    return call(
        6.2,
        project_gating_kernel,
        (total // TILE,),
        gathered_specs(gathered) + [full(weight[0]), full(weight[1]), tiled(1)],
        [tiled(INNER), tiled(HD)],
        [shape((total, INNER)), shape((total, HD), BF)],
        [pltpu.VMEM((TILE, width), BF)],
        1,
    )(scalars, *gathered, *weight, root)


def rows_back_kernel(scalars, l, r, lo, ro, mine, theirs, ssm, gating, root, gain, mixer_ref, attn_ref, along_ref, gain_ref, rows):
    place_rows(scalars, (l, r, lo, ro), rows)
    product = halves_product(rows[...], mine, theirs)
    mixer = product[:, :INNER]
    mixer_ref[...] = mixer
    attn_ref[...] = product[:, INNER:].astype(BF)
    norm = ssm[...] * silu_value(gating[...]) * root[...]
    together = mixer * norm
    along_ref[0] = exact(jnp.ones((8, INNER), F32), together * gain[...], (1, 1))

    @pl.when(pl.program_id(0) == 0)
    def _():
        gain_ref[...] = jnp.zeros_like(gain_ref)

    gain_ref[...] += jnp.sum(together, axis=0, keepdims=True)


def rows_back(scalars, gathered, weight, ssm, gating, root, gain):
    total, width = root.shape[0], 2 * gathered[0].shape[2]
    tiles = total // TILE
    return call(
        9.1,
        rows_back_kernel,
        (tiles,),
        gathered_specs(gathered)
        + [full(weight[0]), full(weight[1]), tiled(INNER), tiled(INNER), tiled(1), full(gain)],
        [
            tiled(INNER),
            tiled(HD),
            pl.BlockSpec((1, 8, TILE), lambda i, s: (i, 0, 0)),
            pl.BlockSpec((1, INNER), lambda i, s: (0, 0)),
        ],
        [
            shape((total, INNER)),
            shape((total, HD), BF),
            shape((tiles, 8, TILE)),
            shape((1, INNER)),
        ],
        [pltpu.VMEM((TILE, width), BF)],
        1,
    )(scalars, *gathered, *weight, ssm, gating, root, gain)


def back_dot_kernel(terms, halves, scalars, *refs):
    ins, outs = refs[: terms * 4], refs[terms * 4 :]
    i = pl.program_id(0)
    for half in range(2):
        product = None
        for t in range(terms):
            first, second = ins[4 * t], ins[4 * t + 1]
            weight = ins[4 * t + 2 + half]
            rows = jnp.concatenate([first[...], second[...]], 0)
            at = (1, 1) if weight.shape[1] == rows.shape[1] else (1, 0)
            one = dot(rows, weight[...], at)
            product = one if product is None else product + one
        product = product.reshape(outs[half].shape)

        @pl.when(i < halves)
        def _():
            outs[2 + half][...] = product.astype(BF)

        @pl.when(i >= halves)
        def _():
            outs[half][...] = product


def back_dot(order, terms):
    total = terms[0][0].shape[0]
    half = terms[0][1][0].shape[0]
    halves = total // TILE // 2
    specs, arrays = [], []
    for rows, weights in terms:
        width = rows.shape[1]
        specs += [
            pl.BlockSpec((BLOCK, width), lambda i, s: (s[(2 * i + 4) % 8], 0)),
            pl.BlockSpec((BLOCK, width), lambda i, s: (s[(2 * i + 5) % 8], 0)),
            full(weights[0]),
            full(weights[1]),
        ]
        arrays += [rows, rows, *weights]
    kept_spec = pl.BlockSpec((2, BLOCK, half), lambda i, s: (jnp.maximum(i - halves, 0), 0, 0))
    given_spec = pl.BlockSpec((2, BLOCK, half), lambda i, s: (jnp.minimum(i, halves - 1), 0, 0))
    blocks = total // BLOCK // 2
    return call(
        3 + 3 * len(terms),
        lambda *refs: back_dot_kernel(len(terms), halves, *refs),
        (2 * halves,),
        specs,
        [kept_spec, kept_spec, given_spec, given_spec],
        [shape((blocks, BLOCK, half))] * 2 + [shape((blocks, BLOCK, half), BF)] * 2,
        (),
        1,
    )(order, *arrays)


def grad_dot_kernel(scalars, own, other, against, *refs):
    out, ordered = refs[-2], refs[-1]

    @pl.when(pl.program_id(0) == 0)
    def _():
        for k in range(8):
            start = pl.multiple_of(scalars[k] * BLOCK, BLOCK)
            ordered[k * BLOCK : (k + 1) * BLOCK] = against[pl.ds(start, BLOCK), :]

    tile = own.shape[2]
    rows = own.shape[0] * own.shape[1]
    product = dot(own[...].reshape(rows, tile), ordered[:rows], (0, 0))
    product = product + dot(other[...].reshape(rows, tile), ordered[rows:], (0, 0))
    out[...] = product.astype(out.dtype)


def grad_dot(order, parts, against, dtype):
    total, width = against.shape
    blocks = total // BLOCK // 2
    tile = 512
    half = parts[0][3]
    specs = [
        pl.BlockSpec((blocks, BLOCK, tile), lambda i, s, at=at, off=off: (at, 0, i + off // tile))
        for _, at, off, _ in parts
    ]
    return call(
        3.1,
        grad_dot_kernel,
        (half // tile,),
        [*specs, full(against)],
        pl.BlockSpec((tile, width), lambda i, s: (i, 0)),
        shape((half, width), dtype),
        [pltpu.VMEM((total, width), BF)],
        1,
    )(order, *(array for array, _, _, _ in parts), against)


def gathered_halves(gathered):
    left, right, left_other, right_other = gathered
    half = left.shape[2]
    return [(left, 0, 0, half), (left_other, 0, 0, half)], [
        (right, 0, 0, half),
        (right_other, 0, 0, half),
    ]


def straight_halves(rows):
    total, width = rows.shape
    rows = rows.reshape(total // BLOCK, BLOCK, width)
    half = width // 2
    return [(rows, 0, 0, half), (rows, 1, 0, half)], [(rows, 0, half, half), (rows, 1, half, half)]


def feed_grads_kernel(order, l, r, lo, ro, cotangent, active, gate, lift, *refs):
    mine, theirs, (gate_rows, lift_rows) = refs[:3], refs[3:6], refs[6:]
    i = pl.program_id(0)

    @pl.when(i == 0)
    def _():
        for k in range(8):
            start = pl.multiple_of(order[k] * BLOCK, BLOCK)
            gate_rows[k * BLOCK : (k + 1) * BLOCK] = gate[pl.ds(start, BLOCK), :]
            lift_rows[k * BLOCK : (k + 1) * BLOCK] = lift[pl.ds(start, BLOCK), :]

    def run(own, other, out):
        tile = own.shape[2]
        rows = own.shape[0] * own.shape[1]
        own, other = own[...].reshape(rows, tile), other[...].reshape(rows, tile)
        for at, against in ((0, gate_rows), (1, lift_rows)):
            product = dot(own, against[:rows], (0, 0)) + dot(other, against[rows:], (0, 0))
            out[at][...] = product.astype(BF)
        out[2][...] = dot(cotangent[...], active[...], (0, 0)).astype(BF)

    @pl.when(i < pl.num_programs(0) // 2)
    def _():
        run(r, ro, theirs)

    @pl.when(i >= pl.num_programs(0) // 2)
    def _():
        run(l, lo, mine)


def feed_grads(order, gathered, cotangent, active, gate, lift):
    total, width = cotangent.shape
    tile = 512
    tiles = width // tile
    half = tiles // 2
    dims = gathered[0].shape[:2] + (tile,)
    right = pl.BlockSpec(dims, lambda i, s: (0, 0, jnp.minimum(i, half - 1)))
    left = pl.BlockSpec(dims, lambda i, s: (0, 0, jnp.maximum(i - half, 0)))
    return call(
        13,
        feed_grads_kernel,
        (tiles,),
        [left, right, left, right, pl.BlockSpec((total, tile), lambda i, s: (0, (i + half) % tiles))]
        + [full(x) for x in (active, gate, lift)],
        [
            *[pl.BlockSpec((tile, LANES), lambda i, s: (jnp.maximum(i - half, 0), 0))] * 3,
            *[pl.BlockSpec((tile, LANES), lambda i, s: (jnp.minimum(i, half - 1), 0))] * 3,
        ],
        [shape((width // 2, LANES), BF)] * 6,
        [pltpu.VMEM((total, LANES), BF)] * 2,
        1,
    )(order, *gathered, cotangent, active, gate, lift)


def grad_halves(order, halves, against):
    theirs = grad_dot(order, halves[1], against, BF)
    return grad_dot(order, halves[0], against, F32), theirs


def feed_kernel(scalars, l, r, lo, ro, cotangent, gm, gt, lm, lt, dm, dt, active_ref, gate_ref, lift_ref, rows):
    place_rows(scalars, (l, r, lo, ro), rows)
    values = rows[...]
    gate = halves_product(values, gm, gt)
    lift = halves_product(values, lm, lt)
    grad = halves_product(cotangent[...], dm, dt)
    sigmoid_part = jax.nn.sigmoid(gate)
    swish = gate * sigmoid_part
    active_ref[...] = (swish * lift).astype(BF)
    gate_ref[...] = (grad * lift * sigmoid_part * (1.0 + gate * (1.0 - sigmoid_part))).astype(BF)
    lift_ref[...] = (grad * swish).astype(BF)


def feed_block(scalars, gathered, cotangent, gate, lift, drop):
    total, width = cotangent.shape
    weights = [*gate, *lift, *drop]
    return call(
        11.8,
        feed_kernel,
        (total // TILE,),
        gathered_specs(gathered) + [tiled(width)] + [full(w) for w in weights],
        [tiled(LANES)] * 3,
        [shape((total, LANES), BF)] * 3,
        [pltpu.VMEM((TILE, width), BF)],
        1,
    )(scalars, *gathered, cotangent, *weights)


def forth_dot_kernel(rows, mine, theirs, out):
    half = mine.shape[0]
    out[:, :half] = dot(rows[...], mine[...], (1, 1)).astype(BF)
    out[:, half:] = dot(rows[...], theirs[...], (1, 1)).astype(BF)


def forth_dot(rows, weights):
    total, k = rows.shape
    width = 2 * weights[0].shape[0]
    return call(
        4.4,
        forth_dot_kernel,
        (total // TILE,),
        [tiled(k), full(weights[0]), full(weights[1])],
        tiled(width),
        shape((total, width), BF),
    )(rows, *weights)


def keys_kernel(seqs, parts, out):
    for n in range(seqs):
        out[n] = jnp.concatenate([parts[r][:, n * SIDE : (n + 1) * SIDE] for r in range(4)], 1)


def keys_of(seqs, parts):
    count = parts.shape[1]
    return call(
        1.7,
        lambda *refs: keys_kernel(seqs, *refs),
        (count // TILE,),
        [pl.BlockSpec((4, TILE, seqs * SIDE), lambda i: (0, i, 0))],
        pl.BlockSpec((seqs, TILE, 2 * HD), lambda i: (0, i, 0)),
        shape((seqs, count, 2 * HD), BF),
    )(parts)


def scores_of(place, queries, keys):
    count, whole = queries.shape[0], keys.shape[0]
    scores = dot(queries, keys, (1, 1)) * HD**-0.5
    row = place + pl.program_id(1) * count + lax.broadcasted_iota(jnp.int32, (count, whole), 0)
    column = lax.broadcasted_iota(jnp.int32, (count, whole), 1)
    return scores, row >= column


def attend_kernel(place, queries, key_value, out_ref, log_ref):
    keys, values = key_value[0, :, :HD], key_value[0, :, HD:]
    scores, visible = scores_of(place[0], queries[...], keys)
    scores = jnp.where(visible, scores, negative)
    top = jnp.max(scores, axis=-1, keepdims=True)
    weights = jnp.exp(scores - top)
    total = jnp.sum(weights, axis=-1, keepdims=True)
    log_ref[...] = top + jnp.log(total)
    out_ref[...] = dot(weights.astype(BF), values, (1, 0)) / total


def attend_specs(seqs, total):
    tiles = total // TILE // seqs
    rows = lambda width: pl.BlockSpec((TILE, width), lambda n, i, s: (n * tiles + i, 0))
    return (seqs, tiles), rows


def attend(place, queries, key_value):
    seqs, whole, width = key_value.shape
    total = queries.shape[0]
    grid, rows = attend_specs(seqs, total)
    return call(
        2.8,
        attend_kernel,
        grid,
        [rows(HD), pl.BlockSpec((1, whole, width), lambda n, i, s: (n, 0, 0))],
        [rows(HD), rows(1)],
        [shape((total, HD)), shape((total, 1))],
        (),
        1,
    )(place, queries, key_value)


def attend_back_kernel(place, queries, grads, attended, logs, root, key_value, query_ref, sum_ref):
    keys, values = key_value[0, :, :HD], key_value[0, :, HD:]
    scores, visible = scores_of(place[0], queries[...], keys)
    probs = jnp.where(visible, jnp.exp(scores - logs[...]), 0.0)
    grad = grads[...]
    delta = jnp.sum(grad.astype(F32) * attended[...], axis=-1, keepdims=True)
    scores_grad = (probs * (dot(grad, values, (1, 1)) - delta)).astype(BF)
    query_ref[...] = (dot(scores_grad, keys, (1, 0)) * (HD**-0.5 * root[...])).astype(BF)

    @pl.when((pl.program_id(0) == 0) & (pl.program_id(1) == 0))
    def _():
        sum_ref[...] = jnp.zeros_like(sum_ref)

    key_sum = dot(scores_grad, queries[...], (0, 0)) * HD**-0.5
    value_sum = dot(probs.astype(BF), grad, (0, 0))
    for n in range(sum_ref.shape[2] // SIDE):

        @pl.when(pl.program_id(0) == n)
        def _():
            at = slice(n * SIDE, (n + 1) * SIDE)
            sum_ref[0, :, at] += key_sum[:, :SIDE]
            sum_ref[1, :, at] += key_sum[:, SIDE:]
            sum_ref[2, :, at] += value_sum[:, :SIDE]
            sum_ref[3, :, at] += value_sum[:, SIDE:]


def attend_back(place, queries, grads, attended, logs, root, key_value):
    seqs, whole, width = key_value.shape
    total = queries.shape[0]
    grid, rows = attend_specs(seqs, total)
    sums = pl.BlockSpec((1, whole, width), lambda n, i, s: (n, 0, 0))
    return call(
        6.4,
        attend_back_kernel,
        grid,
        [rows(HD), rows(HD), rows(HD), rows(1), rows(1), sums],
        [rows(HD), pl.BlockSpec((4, whole, seqs * SIDE), lambda n, i, s: (0, 0, 0))],
        [shape((total, HD), BF), shape((4, whole, seqs * SIDE))],
        (),
        1,
    )(place, queries, grads, attended, logs, root, key_value)


def over_heads(values):
    rows = values.shape[0]
    return jnp.concatenate(
        [jnp.broadcast_to(values[:, h : h + 1], (rows, PM)) for h in range(HEADS)], 1
    )


def head_sums(values):
    channel = lax.broadcasted_iota(jnp.int32, (INNER, 8), 0)
    head = lax.broadcasted_iota(jnp.int32, (INNER, 8), 1)
    return exact(values, jnp.where(channel // PM == head, 1.0, 0.0), (1, 0))


def triangle():
    row = lax.broadcasted_iota(jnp.int32, (BLOCK, BLOCK), 0)
    column = lax.broadcasted_iota(jnp.int32, (BLOCK, BLOCK), 1)
    return row, column


def block_steps(step_pre, head):
    arg = step_pre + head[0:1, :]
    size = jnp.maximum(arg, 0.0) + jnp.log1p(jnp.exp(-jnp.abs(arg)))
    row, column = triangle()
    cum = exact(jnp.where(row >= column, 1.0, 0.0), size * head[1:2, :], (1, 0))
    return arg, size, cum


def as_rows(values):
    row, column = triangle()
    return exact(values, jnp.where(row == column, 1.0, 0.0), (0, 0))


def as_columns(values):
    row, column = triangle()
    return exact(jnp.where(row == column, 1.0, 0.0), values, (1, 1))


def joined(sides, first, n):
    return jnp.concatenate(
        [sides[r][:, n * SIDE : (n + 1) * SIDE] for r in range(first, first + 4)], 1
    )


def pair(seqs, width, back=0):
    if back:
        return pl.BlockSpec((seqs, BLOCK, width), lambda i, *s: (0, back - 1 - i, 0))
    return pl.BlockSpec((seqs, BLOCK, width), lambda i, *s: (0, i, 0))


def by_seq(seqs, *arrays):
    return [a.reshape(*a.shape[:-2], seqs, -1, a.shape[-1]) for a in arrays]


def states_kernel(seqs, blocks, step_pre, head, conv, sides, out_ref, decay_ref, run):
    i = pl.program_id(0)

    @pl.when(i == 0)
    def _():
        run[...] = jnp.zeros_like(run)
        decay_ref[...] = jnp.ones_like(decay_ref)

    for n in range(seqs):
        _, size, cum = block_steps(step_pre[n], head)
        last = cum[BLOCK - 1 :, :]
        feeding = jnp.exp(last - cum) * size
        inner = silu_value(conv[n, :, :INNER])
        in_state = joined(sides, 0, n)
        fresh = dot(in_state, (over_heads(feeding) * inner).astype(BF), (0, 0))
        decay = over_heads(jnp.exp(last))
        run[n] = decay * run[n] + fresh
        decay_ref[n] = decay_ref[n] * decay

    @pl.when(i == blocks - 1)
    def _():
        out_ref[...] = run[...].astype(BF)


def states(seqs, step_pre, head, conv, sides):
    step_pre, conv = by_seq(seqs, step_pre, conv)
    blocks = conv.shape[1] // BLOCK
    return call(
        4.2,
        lambda *refs: states_kernel(seqs, blocks, *refs),
        (blocks,),
        [
            pair(seqs, 8),
            full(head),
            pair(seqs, LANES),
            pl.BlockSpec((4, BLOCK, seqs * SIDE), lambda i: (0, i, 0)),
        ],
        [
            pl.BlockSpec((seqs, NS, INNER), lambda i: (0, 0, 0)),
            pl.BlockSpec((seqs, 1, INNER), lambda i: (0, 0, 0)),
        ],
        [shape((seqs, NS, INNER), BF), shape((seqs, 1, INNER))],
        [pltpu.VMEM((seqs, NS, INNER), F32)],
    )(step_pre, head, conv, sides)


def fading_of(cum, cum_rows, h):
    row, column = triangle()
    span = cum[:, h : h + 1] - cum_rows[h : h + 1, :]
    return jnp.where(row >= column, jnp.exp(jnp.minimum(span, 0.0)), 0.0)


def ssm_kernel(seqs, step_pre, head, conv, sides, gating, entry, ssm_ref, carried_ref, square_ref, run):
    @pl.when(pl.program_id(0) == 0)
    def _():
        run[...] = entry[...].astype(F32)

    for n in range(seqs):
        _, size, cum = block_steps(step_pre[n], head)
        size_rows, cum_rows = as_rows(size), as_rows(cum)
        last = cum[BLOCK - 1 :, :]
        inner = silu_value(conv[n, :, :INNER])
        inner_low = inner.astype(BF)
        in_state, out_state = joined(sides, 0, n), joined(sides, 4, n)
        before = run[n]
        carried = before.astype(BF)
        carried_ref[n, 0] = carried
        pairing = dot(out_state, in_state, (1, 1))
        within = []
        for h in range(HEADS):
            mixing = fading_of(cum, cum_rows, h) * pairing * size_rows[h : h + 1, :]
            within.append(dot(mixing.astype(BF), inner_low[:, h * PM : (h + 1) * PM], (1, 0)))
        readout = dot(out_state, carried, (1, 0))
        ssm = (
            jnp.concatenate(within, 1)
            + over_heads(jnp.exp(cum)) * readout
            + over_heads(head[2:3, :]) * inner
        )
        ssm_ref[n] = ssm
        gated = ssm * silu_value(gating[n])
        square_ref[0, n] = exact(jnp.ones((8, INNER), F32), gated * gated, (1, 1))
        feeding = jnp.exp(last - cum) * size
        fresh = dot(in_state, (over_heads(feeding) * inner).astype(BF), (0, 0))
        run[n] = over_heads(jnp.exp(last)) * before + fresh


def ssm_block(seqs, step_pre, head, conv, sides, gating, entry):
    total = conv.shape[0]
    step_pre, conv, gating = by_seq(seqs, step_pre, conv, gating)
    count = conv.shape[1]
    blocks = count // BLOCK
    ssm, carried, square = call(
        10.8,
        lambda *refs: ssm_kernel(seqs, *refs),
        (blocks,),
        [
            pair(seqs, 8),
            full(head),
            pair(seqs, LANES),
            pl.BlockSpec((RANKS, BLOCK, seqs * SIDE), lambda i: (0, i, 0)),
            pair(seqs, INNER),
            full(entry),
        ],
        [
            pair(seqs, INNER),
            pl.BlockSpec((seqs, 1, NS, INNER), lambda i: (0, i, 0, 0)),
            pl.BlockSpec((1, seqs, 8, BLOCK), lambda i: (i, 0, 0, 0)),
        ],
        [
            shape((seqs, count, INNER)),
            shape((seqs, blocks, NS, INNER), BF),
            shape((blocks, seqs, 8, BLOCK)),
        ],
        [pltpu.VMEM((seqs, NS, INNER), F32)],
    )(step_pre, head, conv, sides, gating, entry)
    square = square[:, :, 0].swapaxes(0, 1).reshape(total // BLOCK, BLOCK)
    return ssm.reshape(total, INNER), carried, square


def states_back_kernel(seqs, blocks, step_pre, head, sides, mixer, ssm, gating, mixer_root, along, gain, root, grad_ref, gating_ref, out_ref, run):
    i = pl.program_id(0)

    @pl.when(i == 0)
    def _():
        run[...] = jnp.zeros_like(run)

    for n in range(seqs):
        _, _, cum = block_steps(step_pre[n], head)
        gate = gating[n]
        sigmoid_part = jax.nn.sigmoid(gate)
        act = gate * sigmoid_part
        values = ssm[n]
        scaled = mixer_root[n]
        norm = values * act * scaled
        gated_grad = scaled * (mixer[n] * gain[...] - norm * along[n])
        grad = gated_grad * act
        grad_ref[n] = grad
        slope = sigmoid_part * (1.0 + gate * (1.0 - sigmoid_part))
        gating_ref[n] = (gated_grad * values * slope * root[n]).astype(BF)
        grown = (over_heads(jnp.exp(cum)) * grad).astype(BF)
        fresh = dot(joined(sides, 0, n), grown, (0, 0))
        run[n] = over_heads(jnp.exp(cum[BLOCK - 1 :, :])) * run[n] + fresh

    @pl.when(i == blocks - 1)
    def _():
        out_ref[...] = run[...].astype(BF)


def states_back(seqs, step_pre, head, sides, mixer, ssm, gating, mixer_root, along, gain, root):
    total = ssm.shape[0]
    step_pre, mixer, ssm, gating, mixer_root, along, root = by_seq(
        seqs, step_pre, mixer, ssm, gating, mixer_root, along, root
    )
    count = ssm.shape[1]
    blocks = count // BLOCK
    back = lambda width: pair(seqs, width, blocks)
    grad, gating_grad, leaving = call(
        5.7,
        lambda *refs: states_back_kernel(seqs, blocks, *refs),
        (blocks,),
        [back(8), full(head)]
        + [pl.BlockSpec((4, BLOCK, seqs * SIDE), lambda i: (1, blocks - 1 - i, 0))]
        + [back(INNER), back(INNER), back(INNER), back(1), back(1), full(gain), back(1)],
        [back(INNER), back(INNER), pl.BlockSpec((seqs, NS, INNER), lambda i: (0, 0, 0))],
        [
            shape((seqs, count, INNER)),
            shape((seqs, count, INNER), BF),
            shape((seqs, NS, INNER), BF),
        ],
        [pltpu.VMEM((seqs, NS, INNER), F32)],
    )(step_pre, head, sides, mixer, ssm, gating, mixer_root, along, gain, root)
    return grad.reshape(total, INNER), gating_grad.reshape(total, INNER), leaving


def ssm_back_one(n, step_pre, head, conv, sides, grads, carried_ref, root, conv_ref, step_ref, sums_ref, later):
    arg, size, cum = block_steps(step_pre[n], head)
    size_rows, cum_rows = as_rows(size), as_rows(cum)
    last = cum[BLOCK - 1 :, :]
    growth, to_end, decay = jnp.exp(cum), jnp.exp(last - cum), jnp.exp(last)
    feeding = to_end * size
    conv_sum = conv[n, :, :INNER]
    inner = silu_value(conv_sum)
    inner_low = inner.astype(BF)
    in_state, out_state = joined(sides, 0, n), joined(sides, 4, n)
    carried = carried_ref[n, 0]
    after = later[n]
    after_low = after.astype(BF)
    grad = grads[n]
    grad_low = grad.astype(BF)
    pairing = dot(out_state, in_state, (1, 1))
    readout = dot(out_state, carried, (1, 0))
    spread = dot(in_state, after_low, (1, 0))
    grown = (over_heads(growth) * grad).astype(BF)
    feeding_wide = over_heads(feeding)
    fed_inner = (feeding_wide * inner).astype(BF)
    pairing_grad = jnp.zeros((BLOCK, BLOCK), F32)
    inner_parts, flows, step_rows = [], [], []
    for h in range(HEADS):
        at = slice(h * PM, (h + 1) * PM)
        fading = fading_of(cum, cum_rows, h)
        sized = size_rows[h : h + 1, :]
        mixing = (fading * pairing * sized).astype(BF)
        faded = dot(grad_low[:, at], inner_low[:, at], (1, 1)) * fading
        pairing_grad = pairing_grad + faded * sized
        stepwise = faded * pairing
        step_rows.append(jnp.sum(stepwise, axis=0, keepdims=True))
        flows.append(jnp.sum(stepwise * sized, axis=1, keepdims=True))
        inner_parts.append(dot(mixing, grad_low[:, at], (0, 0)))
    empty_row, empty_column = jnp.zeros((2, BLOCK), F32), jnp.zeros((BLOCK, 2), F32)
    step_rows = jnp.concatenate(step_rows + [empty_row], 0)
    flow = jnp.concatenate(flows + [empty_column], 1)
    pairing_low = pairing_grad.astype(BF)
    out_grad = dot(pairing_low, in_state, (1, 0)) + dot(grown, carried, (1, 1))
    in_grad = dot(pairing_low, out_state, (0, 0)) + dot(fed_inner, after_low, (1, 1))
    inner_grad = (
        jnp.concatenate(inner_parts, 1) + over_heads(head[2:3, :]) * grad + feeding_wide * spread
    )
    conv_ref[n] = inner_grad * silu_slope(conv_sum)
    feeding_grad = head_sums(spread * inner)
    fed = feeding_grad * feeding
    through = jnp.sum(after * carried.astype(F32), axis=0, keepdims=True)
    through = head_sums(jnp.broadcast_to(through, (8, INNER)))[:1]
    last_grad = jnp.sum(fed, axis=0, keepdims=True) + through * decay
    cum_grad = flow - as_columns(step_rows * size_rows) + head_sums(grad * readout) * growth - fed
    row, column = triangle()
    increment = exact(jnp.where(column >= row, 1.0, 0.0), cum_grad, (1, 0)) + last_grad
    rates = head[1:2, :]
    step_grad = as_columns(step_rows) + feeding_grad * to_end + increment * rates
    arg_grad = step_grad * jax.nn.sigmoid(arg)
    step_ref[n] = (arg_grad * root[n]).astype(BF)
    skip = jnp.broadcast_to(jnp.sum(grad * inner, axis=0, keepdims=True), (8, INNER))
    sums_ref[0:1, :] += jnp.sum(arg_grad, axis=0, keepdims=True)
    sums_ref[1:2, :] += jnp.sum(increment * size, axis=0, keepdims=True) * rates
    sums_ref[2:3, :] += head_sums(skip)[:1]
    later[n] = over_heads(decay) * after + dot(out_state, grown, (0, 0))
    return in_grad, out_grad


def ssm_back_kernel(seqs, step_pre, head, conv, sides, grads, carried, entry, root, conv_ref, parts_ref, step_ref, sums_ref, later):
    @pl.when(pl.program_id(0) == 0)
    def _():
        later[...] = entry[...].astype(F32)
        sums_ref[...] = jnp.zeros_like(sums_ref)

    grad_pairs = [
        ssm_back_one(
            n, step_pre, head, conv, sides, grads, carried, root, conv_ref, step_ref, sums_ref, later
        )
        for n in range(seqs)
    ]
    for rank in range(RANKS):
        at = (rank % 4) * SIDE
        parts_ref[rank] = jnp.concatenate(
            [grad[rank // 4][:, at : at + SIDE] for grad in grad_pairs], 1
        ).astype(BF)


def ssm_back(seqs, step_pre, head, conv, sides, grads, carried, entry, root):
    total = conv.shape[0]
    step_pre, conv, grads, root = by_seq(seqs, step_pre, conv, grads, root)
    count = conv.shape[1]
    blocks = count // BLOCK
    back = lambda width: pair(seqs, width, blocks)
    conv_grad, parts, step_rows, sums = call(
        18.8,
        lambda *refs: ssm_back_kernel(seqs, *refs),
        (blocks,),
        [
            back(8),
            full(head),
            back(LANES),
            pl.BlockSpec((RANKS, BLOCK, seqs * SIDE), lambda i: (0, blocks - 1 - i, 0)),
            back(INNER),
            pl.BlockSpec((seqs, 1, NS, INNER), lambda i: (0, blocks - 1 - i, 0, 0)),
            full(entry),
            back(1),
        ],
        [
            back(INNER),
            pl.BlockSpec((RANKS, BLOCK, seqs * SIDE), lambda i: (0, blocks - 1 - i, 0)),
            back(8),
            pl.BlockSpec((8, 8), lambda i: (0, 0)),
        ],
        [
            shape((seqs, count, INNER)),
            shape((RANKS, count, seqs * SIDE), BF),
            shape((seqs, count, 8), BF),
            shape((8, 8)),
        ],
        [pltpu.VMEM((seqs, NS, INNER), F32)],
    )(step_pre, head, conv, sides, grads, carried, entry, root)
    return conv_grad.reshape(total, INNER), parts, step_rows.reshape(total, 8), sums


def conv_back_kernel(tiles, inner, parts, keys, conv, pre, edge, grad_ref, sums_ref, line):
    i = pl.program_id(0)
    first = i < tiles
    got = jnp.sum(parts[...].astype(F32), axis=0)
    got = jnp.where(first, got[:, :SIDE], got[:, SIDE:]) * silu_slope(conv[:, INNER:CONV])
    keys_got = keys[...]
    keys_got = jnp.where(first, keys_got[:, :SIDE], keys_got[:, SIDE:])
    got = jnp.concatenate([got, keys_got], 1)
    grad = jnp.concatenate([inner[...], got], 1)
    grad_ref[...] = grad

    @pl.when(i % tiles == 0)
    def _():
        line[:EDGE] = edge[0]

    @pl.when(i % tiles != 0)
    def _():
        line[:EDGE] = line[TILE:]

    @pl.when(i == 0)
    def _():
        sums_ref[...] = jnp.zeros_like(sums_ref)

    line[EDGE:] = pre[...]
    for k in range(KC):
        before = line[EDGE - (KC - 1) + k : EDGE - (KC - 1) + k + TILE, :]
        sums_ref[k : k + 1, :] += jnp.sum(grad * before, axis=0, keepdims=True)
    sums_ref[KC : KC + 1, :] += jnp.sum(grad, axis=0, keepdims=True)


def conv_back(inner, parts, keys, conv, pre, edge):
    total = conv.shape[0]
    tiles = total // TILE // edge.shape[0]
    return call(
        4.8,
        lambda *refs: conv_back_kernel(tiles, *refs),
        (total // TILE,),
        [
            tiled(INNER),
            pl.BlockSpec((RANKS, TILE, 2 * SIDE), lambda i: (0, i % tiles, 0)),
            pl.BlockSpec((TILE, 2 * SIDE), lambda i: (i % tiles, 0)),
            tiled(LANES),
            tiled(LANES),
            pl.BlockSpec((1, EDGE, LANES), lambda i: (i // tiles, 0, 0)),
        ],
        [tiled(LANES), pl.BlockSpec((8, LANES), lambda i: (0, 0))],
        [shape((total, LANES)), shape((8, LANES))],
        [pltpu.VMEM((EDGE + TILE, LANES), F32)],
    )(inner, parts, keys, conv, pre, edge)


def pre_back_kernel(tiles, grad, after, follow, taps, root, out_ref, line):
    i = pl.program_id(0)
    line[:TILE] = grad[...]

    @pl.when(i % tiles == tiles - 1)
    def _():
        line[TILE:] = follow[0]

    @pl.when(i % tiles != tiles - 1)
    def _():
        line[TILE:] = after[...]

    total = taps[KC - 1 : KC, :] * line[:TILE, :]
    for k in range(KC - 1):
        total = total + taps[k : k + 1, :] * line[KC - 1 - k : KC - 1 - k + TILE, :]
    out_ref[...] = (total * root[...]).astype(BF)


def pre_back(grad, follow, taps, root):
    total = grad.shape[0]
    tiles = total // TILE // follow.shape[0]
    last = total // EDGE - 1
    return call(
        1.4,
        lambda *refs: pre_back_kernel(tiles, *refs),
        (total // TILE,),
        [
            tiled(LANES),
            pl.BlockSpec((EDGE, LANES), lambda i: (jnp.minimum((i + 1) * (TILE // EDGE), last), 0)),
            pl.BlockSpec((1, EDGE, LANES), lambda i: (i // tiles, 0, 0)),
            full(taps),
            tiled(1),
        ],
        tiled(LANES),
        shape((total, LANES), BF),
        [pltpu.VMEM((TILE + EDGE, LANES), F32)],
    )(grad, grad, follow, taps, root)


def local(
    tokens,
    cotangent,
    norm_gain,
    gating_weight,
    inner_weight,
    state_weight,
    step_weight,
    conv_weight,
    conv_bias,
    mixer_gain,
    mixer_out,
    query_weight,
    key_weight,
    value_weight,
    output_weight,
    feed_gain,
    gate_matrix,
    lift_matrix,
    drop_matrix,
    step_bias,
    decay_log,
    skip_scale,
):
    sh, sl, ch = lax.axis_size("sh"), lax.axis_size("sl"), lax.axis_size("ch")
    world = sh * sl * ch * 4
    rows, width = tokens.shape
    drows = norm_gain.shape[0]
    my_sl, my_zl, my_core = (lax.axis_index(axis) for axis in TEAM)
    rank = (my_sl * 2 + my_zl) * 2 + my_core
    total = RANKS * rows
    count = 4 * rows
    whole = ch * count

    order = team_order()
    straight = jnp.arange(8, dtype=jnp.int32)
    tiles = [((z ^ my_zl) * 2 + (s ^ my_sl)) for s in (0, 1) for z in (0, 1)]
    scalars = jnp.stack([my_core, *tiles]).astype(jnp.int32)
    place = (lax.axis_index("ch") * count).astype(jnp.int32).reshape(1)
    dims = (sh, sl, ch, width)
    home = column_blocks(sh, sl, ch)
    nowhere = jnp.zeros_like(home)

    def scaled(weight, gain):
        return (weight.astype(F32) * gain.astype(F32)[:, None]).astype(BF)

    key_value = jnp.stack(
        [key_weight.reshape(drows, HK, 2, SIDE), value_weight.reshape(drows, HK, 2, SIDE)], 2
    ).reshape(drows, RANKS * SIDE)
    pack_in = jnp.concatenate(
        [
            by_rank(scaled(w, norm_gain))
            for w in (inner_weight, state_weight, key_value, gating_weight, query_weight)
        ],
        2,
    )
    conv_own, gain_own = conv_weight.shape[1], mixer_gain.shape[0]
    step_sent = jnp.broadcast_to(
        scaled(step_weight, norm_gain).T.reshape(1, sl, 1, 4, HEADS * drows),
        (sh, sl, ch, 4, HEADS * drows),
    ).reshape(world, HEADS * drows)
    shared = jnp.concatenate([conv_weight.reshape(-1), conv_bias, mixer_gain])
    small = jnp.concatenate(
        [jnp.broadcast_to(shared[None], (world, shared.shape[0])), step_sent], 1
    )
    with jax.named_scope("small_exchange"):
        small = lax.all_to_all(small, WORLD, split_axis=0, concat_axis=0, tiled=True)
    small, pack_in = together(small, pack_in)
    with jax.named_scope("weights_in"):
        mixed_in = ranks_exchange(pack_in)
    *own_tokens, own_cotangent = arrive(dims, home, tokens, cotangent)
    with jax.named_scope("tokens_gather"):
        team_tokens = list(team_gather(*own_tokens))
    last = 4
    ends = []
    for seq in range(sl):
        at_block = 2 * (1 - my_zl) + (seq ^ my_sl)
        halves = []
        for own, other in ((team_tokens[0], team_tokens[2]), (team_tokens[1], team_tokens[3])):
            own = lax.dynamic_index_in_dim(own[:, rows - last :], at_block, 0, False)
            other = lax.dynamic_index_in_dim(other[:, rows - last :], at_block, 0, False)
            halves.append(jnp.where(my_core == 1, own, other))
        ends.append(jnp.concatenate(halves, 1))
    halo = jnp.stack(ends)
    with jax.named_scope("weights_first"):
        if ch == 2:
            first = mixed_in[:, :LANES]
            got = swap(jnp.concatenate([first, halo.reshape(-1, LANES)], 0), "ch")
            ready = jnp.concatenate([first, got[: first.shape[0]]], 0)
            halo = got[first.shape[0] :].reshape(sl, last, sh, ch, -1)
            halo = jnp.flip(halo, 3).reshape(sl, last, width)
            halo = jnp.where(lax.axis_index("ch") == 0, jnp.zeros_like(halo), halo)
        else:
            ready = along_ch(mixed_in[:, :LANES])
            halo = shifted(halo, 1)
        halo = jnp.pad(halo, ((0, 0), (EDGE - last, 0), (0, 0)))
    pack_rest = jnp.concatenate(
        [by_rank(mixer_out.T), by_rank(output_weight.T)]
        + [by_rank(scaled(w, feed_gain)) for w in (gate_matrix, lift_matrix)]
        + [by_rank(drop_matrix.T)],
        2,
    )
    pack_rest, *team_tokens = together(pack_rest, *team_tokens)
    with jax.named_scope("weights_rest"):
        mixed_rest = ranks_exchange(pack_rest)
    with jax.named_scope("weights_inner"):
        theirs, gating_ready = together(swap(ready, "sh"), along_ch(mixed_in[:, LANES:]))
    w_inner = (ready, theirs)

    at = (KC + 1) * conv_own
    wide_conv = small[:, :at].reshape(world, KC + 1, conv_own)
    wide_conv = wide_conv.transpose(1, 0, 2).reshape(KC + 1, -1).astype(F32)
    wide_gain = small[:, at : at + gain_own].reshape(1, -1).astype(F32)
    own_step = small[:, at + gain_own :].reshape(sh, sl, ch, 4, HEADS, drows).swapaxes(1, 2)
    own_step = relative(relative(own_step, "sh", 0), "ch", 1)
    own_step = own_step.reshape(-1, HEADS, drows).swapaxes(0, 1).reshape(HEADS, width)
    own_step = jnp.pad(own_step, ((0, 8 - HEADS), (0, 0)))
    taps = jnp.concatenate(
        [
            lax.dynamic_slice_in_dim(wide_conv, rank * INNER, INNER, 1),
            lax.dynamic_slice_in_dim(wide_conv, DI + rank * SIDE, SIDE, 1),
            jnp.zeros((KC + 1, LANES - CONV), F32).at[KC - 1].set(1.0),
        ],
        1,
    )
    taps = jnp.pad(taps, ((0, 8 - KC - 1), (0, 0)))
    own_gain = lax.dynamic_slice_in_dim(wide_gain, rank * INNER, INNER, 1)
    head = jnp.stack([step_bias, -jnp.exp(decay_log), skip_scale])
    head = lax.dynamic_slice_in_dim(head, rank * HEADS, HEADS, 1)
    head = jnp.pad(head, ((0, 5), (0, 8 - HEADS)))

    pre, conv, side, own_keys, step_pre, root, edge = project_inner(
        scalars, team_tokens, w_inner, halo, taps, own_step
    )
    def packed(values):
        return values.reshape(sl, count, SIDE).swapaxes(0, 1).reshape(count, sl * SIDE)

    sides = lax.all_gather(packed(side), TEAM)
    sent_cotangent, sides = together(own_cotangent, sides)
    team_cotangent = lax.all_gather(sent_cotangent, TEAM, axis=0, tiled=True)
    with jax.named_scope("keys_exchange"):
        own_keys = packed(own_keys)[None]
        if ch == 2:
            own_keys = paired(own_keys[0], swap(own_keys[0], "ch"), "ch", 0)
        elif ch > 2:
            own_keys = lax.all_gather(own_keys[0], "ch")
        own_keys = paired(own_keys, swap(own_keys, "zl"), "zl", 0)
        own_keys = paired(own_keys, swap(own_keys, "core"), "core", 1)
        key_value_rows = keys_of(sl, own_keys.reshape(4, whole, sl * SIDE))
    with jax.named_scope("weights_gating"):
        theirs, out_ready = together(
            swap(gating_ready, "sh"), along_ch(mixed_rest[:, :LANES])
        )
    w_gating = (gating_ready, theirs)
    gating, queries = project_gating(scalars, team_tokens, w_gating, root)
    with jax.named_scope("weights_out"):
        w_out = (out_ready, swap(out_ready, "sh"))
    sides, gating = together(sides, gating)
    leaving, piece_decay = states(sl, step_pre, head, conv, sides)
    with jax.named_scope("state_exchange"):
        entry = entering(piece_decay[:, 0], leaving, False)
    entry, mixed_rest = together(entry, mixed_rest)
    rest = [mixed_rest[:, at * LANES : (at + 1) * LANES] for at in range(1, 4)]
    with jax.named_scope("weights_gate_first"):
        gate_ready = along_ch(rest[0])
    attended, logs = attend(place, queries, key_value_rows)
    ssm, carried, square = ssm_block(sl, step_pre, head, conv, sides, gating, entry)
    with jax.named_scope("square_sum"):
        square = team_sum(square)
    mixer_root = lax.rsqrt(square / DI + epsilon).reshape(total, 1)
    branch_rows = jnp.concatenate(
        [(ssm * silu_value(gating) * mixer_root * own_gain).astype(BF), attended.astype(BF)], 1
    )
    branch_rows, gate_ready, rest[1] = together(branch_rows, gate_ready, rest[1])
    with jax.named_scope("weights_gate"):
        theirs, lift_ready = together(swap(gate_ready, "sh"), along_ch(rest[1]))
    w_gate = (gate_ready, theirs)
    branch_parts = back_dot(order, [(branch_rows, w_out)])
    with jax.named_scope("branch_scatter"):
        branch = scatter_core(branch_parts)
    lift_ready, rest[2], *branch = together(lift_ready, rest[2], *branch)
    with jax.named_scope("weights_lift"):
        theirs, drop_ready = together(swap(lift_ready, "sh"), along_ch(rest[2]))
    w_lift = (lift_ready, theirs)
    with jax.named_scope("branch_scatter"):
        branch = scatter_last(scatter_near(branch))
    branch = list(branch)
    drop_ready, branch[0] = together(drop_ready, branch[0])
    with jax.named_scope("weights_drop"):
        w_drop = (drop_ready, swap(drop_ready, "sh"))
    residual, feed_root, *feed_halves = home_forward(dims, nowhere, branch, own_tokens)
    with jax.named_scope("feed_gather"):
        feed_rows = team_gather(*feed_halves)
    active, gate_rows_grad, lift_rows_grad = feed_block(
        scalars, feed_rows, team_cotangent, w_gate, w_lift, w_drop
    )
    feed_parts = back_dot(order, [(gate_rows_grad, w_gate), (lift_rows_grad, w_lift)])
    with jax.named_scope("feed_scatter"):
        feed_grad = team_scatter(feed_parts)
    feed_back = feed_grads(
        order, feed_rows, team_cotangent, active, gate_rows_grad, lift_rows_grad
    )
    mine, given_parts = feed_back[:3], feed_back[3:]
    with jax.named_scope("gate_back"):
        gate_got = swap(given_parts[0], "sh")
    feed_grad = list(feed_grad)
    feed_grad[0], active, gate_got = together(feed_grad[0], active, gate_got)
    layer_part = forth_dot(active, w_drop)
    with jax.named_scope("lift_back"):
        lift_got, gate_part = together(swap(given_parts[1], "sh"), ch_part(added(mine[0], gate_got)))
    residual_grad, *branch_halves = home_back(
        dims, nowhere, feed_grad, residual, feed_root, own_cotangent
    )
    with jax.named_scope("branch_gather"):
        branch_grad = team_gather(*branch_halves)
    layer_part, *branch_grad = together(layer_part, *branch_grad)
    layer_part = lax.psum_scatter(layer_part, TEAM, scatter_dimension=0, tiled=True)

    mixer_rows_grad, attn_grad, along, gain_part = rows_back(
        scalars, branch_grad, w_out, ssm, gating, mixer_root, own_gain
    )
    mixer_rows_grad, lift_got, gate_part = together(mixer_rows_grad, lift_got, gate_part)
    with jax.named_scope("drop_back"):
        drop_got, lift_part = together(swap(given_parts[2], "sh"), ch_part(added(mine[1], lift_got)))
    with jax.named_scope("along_sum"):
        along = team_sum(along[:, 0]).reshape(total, 1) / DI
    query_grad, key_parts = attend_back(
        place, queries, attn_grad, attended, logs, root, key_value_rows
    )
    with jax.named_scope("keys_back"):
        key_parts = lax.all_to_all(
            key_parts.astype(BF), ("zl", "core"), split_axis=0, concat_axis=0, tiled=True
        )
        key_parts = jnp.sum(key_parts.astype(F32), axis=0).reshape(ch, count, sl * SIDE)
        if ch == 1:
            key_grad = key_parts[0]
        elif ch == 2:
            key_grad = added(
                kept(key_parts, "ch", 0), swap(given(key_parts, "ch", 0).astype(BF), "ch")
            )
        else:
            key_grad = lax.psum_scatter(
                key_parts.astype(BF), "ch", scatter_dimension=0, tiled=False
            ).astype(F32)
    out_mine, out_theirs = grad_halves(order, gathered_halves(branch_grad), branch_rows)
    along, drop_got, lift_part, out_theirs = together(along, drop_got, lift_part, out_theirs)
    with jax.named_scope("out_back"):
        out_theirs, drop_part = together(
            swap(out_theirs, "sh"), ch_part(added(mine[2], drop_got))
        )
    ssm_grad, gating_grad, leaving_back = states_back(
        sl, step_pre, head, sides, mixer_rows_grad, ssm, gating, mixer_root, along, own_gain, root
    )
    with jax.named_scope("state_back"):
        entry_back = entering(piece_decay[:, 0], leaving_back, True)
    gating_rows_grad = jnp.concatenate([gating_grad, query_grad], 1)
    gating_mine, gating_theirs = grad_halves(order, gathered_halves(team_tokens), gating_rows_grad)
    entry_back, out_theirs, drop_part = together(entry_back, out_theirs, drop_part)
    with jax.named_scope("first_return"):
        first_back = ranks_return([gate_part, lift_part, drop_part], drows)
    inner_conv_grad, parts, step_rows_grad, sums = ssm_back(
        sl, step_pre, head, conv, sides, ssm_grad, carried, entry_back, root
    )
    parts, key_grad, first_back = together(parts, key_grad, first_back)
    with jax.named_scope("parts_exchange"):
        parts = lax.all_to_all(parts, TEAM, split_axis=0, concat_axis=0, tiled=True)
    with jax.named_scope("gating_back"):
        gating_theirs, out_part = together(
            swap(gating_theirs, "sh"), ch_part(added(out_mine, out_theirs))
        )
    conv_grad, conv_sums = conv_back(inner_conv_grad, parts, key_grad, conv, pre, edge)
    with jax.named_scope("follow"):
        follow = shifted(conv_grad.reshape(sl, count, LANES)[:, :EDGE], -1)
    inner_rows_grad = pre_back(conv_grad, follow, taps, root)
    inner_rows_grad, gating_theirs, out_part = together(inner_rows_grad, gating_theirs, out_part)
    inner_theirs = grad_dot(order, gathered_halves(team_tokens)[1], inner_rows_grad, BF)
    inner_mine = grad_dot(order, gathered_halves(team_tokens)[0], inner_rows_grad, F32)
    inner_rows_grad, inner_theirs = together(inner_rows_grad, inner_theirs)
    half = width // 2
    step_halves = (own_step[:, : width // 2], own_step[:, width // 2 :])
    hidden_parts = back_dot(
        order,
        [
            (inner_rows_grad, w_inner),
            (gating_rows_grad, w_gating),
            (step_rows_grad, step_halves),
        ],
    )
    with jax.named_scope("inner_back"):
        inner_theirs = swap(inner_theirs, "sh")
    with jax.named_scope("second_return"):
        second_back = ranks_return([out_part], drows)
    inner_theirs, second_back, *hidden_parts = together(inner_theirs, second_back, *hidden_parts)
    with jax.named_scope("gating_part"):
        gating_part = ch_part(added(gating_mine, gating_theirs))
    with jax.named_scope("hidden_scatter"):
        hidden_parts = team_scatter(hidden_parts)
    with jax.named_scope("inner_part"):
        inner_part = ch_part(added(inner_mine, inner_theirs))
    with jax.named_scope("third_return"):
        third_back = ranks_return([gating_part, inner_part], drows).astype(F32)
    first_back = first_back.astype(F32)
    gate_back = first_back[:, :, :LANES]
    lift_back = first_back[:, :, LANES : 2 * LANES]
    drop_back = first_back[:, :, 2 * LANES : 3 * LANES]
    out_back = second_back.astype(F32)
    gating_back = third_back[:, :, :LANES]
    inner_back = third_back[:, :, LANES:]
    token_values = jnp.concatenate(own_tokens, 1)
    token_root = inverse_root(token_values.astype(F32))
    hidden_parts = [part.astype(F32) / token_root for part in hidden_parts]
    half = width // 2
    tokens_grad, _, _ = home_back(
        dims, nowhere, hidden_parts, token_values, token_root, residual_grad
    )
    tokens_out = leave(dims, home, tokens_grad, None, F32)
    layer_output = leave(dims, home, residual, layer_part, BF)
    token_left, token_right = gathered_halves(team_tokens)
    step_back = jnp.concatenate(
        [
            grad_dot(order, token_left, step_rows_grad, F32),
            grad_dot(order, token_right, step_rows_grad, F32),
        ],
        0,
    )[:, :HEADS].T

    def placed(part, extent, at):
        base = jnp.zeros(part.shape[:-1] + (extent,), F32)
        return lax.dynamic_update_slice_in_dim(base, part, at, part.ndim - 1)

    conv_all = jnp.concatenate(
        [
            placed(conv_sums[: KC + 1, :INNER], DI, rank * INNER),
            placed(conv_sums[: KC + 1, INNER:CONV], 2 * NS, rank * SIDE),
        ],
        1,
    )
    gain_all = placed(gain_part[0], DI, rank * INNER)
    step_all = step_back.reshape(HEADS, -1, drows).swapaxes(0, 1)
    step_all = step_all.reshape(sh, ch, sl, 4, HEADS * drows)
    step_all = relative(relative(step_all, "sh", 0), "ch", 1).swapaxes(1, 2)
    per_head = jnp.concatenate(
        [placed(sums[at, :HEADS], HM, rank * HEADS) for at in range(3)]
    )
    sent = jnp.concatenate(
        [
            conv_all.reshape(KC + 1, world, conv_own).swapaxes(0, 1).reshape(world, -1),
            gain_all.reshape(world, -1),
            step_all.reshape(world, -1),
            jnp.broadcast_to(per_head[None], (world, 3 * HM)),
        ],
        1,
    )
    got_all = lax.all_to_all(sent, WORLD, split_axis=0, concat_axis=0, tiled=True)
    at = KC * conv_own + conv_own + gain_own
    step_core = got_all[:, at : at + HEADS * drows].reshape(sh, sl, ch, 4, HEADS, drows)
    step_core = jnp.sum(step_core, axis=(0, 2)).reshape(HM, drows).T
    got = jnp.sum(got_all, axis=0)
    at = 0
    conv_out = got[at : at + KC * conv_own].reshape(KC, conv_own)
    at += KC * conv_own
    conv_bias_out = got[at : at + conv_own]
    at += conv_own
    gain_out = got[at : at + gain_own]
    at += gain_own + HEADS * drows
    bias_out, decay_out, skip_out = (got[at + i * HM : at + (i + 1) * HM] for i in range(3))

    def against(weight, grad):
        return jnp.sum(weight.astype(F32) * grad, axis=1)

    inner_core = to_columns(inner_back[:, :, :INNER])
    state_core = to_columns(inner_back[:, :, INNER:CONV])
    key_value_core = to_columns(inner_back[:, :, CONV:]).reshape(drows, HK, 2, 2 * SIDE)
    key_core = key_value_core[:, :, 0].reshape(drows, HK * HD)
    value_core = key_value_core[:, :, 1].reshape(drows, HK * HD)
    gating_core = to_columns(gating_back[:, :, :INNER])
    query_core = to_columns(gating_back[:, :, INNER:])
    gate_core, lift_core = to_columns(gate_back), to_columns(lift_back)
    norm_out = (
        against(gating_weight, gating_core)
        + against(inner_weight, inner_core)
        + against(state_weight, state_core)
        + against(step_weight, step_core)
        + against(query_weight, query_core)
        + against(key_weight, key_core)
        + against(value_weight, value_core)
    )
    feed_out = against(gate_matrix, gate_core) + against(lift_matrix, lift_core)
    norm_scale = norm_gain.astype(F32)[:, None]
    feed_scale = feed_gain.astype(F32)[:, None]
    mixer_out_out = out_back[:, :, :INNER].transpose(0, 2, 1).reshape(DI, drows)
    output_out = out_back[:, :, INNER:].transpose(0, 2, 1).reshape(HA * HD, drows)
    drop_out = drop_back.transpose(0, 2, 1).reshape(-1, drows)
    return (
        layer_output,
        tokens_out,
        norm_out,
        gating_core * norm_scale,
        inner_core * norm_scale,
        state_core * norm_scale,
        step_core * norm_scale,
        conv_out,
        conv_bias_out,
        gain_out,
        mixer_out_out,
        query_core * norm_scale,
        key_core * norm_scale,
        value_core * norm_scale,
        output_out,
        feed_out,
        gate_core * feed_scale,
        lift_core * feed_scale,
        drop_out,
        bias_out,
        decay_out,
        skip_out,
    )


def solution(mesh):
    seq, ctx = mesh.shape["seq"], mesh.shape["ctx"]
    fine = Mesh(mesh.devices.reshape(seq // 2, 2, ctx // 4, 2, 2), WORLD)
    lead, vector, tail = P(WORLD, None), P(WORLD), P(None, WORLD)
    in_specs = (
        lead,
        lead,
        vector,
        lead,
        lead,
        lead,
        lead,
        tail,
        vector,
        vector,
        tail,
        lead,
        lead,
        lead,
        tail,
        vector,
        lead,
        lead,
        tail,
        P(),
        P(),
        P(),
    )
    out_specs = (
        lead,
        lead,
        vector,
        lead,
        lead,
        lead,
        lead,
        tail,
        vector,
        vector,
        tail,
        lead,
        lead,
        lead,
        tail,
        vector,
        lead,
        lead,
        tail,
        P(),
        P(),
        P(),
    )
    return jax.shard_map(local, mesh=fine, in_specs=in_specs, out_specs=out_specs, check_vma=False)
```

```python
import jax
import jax.numpy as jnp
from jax import lax
from jax.experimental import pallas as pl
from jax.experimental.pallas import tpu as pltpu
from jax.sharding import Mesh
from jax.sharding import PartitionSpec as P

DI = 3072
HM = 48
PM = 64
NS = 256
KC = 4
HA = 8
HK = 2
HD = 128
FF = 4096
BLOCK = 128

epsilon = 1e-06
negative = -1e30
BF = jnp.bfloat16
F32 = jnp.float32

TEAM = ("sl", "zl", "core")
PEERS = ("sh", "ch")
WORLD = ("sh", "sl", "ch", "zl", "core")
RANKS = 8


def swap(value, axis):
    return lax.ppermute(value, axis, [(0, 1), (1, 0)])


def paired(mine, theirs, axis_name, dim):
    bit = lax.axis_index(axis_name)
    return jnp.where(bit == 0, jnp.stack([mine, theirs], dim), jnp.stack([theirs, mine], dim))


def kept(value, axis_name, dim):
    return lax.dynamic_index_in_dim(value, lax.axis_index(axis_name), dim, False)


def given(value, axis_name, dim):
    return lax.dynamic_index_in_dim(value, 1 - lax.axis_index(axis_name), dim, False)


def added(mine, theirs):
    return mine.astype(F32) + theirs.astype(F32)


def team_order():
    s, z, c = (lax.axis_index(axis) for axis in TEAM)
    blocks = [
        ((s ^ sl) * 2 + (z ^ zl)) * 2 + (c ^ core)
        for core in (0, 1)
        for zl in (0, 1)
        for sl in (0, 1)
    ]
    return jnp.stack(blocks).astype(jnp.int32)


def team_gather(left, right):
    left = jnp.stack([left, swap(left, "sl")])
    right = jnp.stack([right, swap(right, "zl")])
    left_z = swap(left, "zl")
    right_x = swap(right, "sl")
    left = jnp.concatenate([left, left_z], 0)
    right = jnp.stack([right[0], right_x[0], right[1], right_x[1]])
    return left, right, swap(left, "core"), swap(right, "core")


def scatter_core(parts):
    left, right, left_given, right_given = parts
    left_got, right_got = swap(left_given, "core"), swap(right_given, "core")
    return (
        added(left[:2], left_got[:2]),
        added(left[2:], left_got[2:]).astype(BF),
        added(right[0::2], right_got[0::2]),
        added(right[1::2], right_got[1::2]).astype(BF),
    )


def scatter_near(parts):
    left, left_given, right, right_given = parts
    left = left + swap(left_given, "zl").astype(F32)
    right = right + swap(right_given, "sl").astype(F32)
    return left[0], left[1].astype(BF), right[0], right[1].astype(BF)


def scatter_last(parts):
    left, left_given, right, right_given = parts
    return left, swap(left_given, "sl"), right, swap(right_given, "zl")


def team_scatter(parts):
    return scatter_last(scatter_near(scatter_core(parts)))


def team_sum(value):
    for axis in TEAM[::-1]:
        value = value + swap(value, axis)
    return value


def relative(value, axis_name, dim):
    if lax.axis_size(axis_name) != 2:
        return value
    return jnp.where(lax.axis_index(axis_name) == 0, value, jnp.flip(value, dim))


def together(*values):
    return lax.optimization_barrier(values)


def along_ch(part):
    size = lax.axis_size("ch")
    if size == 2:
        return jnp.concatenate([part, swap(part, "ch")], 0)
    return lax.all_gather(part, "ch", axis=0, tiled=True)


def peers_gather(parts):
    out = []
    ready = along_ch(parts[0])
    for part in parts[1:]:
        mine = ready
        theirs, ready = together(swap(mine, "sh"), along_ch(part))
        out.append((mine, theirs))
    return out + [(ready, swap(ready, "sh"))]


def ranks_exchange(pack):
    mixed = lax.all_to_all(pack, TEAM, split_axis=0, concat_axis=0, tiled=True)
    return mixed.reshape(-1, pack.shape[2])


def ch_part(part):
    size = lax.axis_size("ch")
    if size == 2:
        half = part.shape[0] // 2
        part = added(part[:half], swap(part[half:].astype(BF), "ch"))
    elif size > 2:
        part = lax.psum_scatter(part.astype(BF), "ch", scatter_dimension=0, tiled=True)
    return part.astype(BF)


def ranks_return(parts, rows):
    pack = jnp.concatenate([p.reshape(RANKS, rows, -1) for p in parts], 2)
    return lax.all_to_all(pack, TEAM, split_axis=0, concat_axis=0, tiled=True)


def by_rank(weight):
    rows = weight.shape[0]
    return weight.reshape(rows, RANKS, -1).transpose(1, 0, 2)


def to_columns(pieces):
    return pieces.transpose(1, 0, 2).reshape(pieces.shape[1], -1)


def column_blocks(sh, sl, ch):
    place = lax.axis_index("sh")
    if ch == 2:
        place = place * 2 + lax.axis_index("ch")
    return place.astype(jnp.int32).reshape(1)


def shifted(value, steps):
    count = lax.axis_size("ch")
    if count == 1:
        return jnp.zeros_like(value)
    leading, last = max(0, -steps), min(count, count - steps)
    return lax.ppermute(value, "ch", [(at, at + steps) for at in range(leading, last)])


def entering(decay, state, reverse):
    count = lax.axis_size("ch")
    if count == 1:
        return jnp.zeros_like(state)
    if count == 2:
        return shifted(state, -1 if reverse else 1)
    place = lax.axis_index("ch")
    ahead = count - 1 - place if reverse else place
    decays = lax.all_gather(decay, "ch")
    states = lax.all_gather(state, "ch")

    def one(step, run):
        source = count - 1 - step if reverse else step
        factor = lax.dynamic_index_in_dim(decays, source, 0, False)
        return factor[:, None] * run + lax.dynamic_index_in_dim(states, source, 0, False).astype(
            F32
        )

    return lax.fori_loop(0, ahead, one, jnp.zeros(state.shape, F32)).astype(state.dtype)


def inverse_root(values):
    return lax.rsqrt(jnp.mean(values * values, axis=-1, keepdims=True) + epsilon)


def norm_back(values, scaled, upstream):
    normed = values * scaled
    return scaled * (upstream - normed * jnp.mean(upstream * normed, axis=-1, keepdims=True))


def silu_value(values):
    return values * jax.nn.sigmoid(values)


def silu_slope(values):
    sigmoid_part = jax.nn.sigmoid(values)
    return sigmoid_part * (1.0 + values * (1.0 - sigmoid_part))


def dot(operand, against, at, precision=None):
    return lax.dot_general(
        operand, against, (((at[0],), (at[1],)), ((), ())), precision=precision, preferred_element_type=F32
    )


def exact(operand, against, at):
    return dot(operand, against, at, lax.Precision.HIGHEST)


TILE = 2 * BLOCK
EDGE = 16
LANES = 512
INNER = DI // RANKS
HEADS = HM // RANKS
SIDE = 2 * NS // RANKS
CONV = INNER + SIDE


def call(cost, kernel, grid, in_specs, out_specs, out_shape, scratch=(), scalars=0):
    return pl.pallas_call(
        kernel,
        grid_spec=pltpu.PrefetchScalarGridSpec(
            num_scalar_prefetch=scalars,
            grid=grid,
            in_specs=in_specs,
            out_specs=out_specs,
            scratch_shapes=list(scratch),
        ),
        out_shape=out_shape,
        compiler_params=pltpu.CompilerParams(vmem_limit_bytes=48 * 1024 * 1024),
        cost_estimate=pl.CostEstimate(flops=int(cost * 10**9), bytes_accessed=10**6, transcendentals=0),
    )


def shape(dims, dtype=F32):
    return jax.ShapeDtypeStruct(dims, dtype)


def full(array):
    return pl.BlockSpec(array.shape, lambda *at: (0,) * array.ndim)


def tiled(width, rows=TILE):
    return pl.BlockSpec((rows, width), lambda i, *at: (i, 0))


def place_rows(scalars, gathered, rows):
    left, right, left_other, right_other = gathered
    half = left.shape[2]
    own = pl.multiple_of(scalars[0] * BLOCK, BLOCK)
    other = pl.multiple_of((1 - scalars[0]) * BLOCK, BLOCK)
    rows[pl.ds(own, BLOCK), :half] = left[0]
    rows[pl.ds(own, BLOCK), half:] = right[0]
    rows[pl.ds(other, BLOCK), :half] = left_other[0]
    rows[pl.ds(other, BLOCK), half:] = right_other[0]


def gathered_specs(gathered):
    spec = pl.BlockSpec((1, BLOCK, gathered[0].shape[2]), lambda i, s: (s[1 + i], 0, 0))
    return [spec] * 4


def halves_product(rows, mine, theirs):
    half = mine.shape[0]
    return dot(rows[:, :half], mine[...], (1, 0)) + dot(rows[:, half:], theirs[...], (1, 0))


def row_root(rows):
    values = rows.astype(F32)
    return lax.rsqrt(jnp.mean(values * values, axis=-1, keepdims=True) + epsilon)


def natural_blocks(dims):
    sh, sl, ch, width = dims
    block = width // (sh * sl * ch)
    return [
        (((a * sl + b) * ch + c) * block, ((a * ch + c) * sl + b) * block, block)
        for a in range(sh)
        for b in range(sl)
        for c in range(ch)
    ]


def related(place, start, dims):
    sh, _, ch, width = dims
    unit = width // (sh * ch) if ch == 2 else width // sh
    return pl.multiple_of(lax.bitwise_xor(place, start // unit) * unit + start % unit, 128)


def related_blocks(dims):
    sh, _, ch, width = dims
    unit = width // (sh * ch) if ch == 2 else width // sh
    return range(0, width, unit), unit


def whole_blocks(width):
    return pl.BlockSpec((BLOCK, width), lambda i, s: (0, 0))


def shuffle_kernel(dims, place, rows, out_refs, scratch):
    width = dims[3]
    for natural, start, block in natural_blocks(dims):
        scratch[:, start : start + block] = rows[:, natural : natural + block].astype(F32)
    starts, unit = related_blocks(dims)
    for start in starts:
        at = related(place, start, dims)
        out = out_refs[start // (width // 2)]
        inside = start % (width // 2)
        out[:, inside : inside + unit] = scratch[:, pl.ds(at, unit)].astype(BF)


def arrive_kernel(dims, place, tokens, cotangent, tl, tr, whole, scratch):
    half = dims[3] // 2
    shuffle_kernel(dims, place[0], tokens, (tl, tr), scratch)
    shuffle_kernel(dims, place[0], cotangent, (whole.at[:, :half], whole.at[:, half:]), scratch)


def arrive(dims, place, tokens, cotangent):
    width = dims[3]
    half = shape((BLOCK, width // 2), BF)
    return call(
        2,
        lambda *refs: arrive_kernel(dims, *refs),
        (1,),
        [whole_blocks(width)] * 2,
        [whole_blocks(width // 2)] * 2 + [whole_blocks(width)],
        [half] * 2 + [shape((BLOCK, width), BF)],
        [pltpu.VMEM((BLOCK, width), F32)],
        1,
    )(place, tokens, cotangent)


def leave_kernel(dims, added_to, place, rows, *refs):
    out, scratch = refs[-2], refs[-1]
    values = rows[...].astype(F32)
    if added_to:
        values = values + refs[0][...].astype(F32)
    scratch[...] = values
    sh, _, ch, width = dims
    unit = related_blocks(dims)[1]
    for natural, start, block in natural_blocks(dims):
        at = pl.multiple_of(related(place[0], start // unit * unit, dims), 128)
        if block % 128 == 0:
            got = scratch[:, pl.ds(pl.multiple_of(at + start % unit, 128), block)]
        else:
            got = scratch[:, pl.ds(at, unit)][:, start % unit : start % unit + block]
        out[:, natural : natural + block] = got.astype(out.dtype)


def leave(dims, place, rows, ordered, dtype):
    width = dims[3]
    ins = [rows] if ordered is None else [rows, ordered]
    return call(
        1.5,
        lambda *refs: leave_kernel(dims, ordered is not None, *refs),
        (1,),
        [whole_blocks(width)] * len(ins),
        whole_blocks(width),
        shape((BLOCK, width), dtype),
        [pltpu.VMEM((BLOCK, width), F32)],
        1,
    )(place, *ins)


def home_forward_kernel(dims, place, left, left_rest, right, right_rest, tl, tr, residual_ref, root_ref, l_ref, r_ref):
    half = left.shape[1]
    a = tl[...].astype(F32) + left[...] + left_rest[...].astype(F32)
    b = tr[...].astype(F32) + right[...] + right_rest[...].astype(F32)
    square = jnp.sum(a * a, axis=-1, keepdims=True) + jnp.sum(b * b, axis=-1, keepdims=True)
    root = lax.rsqrt(square / (2 * half) + epsilon)
    residual_ref[:, :half] = a
    residual_ref[:, half:] = b
    root_ref[...] = root
    starts, unit = related_blocks(dims)
    for start in starts:
        out, inside = (l_ref, start) if start < half else (r_ref, start - half)
        rows = residual_ref[:, pl.ds(related(place[0], start, dims), unit)]
        out[:, inside : inside + unit] = (rows * root).astype(BF)


def home_forward(dims, place, parts, tokens):
    half = dims[3] // 2
    return call(
        1.4,
        lambda *refs: home_forward_kernel(dims, *refs),
        (1,),
        [whole_blocks(half)] * 6,
        [whole_blocks(2 * half), whole_blocks(1), whole_blocks(half), whole_blocks(half)],
        [
            shape((BLOCK, 2 * half)),
            shape((BLOCK, 1)),
            shape((BLOCK, half), BF),
            shape((BLOCK, half), BF),
        ],
        (),
        1,
    )(place, *parts, *tokens)


def home_back_kernel(dims, place, left, left_rest, right, right_rest, values, root, base, grad_ref, l_ref, r_ref, scratch):
    half = left.shape[1]
    width = 2 * half
    scaled = root[...]
    scratch[:, :half] = left[...] + left_rest[...].astype(F32)
    scratch[:, half:] = right[...] + right_rest[...].astype(F32)
    starts, unit = related_blocks(dims)
    mean = jnp.zeros_like(scaled)
    for start in starts:
        norm = values[:, pl.ds(related(place[0], start, dims), unit)].astype(F32) * scaled
        up = scratch[:, start : start + unit]
        mean = mean + jnp.sum(up * norm, axis=-1, keepdims=True)
    mean = mean / width
    for start in starts:
        at = related(place[0], start, dims)
        norm = values[:, pl.ds(at, unit)].astype(F32) * scaled
        up = scratch[:, start : start + unit]
        grad_ref[:, pl.ds(at, unit)] = base[:, pl.ds(at, unit)].astype(F32) + scaled * (
            up - norm * mean
        )
    l_ref[...] = grad_ref[:, :half].astype(BF)
    r_ref[...] = grad_ref[:, half:].astype(BF)


def home_back(dims, place, parts, values, root, base):
    half = dims[3] // 2
    return call(
        1.6,
        lambda *refs: home_back_kernel(dims, *refs),
        (1,),
        [whole_blocks(half)] * 4 + [whole_blocks(2 * half), whole_blocks(1), whole_blocks(2 * half)],
        [whole_blocks(2 * half), whole_blocks(half), whole_blocks(half)],
        [shape((BLOCK, 2 * half)), shape((BLOCK, half), BF), shape((BLOCK, half), BF)],
        [pltpu.VMEM((BLOCK, 2 * half), F32)],
        1,
    )(place, *parts, values, root, base)


def project_inner_kernel(tiles, scalars, l, r, lo, ro, mine, theirs, halo, taps, steps, pre_ref, conv_ref, side_ref, keys_ref, step_ref, root_ref, edge_ref, rows, line):
    i = pl.program_id(0)
    place_rows(scalars, (l, r, lo, ro), rows)
    values = rows[...]
    root = row_root(values)
    root_ref[...] = root
    pre = halves_product(values, mine, theirs) * root
    pre_ref[...] = pre
    step_ref[...] = dot(values, steps[...], (1, 1)) * root

    @pl.when(i % tiles == 0)
    def _():
        before = halo[0]
        edge = halves_product(before, mine, theirs) * row_root(before)
        edge_ref[0] = edge
        line[:EDGE] = edge

    @pl.when(i % tiles != 0)
    def _():
        line[:EDGE] = line[TILE:]

    line[EDGE:] = pre
    conv = taps[KC : KC + 1, :]
    for k in range(KC):
        conv = conv + taps[k : k + 1, :] * line[EDGE - (KC - 1) + k : EDGE - (KC - 1) + k + TILE, :]
    conv_ref[...] = conv
    side_ref[...] = silu_value(conv[:, INNER:CONV]).astype(BF)
    keys_ref[...] = pre[:, CONV:].astype(BF)


def project_inner(scalars, gathered, weight, halo, taps, steps):
    seqs = halo.shape[0]
    total = 2 * 4 * BLOCK
    tiles = total // TILE // seqs
    width = 2 * gathered[0].shape[2]
    return call(
        10.4,
        lambda *refs: project_inner_kernel(tiles, *refs),
        (total // TILE,),
        gathered_specs(gathered)
        + [full(weight[0]), full(weight[1])]
        + [pl.BlockSpec((1, EDGE, width), lambda i, s: (i // tiles, 0, 0)), full(taps), full(steps)],
        [
            tiled(LANES),
            tiled(LANES),
            tiled(SIDE),
            tiled(SIDE),
            tiled(8),
            tiled(1),
            pl.BlockSpec((1, EDGE, LANES), lambda i, s: (i // tiles, 0, 0)),
        ],
        [
            shape((total, LANES)),
            shape((total, LANES)),
            shape((total, SIDE), BF),
            shape((total, SIDE), BF),
            shape((total, 8)),
            shape((total, 1)),
            shape((seqs, EDGE, LANES)),
        ],
        [pltpu.VMEM((TILE, width), BF), pltpu.VMEM((EDGE + TILE, LANES), F32)],
        1,
    )(scalars, *gathered, *weight, halo, taps, steps)


def project_gating_kernel(scalars, l, r, lo, ro, mine, theirs, root, gating_ref, query_ref, rows):
    place_rows(scalars, (l, r, lo, ro), rows)
    product = halves_product(rows[...], mine, theirs) * root[...]
    gating_ref[...] = product[:, :INNER]
    query_ref[...] = product[:, INNER:].astype(BF)


def project_gating(scalars, gathered, weight, root):
    total, width = root.shape[0], 2 * gathered[0].shape[2]
    return call(
        6.2,
        project_gating_kernel,
        (total // TILE,),
        gathered_specs(gathered) + [full(weight[0]), full(weight[1]), tiled(1)],
        [tiled(INNER), tiled(HD)],
        [shape((total, INNER)), shape((total, HD), BF)],
        [pltpu.VMEM((TILE, width), BF)],
        1,
    )(scalars, *gathered, *weight, root)


def rows_back_kernel(scalars, l, r, lo, ro, mine, theirs, ssm, gating, root, gain, mixer_ref, attn_ref, along_ref, gain_ref, rows):
    place_rows(scalars, (l, r, lo, ro), rows)
    product = halves_product(rows[...], mine, theirs)
    mixer = product[:, :INNER]
    mixer_ref[...] = mixer
    attn_ref[...] = product[:, INNER:].astype(BF)
    norm = ssm[...] * silu_value(gating[...]) * root[...]
    together = mixer * norm
    along_ref[0] = exact(jnp.ones((8, INNER), F32), together * gain[...], (1, 1))

    @pl.when(pl.program_id(0) == 0)
    def _():
        gain_ref[...] = jnp.zeros_like(gain_ref)

    gain_ref[...] += jnp.sum(together, axis=0, keepdims=True)


def rows_back(scalars, gathered, weight, ssm, gating, root, gain):
    total, width = root.shape[0], 2 * gathered[0].shape[2]
    tiles = total // TILE
    return call(
        9.1,
        rows_back_kernel,
        (tiles,),
        gathered_specs(gathered)
        + [full(weight[0]), full(weight[1]), tiled(INNER), tiled(INNER), tiled(1), full(gain)],
        [
            tiled(INNER),
            tiled(HD),
            pl.BlockSpec((1, 8, TILE), lambda i, s: (i, 0, 0)),
            pl.BlockSpec((1, INNER), lambda i, s: (0, 0)),
        ],
        [
            shape((total, INNER)),
            shape((total, HD), BF),
            shape((tiles, 8, TILE)),
            shape((1, INNER)),
        ],
        [pltpu.VMEM((TILE, width), BF)],
        1,
    )(scalars, *gathered, *weight, ssm, gating, root, gain)


def back_dot_kernel(terms, halves, scalars, *refs):
    ins, outs = refs[: terms * 4], refs[terms * 4 :]
    i = pl.program_id(0)
    for half in range(2):
        product = None
        for t in range(terms):
            first, second = ins[4 * t], ins[4 * t + 1]
            weight = ins[4 * t + 2 + half]
            rows = jnp.concatenate([first[...], second[...]], 0)
            at = (1, 1) if weight.shape[1] == rows.shape[1] else (1, 0)
            one = dot(rows, weight[...], at)
            product = one if product is None else product + one
        product = product.reshape(outs[half].shape)

        @pl.when(i < halves)
        def _():
            outs[2 + half][...] = product.astype(BF)

        @pl.when(i >= halves)
        def _():
            outs[half][...] = product


def back_dot(order, terms):
    total = terms[0][0].shape[0]
    half = terms[0][1][0].shape[0]
    halves = total // TILE // 2
    specs, arrays = [], []
    for rows, weights in terms:
        width = rows.shape[1]
        specs += [
            pl.BlockSpec((BLOCK, width), lambda i, s: (s[(2 * i + 4) % 8], 0)),
            pl.BlockSpec((BLOCK, width), lambda i, s: (s[(2 * i + 5) % 8], 0)),
            full(weights[0]),
            full(weights[1]),
        ]
        arrays += [rows, rows, *weights]
    kept_spec = pl.BlockSpec((2, BLOCK, half), lambda i, s: (jnp.maximum(i - halves, 0), 0, 0))
    given_spec = pl.BlockSpec((2, BLOCK, half), lambda i, s: (jnp.minimum(i, halves - 1), 0, 0))
    blocks = total // BLOCK // 2
    return call(
        3 + 3 * len(terms),
        lambda *refs: back_dot_kernel(len(terms), halves, *refs),
        (2 * halves,),
        specs,
        [kept_spec, kept_spec, given_spec, given_spec],
        [shape((blocks, BLOCK, half))] * 2 + [shape((blocks, BLOCK, half), BF)] * 2,
        (),
        1,
    )(order, *arrays)


def grad_dot_kernel(scalars, own, other, against, *refs):
    out, ordered = refs[-2], refs[-1]

    @pl.when(pl.program_id(0) == 0)
    def _():
        for k in range(8):
            start = pl.multiple_of(scalars[k] * BLOCK, BLOCK)
            ordered[k * BLOCK : (k + 1) * BLOCK] = against[pl.ds(start, BLOCK), :]

    tile = own.shape[2]
    rows = own.shape[0] * own.shape[1]
    product = dot(own[...].reshape(rows, tile), ordered[:rows], (0, 0))
    product = product + dot(other[...].reshape(rows, tile), ordered[rows:], (0, 0))
    out[...] = product.astype(out.dtype)


def grad_dot(order, parts, against, dtype):
    total, width = against.shape
    blocks = total // BLOCK // 2
    tile = 512
    half = parts[0][3]
    specs = [
        pl.BlockSpec((blocks, BLOCK, tile), lambda i, s, at=at, off=off: (at, 0, i + off // tile))
        for _, at, off, _ in parts
    ]
    return call(
        3.1,
        grad_dot_kernel,
        (half // tile,),
        [*specs, full(against)],
        pl.BlockSpec((tile, width), lambda i, s: (i, 0)),
        shape((half, width), dtype),
        [pltpu.VMEM((total, width), BF)],
        1,
    )(order, *(array for array, _, _, _ in parts), against)


def gathered_halves(gathered):
    left, right, left_other, right_other = gathered
    half = left.shape[2]
    return [(left, 0, 0, half), (left_other, 0, 0, half)], [
        (right, 0, 0, half),
        (right_other, 0, 0, half),
    ]


def straight_halves(rows):
    total, width = rows.shape
    rows = rows.reshape(total // BLOCK, BLOCK, width)
    half = width // 2
    return [(rows, 0, 0, half), (rows, 1, 0, half)], [(rows, 0, half, half), (rows, 1, half, half)]


def feed_grads_kernel(order, l, r, lo, ro, cotangent, active, gate, lift, *refs):
    mine, theirs, (gate_rows, lift_rows) = refs[:3], refs[3:6], refs[6:]
    i = pl.program_id(0)

    @pl.when(i == 0)
    def _():
        for k in range(8):
            start = pl.multiple_of(order[k] * BLOCK, BLOCK)
            gate_rows[k * BLOCK : (k + 1) * BLOCK] = gate[pl.ds(start, BLOCK), :]
            lift_rows[k * BLOCK : (k + 1) * BLOCK] = lift[pl.ds(start, BLOCK), :]

    def run(own, other, out):
        tile = own.shape[2]
        rows = own.shape[0] * own.shape[1]
        own, other = own[...].reshape(rows, tile), other[...].reshape(rows, tile)
        for at, against in ((0, gate_rows), (1, lift_rows)):
            product = dot(own, against[:rows], (0, 0)) + dot(other, against[rows:], (0, 0))
            out[at][...] = product.astype(BF)
        out[2][...] = dot(cotangent[...], active[...], (0, 0)).astype(BF)

    @pl.when(i < pl.num_programs(0) // 2)
    def _():
        run(r, ro, theirs)

    @pl.when(i >= pl.num_programs(0) // 2)
    def _():
        run(l, lo, mine)


def feed_grads(order, gathered, cotangent, active, gate, lift):
    total, width = cotangent.shape
    tile = 512
    tiles = width // tile
    half = tiles // 2
    dims = gathered[0].shape[:2] + (tile,)
    right = pl.BlockSpec(dims, lambda i, s: (0, 0, jnp.minimum(i, half - 1)))
    left = pl.BlockSpec(dims, lambda i, s: (0, 0, jnp.maximum(i - half, 0)))
    return call(
        13,
        feed_grads_kernel,
        (tiles,),
        [left, right, left, right, pl.BlockSpec((total, tile), lambda i, s: (0, (i + half) % tiles))]
        + [full(x) for x in (active, gate, lift)],
        [
            *[pl.BlockSpec((tile, LANES), lambda i, s: (jnp.maximum(i - half, 0), 0))] * 3,
            *[pl.BlockSpec((tile, LANES), lambda i, s: (jnp.minimum(i, half - 1), 0))] * 3,
        ],
        [shape((width // 2, LANES), BF)] * 6,
        [pltpu.VMEM((total, LANES), BF)] * 2,
        1,
    )(order, *gathered, cotangent, active, gate, lift)


def grad_halves(order, halves, against):
    theirs = grad_dot(order, halves[1], against, BF)
    return grad_dot(order, halves[0], against, F32), theirs


def feed_kernel(scalars, l, r, lo, ro, cotangent, gm, gt, lm, lt, dm, dt, active_ref, gate_ref, lift_ref, rows):
    place_rows(scalars, (l, r, lo, ro), rows)
    values = rows[...]
    gate = halves_product(values, gm, gt)
    lift = halves_product(values, lm, lt)
    grad = halves_product(cotangent[...], dm, dt)
    sigmoid_part = jax.nn.sigmoid(gate)
    swish = gate * sigmoid_part
    active_ref[...] = (swish * lift).astype(BF)
    gate_ref[...] = (grad * lift * sigmoid_part * (1.0 + gate * (1.0 - sigmoid_part))).astype(BF)
    lift_ref[...] = (grad * swish).astype(BF)


def feed_block(scalars, gathered, cotangent, gate, lift, drop):
    total, width = cotangent.shape
    weights = [*gate, *lift, *drop]
    return call(
        11.8,
        feed_kernel,
        (total // TILE,),
        gathered_specs(gathered) + [tiled(width)] + [full(w) for w in weights],
        [tiled(LANES)] * 3,
        [shape((total, LANES), BF)] * 3,
        [pltpu.VMEM((TILE, width), BF)],
        1,
    )(scalars, *gathered, cotangent, *weights)


def forth_dot_kernel(rows, mine, theirs, out):
    half = mine.shape[0]
    out[:, :half] = dot(rows[...], mine[...], (1, 1)).astype(BF)
    out[:, half:] = dot(rows[...], theirs[...], (1, 1)).astype(BF)


def forth_dot(rows, weights):
    total, k = rows.shape
    width = 2 * weights[0].shape[0]
    return call(
        4.4,
        forth_dot_kernel,
        (total // TILE,),
        [tiled(k), full(weights[0]), full(weights[1])],
        tiled(width),
        shape((total, width), BF),
    )(rows, *weights)


def keys_kernel(seqs, parts, out):
    for n in range(seqs):
        out[n] = jnp.concatenate([parts[r][:, n * SIDE : (n + 1) * SIDE] for r in range(4)], 1)


def keys_of(seqs, parts):
    count = parts.shape[1]
    return call(
        1.7,
        lambda *refs: keys_kernel(seqs, *refs),
        (count // TILE,),
        [pl.BlockSpec((4, TILE, seqs * SIDE), lambda i: (0, i, 0))],
        pl.BlockSpec((seqs, TILE, 2 * HD), lambda i: (0, i, 0)),
        shape((seqs, count, 2 * HD), BF),
    )(parts)


def scores_of(place, queries, keys):
    count, whole = queries.shape[0], keys.shape[0]
    scores = dot(queries, keys, (1, 1)) * HD**-0.5
    row = place + pl.program_id(1) * count + lax.broadcasted_iota(jnp.int32, (count, whole), 0)
    column = lax.broadcasted_iota(jnp.int32, (count, whole), 1)
    return scores, row >= column


def attend_kernel(place, queries, key_value, out_ref, log_ref):
    keys, values = key_value[0, :, :HD], key_value[0, :, HD:]
    scores, visible = scores_of(place[0], queries[...], keys)
    scores = jnp.where(visible, scores, negative)
    top = jnp.max(scores, axis=-1, keepdims=True)
    weights = jnp.exp(scores - top)
    total = jnp.sum(weights, axis=-1, keepdims=True)
    log_ref[...] = top + jnp.log(total)
    out_ref[...] = dot(weights.astype(BF), values, (1, 0)) / total


def attend_specs(seqs, total):
    tiles = total // TILE // seqs
    rows = lambda width: pl.BlockSpec((TILE, width), lambda n, i, s: (n * tiles + i, 0))
    return (seqs, tiles), rows


def attend(place, queries, key_value):
    seqs, whole, width = key_value.shape
    total = queries.shape[0]
    grid, rows = attend_specs(seqs, total)
    return call(
        2.8,
        attend_kernel,
        grid,
        [rows(HD), pl.BlockSpec((1, whole, width), lambda n, i, s: (n, 0, 0))],
        [rows(HD), rows(1)],
        [shape((total, HD)), shape((total, 1))],
        (),
        1,
    )(place, queries, key_value)


def attend_back_kernel(place, queries, grads, attended, logs, root, key_value, query_ref, sum_ref):
    keys, values = key_value[0, :, :HD], key_value[0, :, HD:]
    scores, visible = scores_of(place[0], queries[...], keys)
    probs = jnp.where(visible, jnp.exp(scores - logs[...]), 0.0)
    grad = grads[...]
    delta = jnp.sum(grad.astype(F32) * attended[...], axis=-1, keepdims=True)
    scores_grad = (probs * (dot(grad, values, (1, 1)) - delta)).astype(BF)
    query_ref[...] = (dot(scores_grad, keys, (1, 0)) * (HD**-0.5 * root[...])).astype(BF)

    @pl.when((pl.program_id(0) == 0) & (pl.program_id(1) == 0))
    def _():
        sum_ref[...] = jnp.zeros_like(sum_ref)

    key_sum = dot(scores_grad, queries[...], (0, 0)) * HD**-0.5
    value_sum = dot(probs.astype(BF), grad, (0, 0))
    for n in range(sum_ref.shape[2] // SIDE):

        @pl.when(pl.program_id(0) == n)
        def _():
            at = slice(n * SIDE, (n + 1) * SIDE)
            sum_ref[0, :, at] += key_sum[:, :SIDE]
            sum_ref[1, :, at] += key_sum[:, SIDE:]
            sum_ref[2, :, at] += value_sum[:, :SIDE]
            sum_ref[3, :, at] += value_sum[:, SIDE:]


def attend_back(place, queries, grads, attended, logs, root, key_value):
    seqs, whole, width = key_value.shape
    total = queries.shape[0]
    grid, rows = attend_specs(seqs, total)
    sums = pl.BlockSpec((1, whole, width), lambda n, i, s: (n, 0, 0))
    return call(
        6.4,
        attend_back_kernel,
        grid,
        [rows(HD), rows(HD), rows(HD), rows(1), rows(1), sums],
        [rows(HD), pl.BlockSpec((4, whole, seqs * SIDE), lambda n, i, s: (0, 0, 0))],
        [shape((total, HD), BF), shape((4, whole, seqs * SIDE))],
        (),
        1,
    )(place, queries, grads, attended, logs, root, key_value)


def over_heads(values):
    rows = values.shape[0]
    return jnp.concatenate(
        [jnp.broadcast_to(values[:, h : h + 1], (rows, PM)) for h in range(HEADS)], 1
    )


def head_sums(values):
    channel = lax.broadcasted_iota(jnp.int32, (INNER, 8), 0)
    head = lax.broadcasted_iota(jnp.int32, (INNER, 8), 1)
    return exact(values, jnp.where(channel // PM == head, 1.0, 0.0), (1, 0))


def triangle():
    row = lax.broadcasted_iota(jnp.int32, (BLOCK, BLOCK), 0)
    column = lax.broadcasted_iota(jnp.int32, (BLOCK, BLOCK), 1)
    return row, column


def block_steps(step_pre, head):
    arg = step_pre + head[0:1, :]
    size = jnp.maximum(arg, 0.0) + jnp.log1p(jnp.exp(-jnp.abs(arg)))
    row, column = triangle()
    cum = exact(jnp.where(row >= column, 1.0, 0.0), size * head[1:2, :], (1, 0))
    return arg, size, cum


def as_rows(values):
    row, column = triangle()
    return exact(values, jnp.where(row == column, 1.0, 0.0), (0, 0))


def as_columns(values):
    row, column = triangle()
    return exact(jnp.where(row == column, 1.0, 0.0), values, (1, 1))


def joined(sides, first, n):
    return jnp.concatenate(
        [sides[r][:, n * SIDE : (n + 1) * SIDE] for r in range(first, first + 4)], 1
    )


def pair(seqs, width, back=0):
    if back:
        return pl.BlockSpec((seqs, BLOCK, width), lambda i, *s: (0, back - 1 - i, 0))
    return pl.BlockSpec((seqs, BLOCK, width), lambda i, *s: (0, i, 0))


def by_seq(seqs, *arrays):
    return [a.reshape(*a.shape[:-2], seqs, -1, a.shape[-1]) for a in arrays]


def states_kernel(seqs, blocks, step_pre, head, conv, sides, out_ref, decay_ref, run):
    i = pl.program_id(0)

    @pl.when(i == 0)
    def _():
        run[...] = jnp.zeros_like(run)
        decay_ref[...] = jnp.ones_like(decay_ref)

    for n in range(seqs):
        _, size, cum = block_steps(step_pre[n], head)
        last = cum[BLOCK - 1 :, :]
        feeding = jnp.exp(last - cum) * size
        inner = silu_value(conv[n, :, :INNER])
        in_state = joined(sides, 0, n)
        fresh = dot(in_state, (over_heads(feeding) * inner).astype(BF), (0, 0))
        decay = over_heads(jnp.exp(last))
        run[n] = decay * run[n] + fresh
        decay_ref[n] = decay_ref[n] * decay

    @pl.when(i == blocks - 1)
    def _():
        out_ref[...] = run[...].astype(BF)


def states(seqs, step_pre, head, conv, sides):
    step_pre, conv = by_seq(seqs, step_pre, conv)
    blocks = conv.shape[1] // BLOCK
    return call(
        4.2,
        lambda *refs: states_kernel(seqs, blocks, *refs),
        (blocks,),
        [
            pair(seqs, 8),
            full(head),
            pair(seqs, LANES),
            pl.BlockSpec((4, BLOCK, seqs * SIDE), lambda i: (0, i, 0)),
        ],
        [
            pl.BlockSpec((seqs, NS, INNER), lambda i: (0, 0, 0)),
            pl.BlockSpec((seqs, 1, INNER), lambda i: (0, 0, 0)),
        ],
        [shape((seqs, NS, INNER), BF), shape((seqs, 1, INNER))],
        [pltpu.VMEM((seqs, NS, INNER), F32)],
    )(step_pre, head, conv, sides)


def fading_of(cum, cum_rows, h):
    row, column = triangle()
    span = cum[:, h : h + 1] - cum_rows[h : h + 1, :]
    return jnp.where(row >= column, jnp.exp(jnp.minimum(span, 0.0)), 0.0)


def ssm_kernel(seqs, step_pre, head, conv, sides, gating, entry, ssm_ref, carried_ref, square_ref, run):
    @pl.when(pl.program_id(0) == 0)
    def _():
        run[...] = entry[...].astype(F32)

    for n in range(seqs):
        _, size, cum = block_steps(step_pre[n], head)
        size_rows, cum_rows = as_rows(size), as_rows(cum)
        last = cum[BLOCK - 1 :, :]
        inner = silu_value(conv[n, :, :INNER])
        inner_low = inner.astype(BF)
        in_state, out_state = joined(sides, 0, n), joined(sides, 4, n)
        before = run[n]
        carried = before.astype(BF)
        carried_ref[n, 0] = carried
        pairing = dot(out_state, in_state, (1, 1))
        within = []
        for h in range(HEADS):
            mixing = fading_of(cum, cum_rows, h) * pairing * size_rows[h : h + 1, :]
            within.append(dot(mixing.astype(BF), inner_low[:, h * PM : (h + 1) * PM], (1, 0)))
        readout = dot(out_state, carried, (1, 0))
        ssm = (
            jnp.concatenate(within, 1)
            + over_heads(jnp.exp(cum)) * readout
            + over_heads(head[2:3, :]) * inner
        )
        ssm_ref[n] = ssm
        gated = ssm * silu_value(gating[n])
        square_ref[0, n] = exact(jnp.ones((8, INNER), F32), gated * gated, (1, 1))
        feeding = jnp.exp(last - cum) * size
        fresh = dot(in_state, (over_heads(feeding) * inner).astype(BF), (0, 0))
        run[n] = over_heads(jnp.exp(last)) * before + fresh


def ssm_block(seqs, step_pre, head, conv, sides, gating, entry):
    total = conv.shape[0]
    step_pre, conv, gating = by_seq(seqs, step_pre, conv, gating)
    count = conv.shape[1]
    blocks = count // BLOCK
    ssm, carried, square = call(
        10.8,
        lambda *refs: ssm_kernel(seqs, *refs),
        (blocks,),
        [
            pair(seqs, 8),
            full(head),
            pair(seqs, LANES),
            pl.BlockSpec((RANKS, BLOCK, seqs * SIDE), lambda i: (0, i, 0)),
            pair(seqs, INNER),
            full(entry),
        ],
        [
            pair(seqs, INNER),
            pl.BlockSpec((seqs, 1, NS, INNER), lambda i: (0, i, 0, 0)),
            pl.BlockSpec((1, seqs, 8, BLOCK), lambda i: (i, 0, 0, 0)),
        ],
        [
            shape((seqs, count, INNER)),
            shape((seqs, blocks, NS, INNER), BF),
            shape((blocks, seqs, 8, BLOCK)),
        ],
        [pltpu.VMEM((seqs, NS, INNER), F32)],
    )(step_pre, head, conv, sides, gating, entry)
    square = square[:, :, 0].swapaxes(0, 1).reshape(total // BLOCK, BLOCK)
    return ssm.reshape(total, INNER), carried, square


def states_back_kernel(seqs, blocks, step_pre, head, sides, mixer, ssm, gating, mixer_root, along, gain, root, grad_ref, gating_ref, out_ref, run):
    i = pl.program_id(0)

    @pl.when(i == 0)
    def _():
        run[...] = jnp.zeros_like(run)

    for n in range(seqs):
        _, _, cum = block_steps(step_pre[n], head)
        gate = gating[n]
        sigmoid_part = jax.nn.sigmoid(gate)
        act = gate * sigmoid_part
        values = ssm[n]
        scaled = mixer_root[n]
        norm = values * act * scaled
        gated_grad = scaled * (mixer[n] * gain[...] - norm * along[n])
        grad = gated_grad * act
        grad_ref[n] = grad
        slope = sigmoid_part * (1.0 + gate * (1.0 - sigmoid_part))
        gating_ref[n] = (gated_grad * values * slope * root[n]).astype(BF)
        grown = (over_heads(jnp.exp(cum)) * grad).astype(BF)
        fresh = dot(joined(sides, 0, n), grown, (0, 0))
        run[n] = over_heads(jnp.exp(cum[BLOCK - 1 :, :])) * run[n] + fresh

    @pl.when(i == blocks - 1)
    def _():
        out_ref[...] = run[...].astype(BF)


def states_back(seqs, step_pre, head, sides, mixer, ssm, gating, mixer_root, along, gain, root):
    total = ssm.shape[0]
    step_pre, mixer, ssm, gating, mixer_root, along, root = by_seq(
        seqs, step_pre, mixer, ssm, gating, mixer_root, along, root
    )
    count = ssm.shape[1]
    blocks = count // BLOCK
    back = lambda width: pair(seqs, width, blocks)
    grad, gating_grad, leaving = call(
        5.7,
        lambda *refs: states_back_kernel(seqs, blocks, *refs),
        (blocks,),
        [back(8), full(head)]
        + [pl.BlockSpec((4, BLOCK, seqs * SIDE), lambda i: (1, blocks - 1 - i, 0))]
        + [back(INNER), back(INNER), back(INNER), back(1), back(1), full(gain), back(1)],
        [back(INNER), back(INNER), pl.BlockSpec((seqs, NS, INNER), lambda i: (0, 0, 0))],
        [
            shape((seqs, count, INNER)),
            shape((seqs, count, INNER), BF),
            shape((seqs, NS, INNER), BF),
        ],
        [pltpu.VMEM((seqs, NS, INNER), F32)],
    )(step_pre, head, sides, mixer, ssm, gating, mixer_root, along, gain, root)
    return grad.reshape(total, INNER), gating_grad.reshape(total, INNER), leaving


def ssm_back_one(n, step_pre, head, conv, sides, grads, carried_ref, root, conv_ref, step_ref, sums_ref, later):
    arg, size, cum = block_steps(step_pre[n], head)
    size_rows, cum_rows = as_rows(size), as_rows(cum)
    last = cum[BLOCK - 1 :, :]
    growth, to_end, decay = jnp.exp(cum), jnp.exp(last - cum), jnp.exp(last)
    feeding = to_end * size
    conv_sum = conv[n, :, :INNER]
    inner = silu_value(conv_sum)
    inner_low = inner.astype(BF)
    in_state, out_state = joined(sides, 0, n), joined(sides, 4, n)
    carried = carried_ref[n, 0]
    after = later[n]
    after_low = after.astype(BF)
    grad = grads[n]
    grad_low = grad.astype(BF)
    pairing = dot(out_state, in_state, (1, 1))
    readout = dot(out_state, carried, (1, 0))
    spread = dot(in_state, after_low, (1, 0))
    grown = (over_heads(growth) * grad).astype(BF)
    feeding_wide = over_heads(feeding)
    fed_inner = (feeding_wide * inner).astype(BF)
    pairing_grad = jnp.zeros((BLOCK, BLOCK), F32)
    inner_parts, flows, step_rows = [], [], []
    for h in range(HEADS):
        at = slice(h * PM, (h + 1) * PM)
        fading = fading_of(cum, cum_rows, h)
        sized = size_rows[h : h + 1, :]
        mixing = (fading * pairing * sized).astype(BF)
        faded = dot(grad_low[:, at], inner_low[:, at], (1, 1)) * fading
        pairing_grad = pairing_grad + faded * sized
        stepwise = faded * pairing
        step_rows.append(jnp.sum(stepwise, axis=0, keepdims=True))
        flows.append(jnp.sum(stepwise * sized, axis=1, keepdims=True))
        inner_parts.append(dot(mixing, grad_low[:, at], (0, 0)))
    empty_row, empty_column = jnp.zeros((2, BLOCK), F32), jnp.zeros((BLOCK, 2), F32)
    step_rows = jnp.concatenate(step_rows + [empty_row], 0)
    flow = jnp.concatenate(flows + [empty_column], 1)
    pairing_low = pairing_grad.astype(BF)
    out_grad = dot(pairing_low, in_state, (1, 0)) + dot(grown, carried, (1, 1))
    in_grad = dot(pairing_low, out_state, (0, 0)) + dot(fed_inner, after_low, (1, 1))
    inner_grad = (
        jnp.concatenate(inner_parts, 1) + over_heads(head[2:3, :]) * grad + feeding_wide * spread
    )
    conv_ref[n] = inner_grad * silu_slope(conv_sum)
    feeding_grad = head_sums(spread * inner)
    fed = feeding_grad * feeding
    through = jnp.sum(after * carried.astype(F32), axis=0, keepdims=True)
    through = head_sums(jnp.broadcast_to(through, (8, INNER)))[:1]
    last_grad = jnp.sum(fed, axis=0, keepdims=True) + through * decay
    cum_grad = flow - as_columns(step_rows * size_rows) + head_sums(grad * readout) * growth - fed
    row, column = triangle()
    increment = exact(jnp.where(column >= row, 1.0, 0.0), cum_grad, (1, 0)) + last_grad
    rates = head[1:2, :]
    step_grad = as_columns(step_rows) + feeding_grad * to_end + increment * rates
    arg_grad = step_grad * jax.nn.sigmoid(arg)
    step_ref[n] = (arg_grad * root[n]).astype(BF)
    skip = jnp.broadcast_to(jnp.sum(grad * inner, axis=0, keepdims=True), (8, INNER))
    sums_ref[0:1, :] += jnp.sum(arg_grad, axis=0, keepdims=True)
    sums_ref[1:2, :] += jnp.sum(increment * size, axis=0, keepdims=True) * rates
    sums_ref[2:3, :] += head_sums(skip)[:1]
    later[n] = over_heads(decay) * after + dot(out_state, grown, (0, 0))
    return in_grad, out_grad


def ssm_back_kernel(seqs, step_pre, head, conv, sides, grads, carried, entry, root, conv_ref, parts_ref, step_ref, sums_ref, later):
    @pl.when(pl.program_id(0) == 0)
    def _():
        later[...] = entry[...].astype(F32)
        sums_ref[...] = jnp.zeros_like(sums_ref)

    grad_pairs = [
        ssm_back_one(
            n, step_pre, head, conv, sides, grads, carried, root, conv_ref, step_ref, sums_ref, later
        )
        for n in range(seqs)
    ]
    for rank in range(RANKS):
        at = (rank % 4) * SIDE
        parts_ref[rank] = jnp.concatenate(
            [grad[rank // 4][:, at : at + SIDE] for grad in grad_pairs], 1
        ).astype(BF)


def ssm_back(seqs, step_pre, head, conv, sides, grads, carried, entry, root):
    total = conv.shape[0]
    step_pre, conv, grads, root = by_seq(seqs, step_pre, conv, grads, root)
    count = conv.shape[1]
    blocks = count // BLOCK
    back = lambda width: pair(seqs, width, blocks)
    conv_grad, parts, step_rows, sums = call(
        18.8,
        lambda *refs: ssm_back_kernel(seqs, *refs),
        (blocks,),
        [
            back(8),
            full(head),
            back(LANES),
            pl.BlockSpec((RANKS, BLOCK, seqs * SIDE), lambda i: (0, blocks - 1 - i, 0)),
            back(INNER),
            pl.BlockSpec((seqs, 1, NS, INNER), lambda i: (0, blocks - 1 - i, 0, 0)),
            full(entry),
            back(1),
        ],
        [
            back(INNER),
            pl.BlockSpec((RANKS, BLOCK, seqs * SIDE), lambda i: (0, blocks - 1 - i, 0)),
            back(8),
            pl.BlockSpec((8, 8), lambda i: (0, 0)),
        ],
        [
            shape((seqs, count, INNER)),
            shape((RANKS, count, seqs * SIDE), BF),
            shape((seqs, count, 8), BF),
            shape((8, 8)),
        ],
        [pltpu.VMEM((seqs, NS, INNER), F32)],
    )(step_pre, head, conv, sides, grads, carried, entry, root)
    return conv_grad.reshape(total, INNER), parts, step_rows.reshape(total, 8), sums


def conv_back_kernel(tiles, inner, parts, keys, conv, pre, edge, grad_ref, sums_ref, line):
    i = pl.program_id(0)
    first = i < tiles
    got = jnp.sum(parts[...].astype(F32), axis=0)
    got = jnp.where(first, got[:, :SIDE], got[:, SIDE:]) * silu_slope(conv[:, INNER:CONV])
    keys_got = keys[...]
    keys_got = jnp.where(first, keys_got[:, :SIDE], keys_got[:, SIDE:])
    got = jnp.concatenate([got, keys_got], 1)
    grad = jnp.concatenate([inner[...], got], 1)
    grad_ref[...] = grad

    @pl.when(i % tiles == 0)
    def _():
        line[:EDGE] = edge[0]

    @pl.when(i % tiles != 0)
    def _():
        line[:EDGE] = line[TILE:]

    @pl.when(i == 0)
    def _():
        sums_ref[...] = jnp.zeros_like(sums_ref)

    line[EDGE:] = pre[...]
    for k in range(KC):
        before = line[EDGE - (KC - 1) + k : EDGE - (KC - 1) + k + TILE, :]
        sums_ref[k : k + 1, :] += jnp.sum(grad * before, axis=0, keepdims=True)
    sums_ref[KC : KC + 1, :] += jnp.sum(grad, axis=0, keepdims=True)


def conv_back(inner, parts, keys, conv, pre, edge):
    total = conv.shape[0]
    tiles = total // TILE // edge.shape[0]
    return call(
        4.8,
        lambda *refs: conv_back_kernel(tiles, *refs),
        (total // TILE,),
        [
            tiled(INNER),
            pl.BlockSpec((RANKS, TILE, 2 * SIDE), lambda i: (0, i % tiles, 0)),
            pl.BlockSpec((TILE, 2 * SIDE), lambda i: (i % tiles, 0)),
            tiled(LANES),
            tiled(LANES),
            pl.BlockSpec((1, EDGE, LANES), lambda i: (i // tiles, 0, 0)),
        ],
        [tiled(LANES), pl.BlockSpec((8, LANES), lambda i: (0, 0))],
        [shape((total, LANES)), shape((8, LANES))],
        [pltpu.VMEM((EDGE + TILE, LANES), F32)],
    )(inner, parts, keys, conv, pre, edge)


def pre_back_kernel(tiles, grad, after, follow, taps, root, out_ref, line):
    i = pl.program_id(0)
    line[:TILE] = grad[...]

    @pl.when(i % tiles == tiles - 1)
    def _():
        line[TILE:] = follow[0]

    @pl.when(i % tiles != tiles - 1)
    def _():
        line[TILE:] = after[...]

    total = taps[KC - 1 : KC, :] * line[:TILE, :]
    for k in range(KC - 1):
        total = total + taps[k : k + 1, :] * line[KC - 1 - k : KC - 1 - k + TILE, :]
    out_ref[...] = (total * root[...]).astype(BF)


def pre_back(grad, follow, taps, root):
    total = grad.shape[0]
    tiles = total // TILE // follow.shape[0]
    last = total // EDGE - 1
    return call(
        1.4,
        lambda *refs: pre_back_kernel(tiles, *refs),
        (total // TILE,),
        [
            tiled(LANES),
            pl.BlockSpec((EDGE, LANES), lambda i: (jnp.minimum((i + 1) * (TILE // EDGE), last), 0)),
            pl.BlockSpec((1, EDGE, LANES), lambda i: (i // tiles, 0, 0)),
            full(taps),
            tiled(1),
        ],
        tiled(LANES),
        shape((total, LANES), BF),
        [pltpu.VMEM((TILE + EDGE, LANES), F32)],
    )(grad, grad, follow, taps, root)


def local(
    tokens,
    cotangent,
    norm_gain,
    gating_weight,
    inner_weight,
    state_weight,
    step_weight,
    conv_weight,
    conv_bias,
    mixer_gain,
    mixer_out,
    query_weight,
    key_weight,
    value_weight,
    output_weight,
    feed_gain,
    gate_matrix,
    lift_matrix,
    drop_matrix,
    step_bias,
    decay_log,
    skip_scale,
):
    sh, sl, ch = lax.axis_size("sh"), lax.axis_size("sl"), lax.axis_size("ch")
    world = sh * sl * ch * 4
    rows, width = tokens.shape
    drows = norm_gain.shape[0]
    my_sl, my_zl, my_core = (lax.axis_index(axis) for axis in TEAM)
    rank = (my_sl * 2 + my_zl) * 2 + my_core
    total = RANKS * rows
    count = 4 * rows
    whole = ch * count

    order = team_order()
    straight = jnp.arange(8, dtype=jnp.int32)
    tiles = [((z ^ my_zl) * 2 + (s ^ my_sl)) for s in (0, 1) for z in (0, 1)]
    scalars = jnp.stack([my_core, *tiles]).astype(jnp.int32)
    place = (lax.axis_index("ch") * count).astype(jnp.int32).reshape(1)
    dims = (sh, sl, ch, width)
    home = column_blocks(sh, sl, ch)
    nowhere = jnp.zeros_like(home)

    def scaled(weight, gain):
        return (weight.astype(F32) * gain.astype(F32)[:, None]).astype(BF)

    key_value = jnp.stack(
        [key_weight.reshape(drows, HK, 2, SIDE), value_weight.reshape(drows, HK, 2, SIDE)], 2
    ).reshape(drows, RANKS * SIDE)
    pack_in = jnp.concatenate(
        [
            by_rank(scaled(w, norm_gain))
            for w in (inner_weight, state_weight, key_value, gating_weight, query_weight)
        ],
        2,
    )
    conv_own, gain_own = conv_weight.shape[1], mixer_gain.shape[0]
    step_sent = jnp.broadcast_to(
        scaled(step_weight, norm_gain).T.reshape(1, sl, 1, 4, HEADS * drows),
        (sh, sl, ch, 4, HEADS * drows),
    ).reshape(world, HEADS * drows)
    shared = jnp.concatenate([conv_weight.reshape(-1), conv_bias, mixer_gain])
    small = jnp.concatenate(
        [jnp.broadcast_to(shared[None], (world, shared.shape[0])), step_sent], 1
    )
    with jax.named_scope("small_exchange"):
        small = lax.all_to_all(small, WORLD, split_axis=0, concat_axis=0, tiled=True)
    small, pack_in = together(small, pack_in)
    with jax.named_scope("weights_in"):
        mixed_in = ranks_exchange(pack_in)
    *own_tokens, own_cotangent = arrive(dims, home, tokens, cotangent)
    with jax.named_scope("tokens_gather"):
        team_tokens = list(team_gather(*own_tokens))
    last = 4
    ends = []
    for seq in range(sl):
        at_block = 2 * (1 - my_zl) + (seq ^ my_sl)
        halves = []
        for own, other in ((team_tokens[0], team_tokens[2]), (team_tokens[1], team_tokens[3])):
            own = lax.dynamic_index_in_dim(own[:, rows - last :], at_block, 0, False)
            other = lax.dynamic_index_in_dim(other[:, rows - last :], at_block, 0, False)
            halves.append(jnp.where(my_core == 1, own, other))
        ends.append(jnp.concatenate(halves, 1))
    halo = jnp.stack(ends)
    with jax.named_scope("weights_first"):
        if ch == 2:
            first = mixed_in[:, :LANES]
            got = swap(jnp.concatenate([first, halo.reshape(-1, LANES)], 0), "ch")
            ready = jnp.concatenate([first, got[: first.shape[0]]], 0)
            halo = got[first.shape[0] :].reshape(sl, last, sh, ch, -1)
            halo = jnp.flip(halo, 3).reshape(sl, last, width)
            halo = jnp.where(lax.axis_index("ch") == 0, jnp.zeros_like(halo), halo)
        else:
            ready = along_ch(mixed_in[:, :LANES])
            halo = shifted(halo, 1)
        halo = jnp.pad(halo, ((0, 0), (EDGE - last, 0), (0, 0)))
    pack_rest = jnp.concatenate(
        [by_rank(mixer_out.T), by_rank(output_weight.T)]
        + [by_rank(scaled(w, feed_gain)) for w in (gate_matrix, lift_matrix)]
        + [by_rank(drop_matrix.T)],
        2,
    )
    pack_rest, *team_tokens = together(pack_rest, *team_tokens)
    with jax.named_scope("weights_rest"):
        mixed_rest = ranks_exchange(pack_rest)
    with jax.named_scope("weights_inner"):
        theirs, gating_ready = together(swap(ready, "sh"), along_ch(mixed_in[:, LANES:]))
    w_inner = (ready, theirs)

    at = (KC + 1) * conv_own
    wide_conv = small[:, :at].reshape(world, KC + 1, conv_own)
    wide_conv = wide_conv.transpose(1, 0, 2).reshape(KC + 1, -1).astype(F32)
    wide_gain = small[:, at : at + gain_own].reshape(1, -1).astype(F32)
    own_step = small[:, at + gain_own :].reshape(sh, sl, ch, 4, HEADS, drows).swapaxes(1, 2)
    own_step = relative(relative(own_step, "sh", 0), "ch", 1)
    own_step = own_step.reshape(-1, HEADS, drows).swapaxes(0, 1).reshape(HEADS, width)
    own_step = jnp.pad(own_step, ((0, 8 - HEADS), (0, 0)))
    taps = jnp.concatenate(
        [
            lax.dynamic_slice_in_dim(wide_conv, rank * INNER, INNER, 1),
            lax.dynamic_slice_in_dim(wide_conv, DI + rank * SIDE, SIDE, 1),
            jnp.zeros((KC + 1, LANES - CONV), F32).at[KC - 1].set(1.0),
        ],
        1,
    )
    taps = jnp.pad(taps, ((0, 8 - KC - 1), (0, 0)))
    own_gain = lax.dynamic_slice_in_dim(wide_gain, rank * INNER, INNER, 1)
    head = jnp.stack([step_bias, -jnp.exp(decay_log), skip_scale])
    head = lax.dynamic_slice_in_dim(head, rank * HEADS, HEADS, 1)
    head = jnp.pad(head, ((0, 5), (0, 8 - HEADS)))

    pre, conv, side, own_keys, step_pre, root, edge = project_inner(
        scalars, team_tokens, w_inner, halo, taps, own_step
    )
    def packed(values):
        return values.reshape(sl, count, SIDE).swapaxes(0, 1).reshape(count, sl * SIDE)

    sides = lax.all_gather(packed(side), TEAM)
    sent_cotangent, sides = together(own_cotangent, sides)
    team_cotangent = lax.all_gather(sent_cotangent, TEAM, axis=0, tiled=True)
    with jax.named_scope("keys_exchange"):
        own_keys = packed(own_keys)[None]
        if ch == 2:
            own_keys = paired(own_keys[0], swap(own_keys[0], "ch"), "ch", 0)
        elif ch > 2:
            own_keys = lax.all_gather(own_keys[0], "ch")
        own_keys = paired(own_keys, swap(own_keys, "zl"), "zl", 0)
        own_keys = paired(own_keys, swap(own_keys, "core"), "core", 1)
        key_value_rows = keys_of(sl, own_keys.reshape(4, whole, sl * SIDE))
    with jax.named_scope("weights_gating"):
        theirs, out_ready = together(
            swap(gating_ready, "sh"), along_ch(mixed_rest[:, :LANES])
        )
    w_gating = (gating_ready, theirs)
    gating, queries = project_gating(scalars, team_tokens, w_gating, root)
    with jax.named_scope("weights_out"):
        w_out = (out_ready, swap(out_ready, "sh"))
    sides, gating = together(sides, gating)
    leaving, piece_decay = states(sl, step_pre, head, conv, sides)
    with jax.named_scope("state_exchange"):
        entry = entering(piece_decay[:, 0], leaving, False)
    entry, mixed_rest = together(entry, mixed_rest)
    rest = [mixed_rest[:, at * LANES : (at + 1) * LANES] for at in range(1, 4)]
    with jax.named_scope("weights_gate_first"):
        gate_ready = along_ch(rest[0])
    attended, logs = attend(place, queries, key_value_rows)
    ssm, carried, square = ssm_block(sl, step_pre, head, conv, sides, gating, entry)
    with jax.named_scope("square_sum"):
        square = team_sum(square)
    mixer_root = lax.rsqrt(square / DI + epsilon).reshape(total, 1)
    branch_rows = jnp.concatenate(
        [(ssm * silu_value(gating) * mixer_root * own_gain).astype(BF), attended.astype(BF)], 1
    )
    branch_rows, gate_ready, rest[1] = together(branch_rows, gate_ready, rest[1])
    with jax.named_scope("weights_gate"):
        theirs, lift_ready = together(swap(gate_ready, "sh"), along_ch(rest[1]))
    w_gate = (gate_ready, theirs)
    branch_parts = back_dot(order, [(branch_rows, w_out)])
    with jax.named_scope("branch_scatter"):
        branch = scatter_core(branch_parts)
    lift_ready, rest[2], *branch = together(lift_ready, rest[2], *branch)
    with jax.named_scope("weights_lift"):
        theirs, drop_ready = together(swap(lift_ready, "sh"), along_ch(rest[2]))
    w_lift = (lift_ready, theirs)
    with jax.named_scope("branch_scatter"):
        branch = scatter_last(scatter_near(branch))
    branch = list(branch)
    drop_ready, branch[0] = together(drop_ready, branch[0])
    with jax.named_scope("weights_drop"):
        w_drop = (drop_ready, swap(drop_ready, "sh"))
    residual, feed_root, *feed_halves = home_forward(dims, nowhere, branch, own_tokens)
    with jax.named_scope("feed_gather"):
        feed_rows = team_gather(*feed_halves)
    active, gate_rows_grad, lift_rows_grad = feed_block(
        scalars, feed_rows, team_cotangent, w_gate, w_lift, w_drop
    )
    feed_parts = back_dot(order, [(gate_rows_grad, w_gate), (lift_rows_grad, w_lift)])
    with jax.named_scope("feed_scatter"):
        feed_grad = team_scatter(feed_parts)
    feed_back = feed_grads(
        order, feed_rows, team_cotangent, active, gate_rows_grad, lift_rows_grad
    )
    mine, given_parts = feed_back[:3], feed_back[3:]
    with jax.named_scope("gate_back"):
        gate_got = swap(given_parts[0], "sh")
    feed_grad = list(feed_grad)
    feed_grad[0], active, gate_got = together(feed_grad[0], active, gate_got)
    layer_part = forth_dot(active, w_drop)
    with jax.named_scope("lift_back"):
        lift_got, gate_part = together(swap(given_parts[1], "sh"), ch_part(added(mine[0], gate_got)))
    residual_grad, *branch_halves = home_back(
        dims, nowhere, feed_grad, residual, feed_root, own_cotangent
    )
    with jax.named_scope("branch_gather"):
        branch_grad = team_gather(*branch_halves)
    layer_part, *branch_grad = together(layer_part, *branch_grad)
    layer_part = lax.psum_scatter(layer_part, TEAM, scatter_dimension=0, tiled=True)

    mixer_rows_grad, attn_grad, along, gain_part = rows_back(
        scalars, branch_grad, w_out, ssm, gating, mixer_root, own_gain
    )
    mixer_rows_grad, lift_got, gate_part = together(mixer_rows_grad, lift_got, gate_part)
    with jax.named_scope("drop_back"):
        drop_got, lift_part = together(swap(given_parts[2], "sh"), ch_part(added(mine[1], lift_got)))
    with jax.named_scope("along_sum"):
        along = team_sum(along[:, 0]).reshape(total, 1) / DI
    query_grad, key_parts = attend_back(
        place, queries, attn_grad, attended, logs, root, key_value_rows
    )
    with jax.named_scope("keys_back"):
        key_parts = lax.all_to_all(
            key_parts.astype(BF), ("zl", "core"), split_axis=0, concat_axis=0, tiled=True
        )
        key_parts = jnp.sum(key_parts.astype(F32), axis=0).reshape(ch, count, sl * SIDE)
        if ch == 1:
            key_grad = key_parts[0]
        elif ch == 2:
            key_grad = added(
                kept(key_parts, "ch", 0), swap(given(key_parts, "ch", 0).astype(BF), "ch")
            )
        else:
            key_grad = lax.psum_scatter(
                key_parts.astype(BF), "ch", scatter_dimension=0, tiled=False
            ).astype(F32)
    out_mine, out_theirs = grad_halves(order, gathered_halves(branch_grad), branch_rows)
    along, drop_got, lift_part, out_theirs = together(along, drop_got, lift_part, out_theirs)
    with jax.named_scope("first_return"):
        first_back = ranks_return([gate_part, lift_part], drows)
    with jax.named_scope("out_back"):
        out_theirs, drop_part = together(
            swap(out_theirs, "sh"), ch_part(added(mine[2], drop_got))
        )
    ssm_grad, gating_grad, leaving_back = states_back(
        sl, step_pre, head, sides, mixer_rows_grad, ssm, gating, mixer_root, along, own_gain, root
    )
    with jax.named_scope("state_back"):
        entry_back = entering(piece_decay[:, 0], leaving_back, True)
    gating_rows_grad = jnp.concatenate([gating_grad, query_grad], 1)
    gating_mine, gating_theirs = grad_halves(order, gathered_halves(team_tokens), gating_rows_grad)
    entry_back, out_theirs, drop_part = together(entry_back, out_theirs, drop_part)
    inner_conv_grad, parts, step_rows_grad, sums = ssm_back(
        sl, step_pre, head, conv, sides, ssm_grad, carried, entry_back, root
    )
    parts, key_grad, first_back = together(parts, key_grad, first_back)
    with jax.named_scope("parts_exchange"):
        parts = lax.all_to_all(parts, TEAM, split_axis=0, concat_axis=0, tiled=True)
    with jax.named_scope("gating_back"):
        gating_theirs, out_part = together(
            swap(gating_theirs, "sh"), ch_part(added(out_mine, out_theirs))
        )
    conv_grad, conv_sums = conv_back(inner_conv_grad, parts, key_grad, conv, pre, edge)
    with jax.named_scope("follow"):
        follow = shifted(conv_grad.reshape(sl, count, LANES)[:, :EDGE], -1)
    inner_rows_grad = pre_back(conv_grad, follow, taps, root)
    inner_rows_grad, gating_theirs, out_part = together(inner_rows_grad, gating_theirs, out_part)
    inner_theirs = grad_dot(order, gathered_halves(team_tokens)[1], inner_rows_grad, BF)
    inner_mine = grad_dot(order, gathered_halves(team_tokens)[0], inner_rows_grad, F32)
    inner_rows_grad, inner_theirs = together(inner_rows_grad, inner_theirs)
    half = width // 2
    step_halves = (own_step[:, : width // 2], own_step[:, width // 2 :])
    hidden_parts = back_dot(
        order,
        [
            (inner_rows_grad, w_inner),
            (gating_rows_grad, w_gating),
            (step_rows_grad, step_halves),
        ],
    )
    with jax.named_scope("inner_back"):
        inner_theirs = swap(inner_theirs, "sh")
    with jax.named_scope("second_return"):
        second_back = ranks_return([out_part, drop_part], drows)
    inner_theirs, second_back, *hidden_parts = together(inner_theirs, second_back, *hidden_parts)
    with jax.named_scope("gating_part"):
        gating_part = ch_part(added(gating_mine, gating_theirs))
    with jax.named_scope("hidden_scatter"):
        hidden_parts = team_scatter(hidden_parts)
    with jax.named_scope("inner_part"):
        inner_part = ch_part(added(inner_mine, inner_theirs))
    with jax.named_scope("third_return"):
        third_back = ranks_return([gating_part, inner_part], drows).astype(F32)
    first_back, second_back = first_back.astype(F32), second_back.astype(F32)
    gate_back, lift_back = first_back[:, :, :LANES], first_back[:, :, LANES:]
    out_back, drop_back = second_back[:, :, :LANES], second_back[:, :, LANES:]
    gating_back = third_back[:, :, :LANES]
    inner_back = third_back[:, :, LANES:]
    token_values = jnp.concatenate(own_tokens, 1)
    token_root = inverse_root(token_values.astype(F32))
    hidden_parts = [part.astype(F32) / token_root for part in hidden_parts]
    half = width // 2
    tokens_grad, _, _ = home_back(
        dims, nowhere, hidden_parts, token_values, token_root, residual_grad
    )
    tokens_out = leave(dims, home, tokens_grad, None, F32)
    layer_output = leave(dims, home, residual, layer_part, BF)
    token_left, token_right = gathered_halves(team_tokens)
    step_back = jnp.concatenate(
        [
            grad_dot(order, token_left, step_rows_grad, F32),
            grad_dot(order, token_right, step_rows_grad, F32),
        ],
        0,
    )[:, :HEADS].T

    def placed(part, extent, at):
        base = jnp.zeros(part.shape[:-1] + (extent,), F32)
        return lax.dynamic_update_slice_in_dim(base, part, at, part.ndim - 1)

    conv_all = jnp.concatenate(
        [
            placed(conv_sums[: KC + 1, :INNER], DI, rank * INNER),
            placed(conv_sums[: KC + 1, INNER:CONV], 2 * NS, rank * SIDE),
        ],
        1,
    )
    gain_all = placed(gain_part[0], DI, rank * INNER)
    step_all = step_back.reshape(HEADS, -1, drows).swapaxes(0, 1)
    step_all = step_all.reshape(sh, ch, sl, 4, HEADS * drows)
    step_all = relative(relative(step_all, "sh", 0), "ch", 1).swapaxes(1, 2)
    per_head = jnp.concatenate(
        [placed(sums[at, :HEADS], HM, rank * HEADS) for at in range(3)]
    )
    sent = jnp.concatenate(
        [
            conv_all.reshape(KC + 1, world, conv_own).swapaxes(0, 1).reshape(world, -1),
            gain_all.reshape(world, -1),
            step_all.reshape(world, -1),
            jnp.broadcast_to(per_head[None], (world, 3 * HM)),
        ],
        1,
    )
    got_all = lax.all_to_all(sent, WORLD, split_axis=0, concat_axis=0, tiled=True)
    at = KC * conv_own + conv_own + gain_own
    step_core = got_all[:, at : at + HEADS * drows].reshape(sh, sl, ch, 4, HEADS, drows)
    step_core = jnp.sum(step_core, axis=(0, 2)).reshape(HM, drows).T
    got = jnp.sum(got_all, axis=0)
    at = 0
    conv_out = got[at : at + KC * conv_own].reshape(KC, conv_own)
    at += KC * conv_own
    conv_bias_out = got[at : at + conv_own]
    at += conv_own
    gain_out = got[at : at + gain_own]
    at += gain_own + HEADS * drows
    bias_out, decay_out, skip_out = (got[at + i * HM : at + (i + 1) * HM] for i in range(3))

    def against(weight, grad):
        return jnp.sum(weight.astype(F32) * grad, axis=1)

    inner_core = to_columns(inner_back[:, :, :INNER])
    state_core = to_columns(inner_back[:, :, INNER:CONV])
    key_value_core = to_columns(inner_back[:, :, CONV:]).reshape(drows, HK, 2, 2 * SIDE)
    key_core = key_value_core[:, :, 0].reshape(drows, HK * HD)
    value_core = key_value_core[:, :, 1].reshape(drows, HK * HD)
    gating_core = to_columns(gating_back[:, :, :INNER])
    query_core = to_columns(gating_back[:, :, INNER:])
    gate_core, lift_core = to_columns(gate_back), to_columns(lift_back)
    norm_out = (
        against(gating_weight, gating_core)
        + against(inner_weight, inner_core)
        + against(state_weight, state_core)
        + against(step_weight, step_core)
        + against(query_weight, query_core)
        + against(key_weight, key_core)
        + against(value_weight, value_core)
    )
    feed_out = against(gate_matrix, gate_core) + against(lift_matrix, lift_core)
    norm_scale = norm_gain.astype(F32)[:, None]
    feed_scale = feed_gain.astype(F32)[:, None]
    mixer_out_out = out_back[:, :, :INNER].transpose(0, 2, 1).reshape(DI, drows)
    output_out = out_back[:, :, INNER:].transpose(0, 2, 1).reshape(HA * HD, drows)
    drop_out = drop_back.transpose(0, 2, 1).reshape(-1, drows)
    return (
        layer_output,
        tokens_out,
        norm_out,
        gating_core * norm_scale,
        inner_core * norm_scale,
        state_core * norm_scale,
        step_core * norm_scale,
        conv_out,
        conv_bias_out,
        gain_out,
        mixer_out_out,
        query_core * norm_scale,
        key_core * norm_scale,
        value_core * norm_scale,
        output_out,
        feed_out,
        gate_core * feed_scale,
        lift_core * feed_scale,
        drop_out,
        bias_out,
        decay_out,
        skip_out,
    )


def solution(mesh):
    seq, ctx = mesh.shape["seq"], mesh.shape["ctx"]
    fine = Mesh(mesh.devices.reshape(seq // 2, 2, ctx // 4, 2, 2), WORLD)
    lead, vector, tail = P(WORLD, None), P(WORLD), P(None, WORLD)
    in_specs = (
        lead,
        lead,
        vector,
        lead,
        lead,
        lead,
        lead,
        tail,
        vector,
        vector,
        tail,
        lead,
        lead,
        lead,
        tail,
        vector,
        lead,
        lead,
        tail,
        P(),
        P(),
        P(),
    )
    out_specs = (
        lead,
        lead,
        vector,
        lead,
        lead,
        lead,
        lead,
        tail,
        vector,
        vector,
        tail,
        lead,
        lead,
        lead,
        tail,
        vector,
        lead,
        lead,
        tail,
        P(),
        P(),
        P(),
    )
    return jax.shard_map(local, mesh=fine, in_specs=in_specs, out_specs=out_specs, check_vma=False)
```
